32 devices in a mesh: chord: 4 (over x, core), normal: 8 (over z, y).
Axes of the slice: x: 2, y: 2, z: 4, core: 2. Of those that a mesh axis runs over, the one named last changes fastest.
Arguments:
- direct_modes: bfloat16 [16, 5, 64, 128, 256], P(None, None, 'chord', 'normal'), may hold values from -62 to 62
- adjoint_modes: bfloat16 [16, 5, 64, 128, 256], P(None, None, 'chord', 'normal'), may hold values from -5 to 5
- base_flow: float32 [5, 64, 128, 256], P(None, 'chord', 'normal'), may hold values from -5 to 5
- cell_type: int32 [64, 128, 256], P('chord', 'normal'), may hold values from 0 to 2
- mode_pick: int32 [16], replicated, may hold values from 0 to 15, each once
- flux_mix: float32 [3, 5, 5], replicated, may hold values from -2.5 to 2.5
Outputs:
- sensitivity: float32 [5, 64, 128, 256], P(None, 'chord', 'normal')
The draws below stay inside these ranges and needn't reach their ends.
Inputs may be any that keep to these rules, and one draw needn't show every extreme that they name: `mode_pick`: each mode once.
All inputs are finite; a program needn't handle non-finite values.
Results may differ from the reference program's by a relative error of at most 0.0003.
Values may be sent and summed in bfloat16 or wider, within the bound.
No kernel may reach another device: no remote copies, remote signals or barrier semaphores. Data moves between devices by JAX's collectives and lax.ppermute only.
A program may use at most 256 MiB of HBM per device.

```python
import math
import jax
import jax.numpy as jnp
from jax import lax

M = 16
VARS = 5
NX = 64
NY = 128
NZ = 256


def draw_direct_modes(key, part):
    key_one = jax.random.fold_in(key, 0)
    shape = (M, VARS, NX, NY, NZ)
    rows = jnp.arange(NY, dtype=jnp.float32).reshape(1, 1, 1, NY, 1)
    rising = jnp.exp(math.log(3.0) * rows / max(NY - 1, 1))
    values = jnp.clip(jax.random.normal(key_one, shape, jnp.float32), -4.0, 4.0)
    result = values * rising
    return result.astype(jnp.bfloat16)


def set_ends(entries, own_key, low, top_value):
    shape = entries.shape
    place = [jax.random.randint(jax.random.fold_in(own_key, axis), (), 0, shape[axis]) for axis in range(len(shape))]
    entries = entries.at[tuple(place)].set(low)
    longest = shape.index(max(shape))
    place[longest] = (place[longest] + 1) % shape[longest]
    return entries.at[tuple(place)].set(top_value)


def block_levels(stream_key, dims, cuts, least, high):
    loudness, own = 1.0, jax.random.fold_in(stream_key, 6)
    for dim, parts in cuts:
        steps = jnp.exp(jax.random.uniform(jax.random.fold_in(own, dim), (parts,), jnp.float32, least / len(cuts), high / len(cuts)))
        loudness = loudness * jnp.repeat(steps, dims[dim] // parts).reshape([-1 if axis == dim else 1 for axis in range(len(dims))])
    return loudness


def noise(own_key, shape, width, reach, cuts=(), kind=jnp.bfloat16):
    level = block_levels(own_key, shape, cuts, -0.22, 0.18) if cuts else 1.0
    values = jax.random.normal(own_key, shape, jnp.float32) * width * level
    return jnp.minimum(jnp.maximum(values, -reach), reach).astype(kind)


def setup_inputs(seed: int = 0) -> dict:
    streams_of = jax.random.split(jax.random.key(seed), 7)
    direct_modes = draw_direct_modes(jax.random.fold_in(streams_of[6], 71), 0)
    adjoint_modes = noise(streams_of[1], (M, VARS, NX, NY, NZ), 1.0, 5.0, ((2, 4), (3, 8)))
    base_flow = noise(streams_of[2], (VARS, NX, NY, NZ), 0.7, 5.0, ((1, 4), (2, 8)), jnp.float32)
    cell_type = set_ends(jax.random.randint(streams_of[3], (NX, NY, NZ), 0, 3), jax.random.fold_in(streams_of[3], 1), 0, 2).astype(jnp.int32)
    mode_pick = jax.random.permutation(streams_of[4], M).astype(jnp.int32)
    flux_mix = noise(streams_of[5], (3, VARS, VARS), VARS ** -0.5, 2.5, (), jnp.float32)
    return dict(direct_modes=direct_modes, adjoint_modes=adjoint_modes, base_flow=base_flow, cell_type=cell_type, mode_pick=mode_pick, flux_mix=flux_mix)


def mixing(matrix, field_in):
    return jnp.einsum('ij,i...->j...', matrix, field_in, precision=lax.Precision.HIGHEST)

def diff_chord(padded):
    return padded[..., 2:, 1:-1, :] - padded[..., :-2, 1:-1, :]

def diff_normal(padded):
    return padded[..., 1:-1, 2:, :] - padded[..., 1:-1, :-2, :]

def inner_cells(padded):
    return padded[..., 1:-1, 1:-1, :]

def diff_span(field_in):
    return jnp.roll(field_in, -1, -1) - jnp.roll(field_in, 1, -1)

def pad_plane(field_in):
    return jnp.pad(field_in, [(0, 0)] * (field_in.ndim - 3) + [(1, 1), (1, 1), (0, 0)])

def bilinear_term(left_pad, right_pad, flux_mix):
    summed = jnp.zeros(inner_cells(left_pad).shape, jnp.float32)
    for axis_num, differ in ((0, diff_chord), (1, diff_normal)):
        mixed_adj = mixing(flux_mix[axis_num], right_pad)
        summed = summed + differ(left_pad) * inner_cells(mixed_adj) - differ(left_pad * mixed_adj)
    left_in = inner_cells(left_pad)
    mixed_adj = mixing(flux_mix[2], inner_cells(right_pad))
    return summed + diff_span(left_in) * mixed_adj - diff_span(left_in * mixed_adj)

def cell_weight(cell_type):
    return jnp.where(cell_type == 0, 1.0, jnp.where(cell_type == 1, 0.5, 0.0)).astype(jnp.float32)

def reference(direct_modes, adjoint_modes, base_flow, cell_type, mode_pick, flux_mix):
    modes_count = direct_modes.shape[0]
    energy = lax.map(lambda single: jnp.mean(jnp.square(single.astype(jnp.float32))), direct_modes)
    amplitude = lax.rsqrt(energy + 1e-06)

    def accumulate(summed, number):
        direct = pad_plane(direct_modes[number].astype(jnp.float32))
        adjoint = pad_plane(adjoint_modes[mode_pick[number]].astype(jnp.float32))
        return (summed + amplitude[number] * bilinear_term(direct, adjoint, flux_mix), None)
    gradient, _ = lax.scan(accumulate, jnp.zeros(base_flow.shape, jnp.float32), jnp.arange(modes_count, dtype=jnp.int32))
    gradient = gradient / modes_count
    weight = cell_weight(cell_type)
    base_pad = pad_plane(base_flow)
    once_applied = bilinear_term(base_pad, pad_plane(weight * gradient), flux_mix)
    return bilinear_term(base_pad, pad_plane(weight * once_applied), flux_mix)
```

```python
import jax
import jax.numpy as jnp
import numpy as np
from jax import lax
from jax.experimental import pallas as pl
from jax.experimental.pallas import tpu as pltpu
from jax.sharding import PartitionSpec as P

F32 = jnp.float32
BF16 = jnp.bfloat16
VMEM = pltpu.VMEM
SMEM = pltpu.SMEM
LIMIT = 56 * 1024 * 1024


def in_vmem():
    return pl.BlockSpec(memory_space=VMEM)


def in_smem():
    return pl.BlockSpec(memory_space=SMEM)


def sds(shape, dtype):
    return jax.ShapeDtypeStruct(shape, dtype)


def params():
    return pltpu.CompilerParams(vmem_limit_bytes=LIMIT)


def pack_kernel(with_energy, src, xlo, xhi, ylo, yhi, *energy):
    nv, nx, ny, nz = src.shape[1:]
    xlo[0] = src[0, :, 0]
    xhi[0] = src[0, :, nx - 1]
    total = jnp.zeros((ny, nz), F32)
    for i in range(nv):
        cells = src[0, i].astype(F32)
        ylo[0, i] = cells[:, 0, :].astype(BF16)
        yhi[0, i] = cells[:, ny - 1, :].astype(BF16)
        if with_energy:
            total = total + jnp.sum(cells * cells, axis=0)
    if with_energy:
        energy[0][pl.program_id(0)] = jnp.sum(total)


def pack(modes, with_energy):
    nm, nv, nx, ny, nz = modes.shape
    face_x = sds((nm, nv, ny, nz), BF16)
    face_y = sds((nm, nv, nx, nz), BF16)
    spec_x = pl.BlockSpec((1, nv, ny, nz), lambda m: (m, 0, 0, 0))
    spec_y = pl.BlockSpec((1, nv, nx, nz), lambda m: (m, 0, 0, 0))
    return pl.pallas_call(
        lambda *refs: pack_kernel(with_energy, *refs),
        grid=(nm,),
        in_specs=[pl.BlockSpec((1, nv, nx, ny, nz), lambda m: (m, 0, 0, 0, 0))],
        out_specs=[spec_x, spec_x, spec_y, spec_y] + ([in_smem()] if with_energy else []),
        out_shape=[face_x, face_x, face_y, face_y] + ([sds((nm,), F32)] if with_energy else []),
        compiler_params=params(),
        name="pack_direct" if with_energy else "pack_adjoint",
    )(modes)


def faces_kernel(pick, amp, lw, base, *refs):
    u = refs[0:4]
    q = refs[4:8]
    w_out = refs[8:12]
    send = refs[12:16]
    nm, nv = u[0].shape[:2]
    nx, ny, nz = base.shape[1:]
    for f in range(4):
        d = f // 2
        n = u[f].shape[2]
        rows = nv * n

        def body(m, acc):
            qm = q[f][pick[m]].reshape(rows, nz)
            w = jnp.dot(lw[d], jnp.concatenate([qm, qm], axis=0), preferred_element_type=F32)
            w = w * amp[m]
            w_out[f][m] = w
            return acc + u[f][m].reshape(rows, nz).astype(F32) * w

        acc = lax.fori_loop(0, nm, body, jnp.zeros((rows, nz), F32))
        send[f][0:nv] = acc.reshape(nv, n, nz)
    for j in range(nv):
        send[0][nv + j] = base[j, 0]
        send[1][nv + j] = base[j, nx - 1]
        send[2][nv + j] = base[j][:, 0, :]
        send[3][nv + j] = base[j][:, ny - 1, :]


def faces(pick, amp, lw, base, u_faces, q_faces):
    nm, nv = u_faces[0].shape[:2]
    sizes = [f.shape[2] for f in u_faces]
    nz = base.shape[-1]
    return pl.pallas_call(
        faces_kernel,
        in_specs=[in_smem(), in_smem()] + [in_vmem()] * 10,
        out_specs=[in_vmem()] * 8,
        out_shape=[sds((nm, nv * n, nz), F32) for n in sizes] + [sds((2 * nv, n, nz), F32) for n in sizes],
        compiler_params=params(),
        name="faces",
    )(pick, amp, lw, base, *u_faces, *q_faces)


def shift_up(a):
    n = a.shape[0]
    row = lax.broadcasted_iota(jnp.int32, a.shape, 0)
    return jnp.where(row == n - 1, 0.0, pltpu.roll(a, n - 1, 0))


def shift_down(a):
    row = lax.broadcasted_iota(jnp.int32, a.shape, 0)
    return jnp.where(row == 0, 0.0, pltpu.roll(a, 1, 0))


def diff_lanes(a):
    n = a.shape[-1]
    return pltpu.roll(a, n - 1, a.ndim - 1) - pltpu.roll(a, 1, a.ndim - 1)


UNROLL = 4


def main_kernel(pick, amp, lw, ld, rz, um, uc, up, q, h_out, c0_out, acc):
    nm, nv, _, ny, nz = uc.shape
    rows = nv * ny
    acc[...] = jnp.zeros_like(acc)

    def body(step, carry):
        parts = [None] * 4
        for k in range(UNROLL):
            m = step * UNROLL + k
            qm = q[pick[m], :, 0].reshape(rows, nz)
            u = uc[m, :, 0].reshape(rows, nz)
            w = jnp.dot(lw[...], jnp.concatenate([qm, qm], axis=0), preferred_element_type=F32)
            stacked = jnp.concatenate([um[m, :, 0].reshape(rows, nz), up[m, :, 0].reshape(rows, nz), u], axis=0)
            dxy = jnp.dot(ld[0], stacked, preferred_element_type=F32)
            dz = jnp.dot(u, rz[...], preferred_element_type=F32)
            a = amp[m]
            uf = u.astype(F32) * a
            w0, w1, w2 = w[:rows], w[rows : 2 * rows], w[2 * rows :]
            terms = [(dxy[:rows] * w0 + dxy[rows:] * w1 + dz * w2) * a, uf * w0, uf * w1, uf * w2]
            parts = [t if p is None else p + t for p, t in zip(parts, terms)]
        for n in range(4):
            acc[n] += parts[n]
        return carry

    lax.fori_loop(0, nm // UNROLL, body, 0)
    c0_out[:, 0] = acc[1].reshape(nv, ny, nz)
    h = acc[0] - diff_lanes(acc[3])
    for j in range(nv):
        c1 = acc[2, j * ny : (j + 1) * ny]
        h_out[j, 0] = h[j * ny : (j + 1) * ny] - shift_up(c1) + shift_down(c1)


def main(pick, amp, lw, ld, rz, direct, adjoint):
    nm, nv, nx, ny, nz = direct.shape
    rows = nv * ny
    block = (nm, nv, 1, ny, nz)
    out_spec = pl.BlockSpec((nv, 1, ny, nz), lambda p: (0, p, 0, 0))
    whole = lambda shape: pl.BlockSpec(shape, lambda p: (0,) * len(shape))
    return pl.pallas_call(
        main_kernel,
        grid=(nx,),
        in_specs=[
            in_smem(),
            in_smem(),
            whole(lw.shape),
            pl.BlockSpec((1,) + ld.shape[1:], lambda p: (jnp.where(p == 0, 0, jnp.where(p == nx - 1, 2, 1)), 0, 0)),
            whole(rz.shape),
            pl.BlockSpec(block, lambda p: (0, 0, jnp.maximum(p - 1, 0), 0, 0)),
            pl.BlockSpec(block, lambda p: (0, 0, p, 0, 0)),
            pl.BlockSpec(block, lambda p: (0, 0, jnp.minimum(p + 1, nx - 1), 0, 0)),
            pl.BlockSpec(block, lambda p: (0, 0, p, 0, 0)),
        ],
        out_specs=[out_spec, out_spec],
        out_shape=[sds((nv, nx, ny, nz), F32)] * 2,
        scratch_shapes=[pltpu.VMEM((4, rows, nz), F32)],
        compiler_params=params(),
        cost_estimate=pl.CostEstimate(flops=2 * nm * nx * 480 * 256 * 256, bytes_accessed=4 * direct.size * 2, transcendentals=0),
        name="main",
    )(pick, amp, lw, ld, rz, direct, direct, direct, adjoint)


def weight_of(cells):
    return jnp.where(cells == 0, 1.0, jnp.where(cells == 1, 0.5, 0.0)).astype(F32)


def write_faces(values, j, x, nx, outs):
    ny = values.shape[0]
    if x == 0:
        outs[0][j] = values
    if x == nx - 1:
        outs[1][j] = values
    outs[2][j, x : x + 1] = values[0:1]
    outs[3][j, x : x + 1] = values[ny - 1 : ny]


def edge_rows(lo, hi, shape):
    row = lax.broadcasted_iota(jnp.int32, shape, 0)
    return jnp.where(row == 0, lo, 0.0) + jnp.where(row == shape[0] - 1, hi, 0.0)


def boundary_kernel(scale, h, c0, cell, *refs):
    w = refs[0:4]
    u = refs[4:8]
    got = refs[8:12]
    field = refs[12]
    outs = refs[13:17]
    add = refs[17:21]
    nv, nx, ny, nz = h.shape
    nm = u[0].shape[0]
    for f in range(4):
        n = u[f].shape[2]

        def body(m, acc):
            return acc + u[f][m].reshape(nv * n, nz).astype(F32) * w[f][m]

        total = lax.fori_loop(0, nm, body, jnp.zeros((nv * n, nz), F32))
        sign = -1.0 if f % 2 == 0 else 1.0
        add[f][...] = (sign * total).reshape(nv, n, nz) - sign * got[f][0:nv]
    for x in range(nx):
        weight = weight_of(cell[x]) * scale
        for j in range(nv):
            g = h[j, x]
            if x > 0:
                g = g + c0[j, x - 1]
            else:
                g = g + add[0][j]
            if x < nx - 1:
                g = g - c0[j, x + 1]
            else:
                g = g + add[1][j]
            g = g + edge_rows(add[2][j, x : x + 1], add[3][j, x : x + 1], (ny, nz))
            g = g * weight
            field[j, x] = g
            write_faces(g, j, x, nx, outs)


def boundary(scale, h, c0, cell, w_faces, u_halo, got):
    nv, nx, ny, nz = h.shape
    face = [sds((nv, n, nz), F32) for n in (ny, ny, nx, nx)]
    return pl.pallas_call(
        lambda *refs: boundary_kernel(scale, *refs),
        in_specs=[in_vmem()] * 15,
        out_specs=[in_vmem()] * 5,
        out_shape=[sds(h.shape, F32)] + face,
        scratch_shapes=[pltpu.VMEM(f.shape, F32) for f in face],
        compiler_params=params(),
        name="boundary",
    )(h, c0, cell, *w_faces, *u_halo, *got)


def mixed(mix, d, j, values):
    total = mix[d, 0, j] * values[0]
    for i in range(1, len(values)):
        total = total + mix[d, i, j] * values[i]
    return total


def step_kernel(last, mix, base, cell, *refs):
    field = refs[0]
    got_base = refs[1:5]
    got = refs[5:9]
    out = refs[9]
    outs = refs[10:14]
    wx, wyh = refs[-2:]
    nv, nx, ny, nz = base.shape
    for x in range(-1, nx + 1):
        values = [got[0][i] if x < 0 else got[1][i] if x == nx else field[i, x] for i in range(nv)]
        for j in range(nv):
            wx[j, x + 1] = mixed(mix, 0, j, values)
    for s in range(2):
        values = [got[2 + s][i] for i in range(nv)]
        for j in range(nv):
            wyh[s, j] = mixed(mix, 1, j, values)
    row = lax.broadcasted_iota(jnp.int32, (ny, nz), 0)
    for x in range(nx):
        values = [field[i, x] for i in range(nv)]
        weight = None if last else weight_of(cell[x])
        for j in range(nv):
            b = base[j, x]
            w = wx[j, x + 1]
            b_hi = base[j, x + 1] if x < nx - 1 else got_base[1][nv + j]
            b_lo = base[j, x - 1] if x > 0 else got_base[0][nv + j]
            total = b_hi * (w - wx[j, x + 2]) + b_lo * (wx[j, x] - w)
            w = mixed(mix, 1, j, values)
            b_hi = jnp.where(row == ny - 1, got_base[3][nv + j, x : x + 1], pltpu.roll(b, ny - 1, 0))
            b_lo = jnp.where(row == 0, got_base[2][nv + j, x : x + 1], pltpu.roll(b, 1, 0))
            w_hi = jnp.where(row == ny - 1, wyh[1, j, x : x + 1], pltpu.roll(w, ny - 1, 0))
            w_lo = jnp.where(row == 0, wyh[0, j, x : x + 1], pltpu.roll(w, 1, 0))
            total = total + b_hi * (w - w_hi) + b_lo * (w_lo - w)
            w = mixed(mix, 2, j, values)
            flux = w - pltpu.roll(w, nz - 1, 1)
            total = total + pltpu.roll(b, nz - 1, 1) * flux + pltpu.roll(b, 1, 1) * pltpu.roll(flux, 1, 1)
            if not last:
                total = total * weight
                write_faces(total, j, x, nx, outs)
            out[j, x] = total


def apply_step(last, mix, base, cell, field, got_base, got):
    nv, nx, ny, nz = base.shape
    face = [] if last else [sds((nv, n, nz), F32) for n in (ny, ny, nx, nx)]
    return pl.pallas_call(
        lambda *refs: step_kernel(last, *refs),
        in_specs=[in_smem()] + [in_vmem()] * 11,
        out_specs=[in_vmem()] * (1 + len(face)),
        out_shape=[sds(base.shape, F32)] + face,
        scratch_shapes=[pltpu.VMEM((nv, nx + 2, ny, nz), F32), pltpu.VMEM((2, nv, nx, nz), F32)],
        compiler_params=params(),
        name="step_two" if last else "step_one",
    )(mix, base, cell, field, *got_base, *got)


def exchange(arrays):
    out = []
    for k, axis in enumerate(("chord", "normal")):
        count = lax.axis_size(axis)
        up = [(i, i + 1) for i in range(count - 1)]
        down = [(i + 1, i) for i in range(count - 1)]
        out.append(lax.ppermute(arrays[2 * k + 1], axis, up))
        out.append(lax.ppermute(arrays[2 * k], axis, down))
    return out


def kron_rows(mix, ny):
    nv = mix.shape[1]
    hi = lax.reduce_precision(mix, 8, 7)
    lo = lax.reduce_precision(mix - hi, 8, 7)
    both = jnp.stack([hi, lo], axis=1)
    small = both.transpose(0, 3, 1, 2).reshape(3, nv, 2 * nv)
    rows, cols = np.arange(nv * ny), np.arange(2 * nv * ny)
    left = jnp.asarray((rows[:, None] // ny == np.arange(nv)[None]).astype(np.float32))
    right = jnp.asarray((cols[None] // ny == np.arange(2 * nv)[:, None]).astype(np.float32))
    mask = jnp.asarray((rows[:, None] % ny == cols[None] % ny).astype(np.float32))
    wide = jnp.einsum("rj,djc,ck->drk", left, small, right, precision=lax.Precision.HIGHEST)
    return (wide * mask).astype(BF16)


def difference_rows(nv, ny):
    eye = np.eye(nv * ny, dtype=np.float32)
    dy = np.kron(np.eye(nv, dtype=np.float32), np.eye(ny, k=1, dtype=np.float32) - np.eye(ny, k=-1, dtype=np.float32))
    zero = np.zeros_like(eye)
    kinds = []
    for lo, hi in ((0.0, 1.0), (1.0, 1.0), (1.0, 0.0)):
        kinds.append(np.block([[-lo * eye, hi * eye, zero], [zero, zero, dy]]))
    return jnp.asarray(np.stack(kinds), BF16)


def span_difference(nz):
    eye = np.eye(nz, dtype=np.float32)
    return jnp.asarray(np.roll(eye, -1, 1) - np.roll(eye, 1, 1), BF16)


def per_device(direct, adjoint, base, cell, pick, mix):
    nm, nv, nx, ny, nz = direct.shape
    cells_all = nv * nx * ny * nz * lax.axis_size("chord") * lax.axis_size("normal")
    *u_faces, sums = pack(direct, True)
    u_halo = exchange(u_faces)
    energy = lax.psum(sums, ("chord", "normal")) / cells_all
    amp = lax.rsqrt(energy + 1e-06)
    q_faces = pack(adjoint, False)
    lw_y = kron_rows(mix, ny)
    lw_x = lw_y if nx == ny else kron_rows(mix, nx)
    lw_faces = jnp.stack([lw_y[0], lw_x[1]])
    out = faces(pick, amp, lw_faces, base, u_faces, q_faces)
    w_faces, send = out[:4], out[4:]
    got = exchange(send)
    lw = lw_y.reshape(3 * nv * ny, 2 * nv * ny)
    h, c0 = main(pick, amp, lw, difference_rows(nv, ny), span_difference(nz), direct, adjoint)
    field, *sides = boundary(1.0 / nm, h, c0, cell, w_faces, u_halo, got)
    halo = exchange(sides)
    field, *sides = apply_step(False, mix, base, cell, field, got, halo)
    halo = exchange(sides)
    return apply_step(True, mix, base, cell, field, got, halo)[0]


def solution(mesh):
    return jax.shard_map(
        per_device,
        mesh=mesh,
        in_specs=(
            P(None, None, "chord", "normal", None),
            P(None, None, "chord", "normal", None),
            P(None, "chord", "normal", None),
            P("chord", "normal", None),
            P(),
            P(),
        ),
        out_specs=P(None, "chord", "normal", None),
        check_vma=False,
    )
```

```python
import jax
import jax.numpy as jnp
import numpy as np
from jax import lax
from jax.experimental import pallas as pl
from jax.experimental.pallas import tpu as pltpu
from jax.sharding import PartitionSpec as P

F32 = jnp.float32
BF16 = jnp.bfloat16
VMEM = pltpu.VMEM
SMEM = pltpu.SMEM
LIMIT = 56 * 1024 * 1024


def in_vmem():
    return pl.BlockSpec(memory_space=VMEM)


def in_smem():
    return pl.BlockSpec(memory_space=SMEM)


def sds(shape, dtype):
    return jax.ShapeDtypeStruct(shape, dtype)


def params():
    return pltpu.CompilerParams(vmem_limit_bytes=LIMIT)


LANES = 128


def edge_lines(cells, scratch):
    nx, ny, nz = cells.shape
    flat = cells.reshape(nx * ny, nz)
    out = ([], [])
    for h in range(nz // LANES):
        scratch[h] = flat[:, h * LANES : (h + 1) * LANES]
        for side, first in enumerate((0, ny - 1)):
            out[side].append(scratch[h, pl.ds(first, nx, stride=ny), :])
    return [jnp.concatenate(o, axis=1) for o in out]


def direct_kernel(src, xlo, xhi, ylo, yhi, energy, scratch):
    nv, nx, ny, nz = src.shape[1:]
    xlo[0] = src[0, :, 0]
    xhi[0] = src[0, :, nx - 1]
    total = jnp.zeros((ny, nz), F32)
    for i in range(nv):
        cells = src[0, i].astype(F32)
        lo, hi = edge_lines(cells, scratch.at[i])
        ylo[0, i] = lo.astype(BF16)
        yhi[0, i] = hi.astype(BF16)
        total = total + jnp.sum(cells * cells, axis=0)
    line = jnp.sum(total, axis=0, keepdims=True)
    energy[pl.ds(pl.program_id(0), 1), :] = sum(line[:, h : h + LANES] for h in range(0, nz, LANES))


def pack_direct(modes):
    nm, nv, nx, ny, nz = modes.shape
    face_x = sds((nm, nv, ny, nz), BF16)
    face_y = sds((nm, nv, nx, nz), BF16)
    spec_x = pl.BlockSpec((1, nv, ny, nz), lambda m: (m, 0, 0, 0))
    spec_y = pl.BlockSpec((1, nv, nx, nz), lambda m: (m, 0, 0, 0))
    return pl.pallas_call(
        direct_kernel,
        grid=(nm,),
        in_specs=[pl.BlockSpec((1, nv, nx, ny, nz), lambda m: (m, 0, 0, 0, 0))],
        out_specs=[spec_x, spec_x, spec_y, spec_y, pl.BlockSpec((nm, LANES), lambda m: (0, 0))],
        out_shape=[face_x, face_x, face_y, face_y, sds((nm, LANES), F32)],
        scratch_shapes=[pltpu.VMEM((nv, nz // LANES, nx * ny, LANES), F32)],
        compiler_params=params(),
        cost_estimate=pl.CostEstimate(flops=3 * modes.size, bytes_accessed=2 * modes.size, transcendentals=0),
        name="pack_direct",
    )(modes)


def adjoint_kernel(pick, src, lw_x, lw_y, *refs):
    w_out, scratch = refs[:4], refs[4]
    nv, nx, ny, nz = src.shape[1:]
    lines = [edge_lines(src[0, i].astype(F32), scratch.at[i]) for i in range(nv)]
    for f in range(4):
        if f < 2:
            face = src[0, :, 0 if f == 0 else nx - 1].reshape(nv * ny, nz)
        else:
            face = jnp.concatenate([line[f - 2] for line in lines], axis=0).astype(BF16)
        lw = lw_x if f < 2 else lw_y
        w_out[f][0] = jnp.dot(lw[...], jnp.concatenate([face, face], axis=0), preferred_element_type=F32)


def mix_faces(pick, modes, lw_x, lw_y):
    nm, nv, nx, ny, nz = modes.shape
    rows = [nv * ny, nv * ny, nv * nx, nv * nx]
    return pl.pallas_call(
        adjoint_kernel,
        grid_spec=pltpu.PrefetchScalarGridSpec(
            num_scalar_prefetch=1,
            grid=(nm,),
            in_specs=[
                pl.BlockSpec((1, nv, nx, ny, nz), lambda m, pick: (pick[m], 0, 0, 0, 0)),
                pl.BlockSpec(lw_x.shape, lambda m, pick: (0, 0)),
                pl.BlockSpec(lw_y.shape, lambda m, pick: (0, 0)),
            ],
            out_specs=[pl.BlockSpec((1, r, nz), lambda m, pick: (m, 0, 0)) for r in rows],
            scratch_shapes=[pltpu.VMEM((nv, nz // LANES, nx * ny, LANES), F32)],
        ),
        out_shape=[sds((nm, r, nz), F32) for r in rows],
        compiler_params=params(),
        cost_estimate=pl.CostEstimate(flops=4 * modes.size, bytes_accessed=3 * modes.size, transcendentals=0),
        name="mix_faces",
    )(pick, modes, lw_x, lw_y)


def faces_kernel(amp, base, *refs):
    u = refs[0:4]
    w = refs[4:8]
    send = refs[8:12]
    nm, nv = u[0].shape[:2]
    nx, ny, nz = base.shape[1:]
    for f in range(4):
        n = u[f].shape[2]
        for j in range(nv):
            total = jnp.zeros((n, nz), F32)
            for m in range(nm):
                total = total + amp[m] * (u[f][m, j].astype(F32) * w[f][m, j * n : (j + 1) * n])
            send[f][j] = total
    for j in range(nv):
        send[0][nv + j] = base[j, 0]
        send[1][nv + j] = base[j, nx - 1]
        send[2][nv + j] = base[j][:, 0, :]
        send[3][nv + j] = base[j][:, ny - 1, :]


def faces(amp, base, u_faces, w_faces):
    nv, nz = base.shape[0], base.shape[-1]
    sizes = [f.shape[2] for f in u_faces]
    return pl.pallas_call(
        faces_kernel,
        in_specs=[in_smem()] + [in_vmem()] * 9,
        out_specs=[in_vmem()] * 4,
        out_shape=[sds((2 * nv, n, nz), F32) for n in sizes],
        compiler_params=params(),
        name="faces",
    )(amp, base, *u_faces, *w_faces)


def shift_up(a):
    n = a.shape[0]
    row = lax.broadcasted_iota(jnp.int32, a.shape, 0)
    return jnp.where(row == n - 1, 0.0, pltpu.roll(a, n - 1, 0))


def shift_down(a):
    row = lax.broadcasted_iota(jnp.int32, a.shape, 0)
    return jnp.where(row == 0, 0.0, pltpu.roll(a, 1, 0))


def diff_lanes(a):
    n = a.shape[-1]
    return pltpu.roll(a, n - 1, a.ndim - 1) - pltpu.roll(a, 1, a.ndim - 1)


UNROLL = 4


def main_kernel(pick, amp, lw, um, uc, up, q, h_out, c0_out, acc):
    nm, nv, _, ny, nz = uc.shape
    rows = nv * ny
    acc[...] = jnp.zeros_like(acc)

    def body(step, carry):
        parts = [None] * 4
        for k in range(UNROLL):
            m = step * UNROLL + k
            qm = q[pick[m], :, 0].reshape(rows, nz)
            u = uc[m, :, 0].reshape(rows, nz)
            w = jnp.dot(lw[...], jnp.concatenate([qm, qm, u], axis=0), preferred_element_type=F32)
            w0, w1, w2, dy = (w[n * rows : (n + 1) * rows] for n in range(4))
            dx = up[m, :, 0].reshape(rows, nz).astype(F32) - um[m, :, 0].reshape(rows, nz).astype(F32)
            a = amp[m]
            uf = u.astype(F32)
            dz = diff_lanes(uf)
            uf = uf * a
            terms = [(dx * w0 + dy * w1 + dz * w2) * a, uf * w0, uf * w1, uf * w2]
            parts = [t if p is None else p + t for p, t in zip(parts, terms)]
        for n in range(4):
            acc[n] += parts[n]
        return carry

    lax.fori_loop(0, nm // UNROLL, body, 0)
    p = pl.program_id(0)
    ends = jnp.where(p == 0, 1.0, 0.0) - jnp.where(p == pl.num_programs(0) - 1, 1.0, 0.0)
    c0_out[:, 0] = acc[1].reshape(nv, ny, nz)
    h = acc[0] - diff_lanes(acc[3]) + ends * acc[1]
    for j in range(nv):
        c1 = acc[2, j * ny : (j + 1) * ny]
        h_out[j, 0] = h[j * ny : (j + 1) * ny] - shift_up(c1) + shift_down(c1)


def main(pick, amp, lw, direct, adjoint):
    nm, nv, nx, ny, nz = direct.shape
    rows = nv * ny
    block = (nm, nv, 1, ny, nz)
    out_spec = pl.BlockSpec((nv, 1, ny, nz), lambda p: (0, p, 0, 0))
    return pl.pallas_call(
        main_kernel,
        grid=(nx,),
        in_specs=[
            in_smem(),
            in_smem(),
            pl.BlockSpec(lw.shape, lambda p: (0, 0)),
            pl.BlockSpec(block, lambda p: (0, 0, jnp.maximum(p - 1, 0), 0, 0)),
            pl.BlockSpec(block, lambda p: (0, 0, p, 0, 0)),
            pl.BlockSpec(block, lambda p: (0, 0, jnp.minimum(p + 1, nx - 1), 0, 0)),
            pl.BlockSpec(block, lambda p: (0, 0, p, 0, 0)),
        ],
        out_specs=[out_spec, out_spec],
        out_shape=[sds((nv, nx, ny, nz), F32)] * 2,
        scratch_shapes=[pltpu.VMEM((4, rows, nz), F32)],
        compiler_params=params(),
        cost_estimate=pl.CostEstimate(flops=2 * nm * nx * 480 * 256 * 256, bytes_accessed=4 * direct.size * 2, transcendentals=0),
        name="main",
    )(pick, amp, lw, direct, direct, direct, adjoint)


def weight_of(cells):
    return jnp.where(cells == 0, 1.0, jnp.where(cells == 1, 0.5, 0.0)).astype(F32)


def write_faces(values, j, x, nx, outs):
    ny = values.shape[0]
    if x == 0:
        outs[0][j] = values
    if x == nx - 1:
        outs[1][j] = values
    outs[2][j, x : x + 1] = values[0:1]
    outs[3][j, x : x + 1] = values[ny - 1 : ny]


def edge_rows(lo, hi, shape):
    row = lax.broadcasted_iota(jnp.int32, shape, 0)
    return jnp.where(row == 0, lo, 0.0) + jnp.where(row == shape[0] - 1, hi, 0.0)


def boundary_kernel(scale, amp, h, c0, cell, *refs):
    w = refs[0:4]
    u = refs[4:8]
    got = refs[8:12]
    field = refs[12]
    outs = refs[13:17]
    add = refs[17:21]
    nv, nx, ny, nz = h.shape
    nm = u[0].shape[0]
    for f in range(4):
        n = u[f].shape[2]
        sign = -1.0 if f % 2 == 0 else 1.0
        for j in range(nv):
            total = jnp.zeros((n, nz), F32)
            for m in range(nm):
                total = total + amp[m] * (u[f][m, j].astype(F32) * w[f][m, j * n : (j + 1) * n])
            add[f][j] = sign * (total - got[f][j])
    for x in range(nx):
        weight = weight_of(cell[x]) * scale
        for j in range(nv):
            g = h[j, x]
            if x > 0:
                g = g + c0[j, x - 1]
            else:
                g = g + add[0][j]
            if x < nx - 1:
                g = g - c0[j, x + 1]
            else:
                g = g + add[1][j]
            g = g + edge_rows(add[2][j, x : x + 1], add[3][j, x : x + 1], (ny, nz))
            g = g * weight
            field[j, x] = g
            write_faces(g, j, x, nx, outs)


def boundary(scale, amp, h, c0, cell, w_faces, u_halo, got):
    nv, nx, ny, nz = h.shape
    face = [sds((nv, n, nz), F32) for n in (ny, ny, nx, nx)]
    return pl.pallas_call(
        lambda *refs: boundary_kernel(scale, *refs),
        in_specs=[in_smem()] + [in_vmem()] * 15,
        out_specs=[in_vmem()] * 5,
        out_shape=[sds(h.shape, F32)] + face,
        scratch_shapes=[pltpu.VMEM(f.shape, F32) for f in face],
        compiler_params=params(),
        name="boundary",
    )(amp, h, c0, cell, *w_faces, *u_halo, *got)


def mixed(mix, d, j, values):
    total = mix[d, 0, j] * values[0]
    for i in range(1, len(values)):
        total = total + mix[d, i, j] * values[i]
    return total


def step_kernel(last, mix, base, cell, *refs):
    field = refs[0]
    got_base = refs[1:5]
    got = refs[5:9]
    out = refs[9]
    outs = refs[10:14]
    wx, wyh = refs[-2:]
    nv, nx, ny, nz = base.shape
    for x in range(-1, nx + 1):
        values = [got[0][i] if x < 0 else got[1][i] if x == nx else field[i, x] for i in range(nv)]
        for j in range(nv):
            wx[j, x + 1] = mixed(mix, 0, j, values)
    for s in range(2):
        values = [got[2 + s][i] for i in range(nv)]
        for j in range(nv):
            wyh[s, j] = mixed(mix, 1, j, values)
    row = lax.broadcasted_iota(jnp.int32, (ny, nz), 0)
    for x in range(nx):
        values = [field[i, x] for i in range(nv)]
        weight = None if last else weight_of(cell[x])
        for j in range(nv):
            b = base[j, x]
            w = wx[j, x + 1]
            b_hi = base[j, x + 1] if x < nx - 1 else got_base[1][nv + j]
            b_lo = base[j, x - 1] if x > 0 else got_base[0][nv + j]
            total = b_hi * (w - wx[j, x + 2]) + b_lo * (wx[j, x] - w)
            w = mixed(mix, 1, j, values)
            b_hi = jnp.where(row == ny - 1, got_base[3][nv + j, x : x + 1], pltpu.roll(b, ny - 1, 0))
            b_lo = jnp.where(row == 0, got_base[2][nv + j, x : x + 1], pltpu.roll(b, 1, 0))
            w_hi = jnp.where(row == ny - 1, wyh[1, j, x : x + 1], pltpu.roll(w, ny - 1, 0))
            w_lo = jnp.where(row == 0, wyh[0, j, x : x + 1], pltpu.roll(w, 1, 0))
            total = total + b_hi * (w - w_hi) + b_lo * (w_lo - w)
            w = mixed(mix, 2, j, values)
            flux = w - pltpu.roll(w, nz - 1, 1)
            total = total + pltpu.roll(b, nz - 1, 1) * flux + pltpu.roll(b, 1, 1) * pltpu.roll(flux, 1, 1)
            if not last:
                total = total * weight
                write_faces(total, j, x, nx, outs)
            out[j, x] = total


def apply_step(last, mix, base, cell, field, got_base, got):
    nv, nx, ny, nz = base.shape
    face = [] if last else [sds((nv, n, nz), F32) for n in (ny, ny, nx, nx)]
    return pl.pallas_call(
        lambda *refs: step_kernel(last, *refs),
        in_specs=[in_smem()] + [in_vmem()] * 11,
        out_specs=[in_vmem()] * (1 + len(face)),
        out_shape=[sds(base.shape, F32)] + face,
        scratch_shapes=[pltpu.VMEM((nv, nx + 2, ny, nz), F32), pltpu.VMEM((2, nv, nx, nz), F32)],
        compiler_params=params(),
        name="step_two" if last else "step_one",
    )(mix, base, cell, field, *got_base, *got)


def exchange(arrays):
    out = []
    for k, axis in enumerate(("chord", "normal")):
        count = lax.axis_size(axis)
        up = [(i, i + 1) for i in range(count - 1)]
        down = [(i + 1, i) for i in range(count - 1)]
        out.append(lax.ppermute(arrays[2 * k + 1], axis, up))
        out.append(lax.ppermute(arrays[2 * k], axis, down))
    return out


def kron_rows(mix, ny):
    nv = mix.shape[1]
    hi = lax.reduce_precision(mix, 8, 7)
    lo = lax.reduce_precision(mix - hi, 8, 7)
    both = jnp.stack([hi, lo], axis=1)
    small = both.transpose(0, 3, 1, 2).reshape(3, nv, 2 * nv)
    rows, cols = np.arange(nv * ny), np.arange(2 * nv * ny)
    left = jnp.asarray((rows[:, None] // ny == np.arange(nv)[None]).astype(np.float32))
    right = jnp.asarray((cols[None] // ny == np.arange(2 * nv)[:, None]).astype(np.float32))
    mask = jnp.asarray((rows[:, None] % ny == cols[None] % ny).astype(np.float32))
    wide = jnp.einsum("rj,djc,ck->drk", left, small, right, precision=lax.Precision.HIGHEST)
    return (wide * mask).astype(BF16)


def main_rows(lw, nv, ny):
    dy = np.kron(np.eye(nv, dtype=np.float32), np.eye(ny, k=1, dtype=np.float32) - np.eye(ny, k=-1, dtype=np.float32))
    rows = nv * ny
    top = jnp.pad(lw.reshape(3 * rows, 2 * rows), ((0, 0), (0, rows)))
    return jnp.concatenate([top, jnp.pad(jnp.asarray(dy, BF16), ((0, 0), (2 * rows, 0)))], axis=0)


def per_device(direct, adjoint, base, cell, pick, mix):
    nm, nv, nx, ny, nz = direct.shape
    cells_all = nv * nx * ny * nz * lax.axis_size("chord") * lax.axis_size("normal")
    *u_faces, sums = pack_direct(direct)
    u_halo = exchange(u_faces)
    energy = jnp.sum(lax.all_gather(sums, ("chord", "normal")), axis=(0, 2)) / cells_all
    amp = lax.rsqrt(energy + 1e-06)
    lw_y = kron_rows(mix, ny)
    lw_x = lw_y if nx == ny else kron_rows(mix, nx)
    w_faces = mix_faces(pick, adjoint, lw_y[0], lw_x[1])
    got = exchange(faces(amp, base, u_faces, w_faces))
    h, c0 = main(pick, amp, main_rows(lw_y, nv, ny), direct, adjoint)
    field, *sides = boundary(1.0 / nm, amp, h, c0, cell, w_faces, u_halo, got)
    halo = exchange(sides)
    field, *sides = apply_step(False, mix, base, cell, field, got, halo)
    halo = exchange(sides)
    return apply_step(True, mix, base, cell, field, got, halo)[0]


def solution(mesh):
    return jax.shard_map(
        per_device,
        mesh=mesh,
        in_specs=(
            P(None, None, "chord", "normal", None),
            P(None, None, "chord", "normal", None),
            P(None, "chord", "normal", None),
            P("chord", "normal", None),
            P(),
            P(),
        ),
        out_specs=P(None, "chord", "normal", None),
        check_vma=False,
    )
```

```python
import jax
import jax.numpy as jnp
import numpy as np
from jax import lax
from jax.experimental import pallas as pl
from jax.experimental.pallas import tpu as pltpu
from jax.sharding import PartitionSpec as P

F32 = jnp.float32
BF16 = jnp.bfloat16
LANES = 128
MIB = 1024 * 1024
GROUP = 4


def in_vmem():
    return pl.BlockSpec(memory_space=pltpu.VMEM)


def in_smem():
    return pl.BlockSpec(memory_space=pltpu.SMEM)


def in_hbm():
    return pl.BlockSpec(memory_space=pl.ANY)


def sds(shape, dtype):
    return jax.ShapeDtypeStruct(shape, dtype)


def params(mib):
    return pltpu.CompilerParams(vmem_limit_bytes=mib * MIB)


def edge_lines(cells, scratch):
    nx, ny, nz = cells.shape
    flat = cells.reshape(nx * ny, nz)
    out = ([], [])
    for h in range(nz // LANES):
        scratch[h] = flat[:, h * LANES : (h + 1) * LANES]
        for side, first in enumerate((0, ny - 1)):
            out[side].append(scratch[h, pl.ds(first, nx, stride=ny), :])
    return [jnp.concatenate(o, axis=1) for o in out]


def copy_faces(src, outs, scratch, energy):
    group, nv, nx, ny, nz = src.shape

    def body(m, carry):
        outs[0][m] = src[m, :, 0]
        outs[1][m] = src[m, :, nx - 1]
        total = jnp.zeros((ny, nz), F32)
        for i in range(nv):
            cells = src[m, i].astype(F32)
            lo, hi = edge_lines(cells, scratch.at[i])
            outs[2][m, i] = lo.astype(BF16)
            outs[3][m, i] = hi.astype(BF16)
            if energy is not None:
                total = total + jnp.sum(cells * cells, axis=0)
        if energy is not None:
            line = jnp.sum(total, axis=0, keepdims=True)
            line = sum(line[:, h : h + LANES] for h in range(0, nz, LANES))
            energy[pl.ds(pl.program_id(0) * group + m, 1), :] = line
        return carry

    lax.fori_loop(0, group, body, 0)


def direct_kernel(src, xlo, xhi, ylo, yhi, energy, scratch):
    copy_faces(src, (xlo, xhi, ylo, yhi), scratch, energy)


def adjoint_kernel(steps, src, base, *refs):
    xlo, xhi, ylo, yhi = outs = refs[4:8]
    scratch = refs[8]
    nv, nx, ny, nz = base.shape

    @pl.when(pl.program_id(0) < steps)
    def _():
        copy_faces(src, outs, scratch, None)

    @pl.when(pl.program_id(0) == steps)
    def _():
        for j in range(nv):
            lines = [base[j, 0], base[j, nx - 1], *edge_lines(base[j], scratch.at[j])]
            for out, line in zip(outs, lines):
                for part in range(3):
                    rounded = line.astype(BF16)
                    out[part, j] = rounded
                    line = line - rounded.astype(F32)
                out[3, j] = jnp.zeros(out.shape[2:], BF16)


def face_spec(n, nv, nz, first):
    return pl.BlockSpec((GROUP, nv, n, nz), lambda s: (s + first, 0, 0, 0))


def pack(direct, adjoint, base):
    nm, nv, nx, ny, nz = direct.shape
    steps = nm // GROUP
    sizes = (ny, ny, nx, nx)
    shapes = [sds((2 * nm + GROUP, nv, n, nz), BF16) for n in sizes]
    block = (GROUP, nv, nx, ny, nz)
    scratch = [pltpu.VMEM((nv, nz // LANES, nx * ny, LANES), F32)]
    cost = pl.CostEstimate(flops=3 * direct.size, bytes_accessed=2 * direct.size, transcendentals=0)
    *partial, energy = pl.pallas_call(
        direct_kernel,
        grid=(steps,),
        in_specs=[pl.BlockSpec(block, lambda s: (s, 0, 0, 0, 0))],
        out_specs=[face_spec(n, nv, nz, 0) for n in sizes] + [pl.BlockSpec((nm, LANES), lambda s: (0, 0))],
        out_shape=shapes + [sds((nm, LANES), F32)],
        scratch_shapes=scratch,
        compiler_params=params(24),
        cost_estimate=cost,
        name="pack_direct",
    )(direct)
    full = pl.pallas_call(
        lambda *refs: adjoint_kernel(steps, *refs),
        grid=(steps + 1,),
        in_specs=[
            pl.BlockSpec(block, lambda s: (jnp.minimum(s, steps - 1), 0, 0, 0, 0)),
            pl.BlockSpec(base.shape, lambda s: (0, 0, 0, 0)),
        ]
        + [in_hbm()] * 4,
        out_specs=[face_spec(n, nv, nz, steps) for n in sizes],
        out_shape=shapes,
        input_output_aliases={2: 0, 3: 1, 4: 2, 5: 3},
        scratch_shapes=scratch,
        compiler_params=params(24),
        cost_estimate=cost,
        name="pack_adjoint",
    )(adjoint, base, *partial)
    return full, energy


def row_of(shape, n):
    return lax.broadcasted_iota(jnp.int32, shape, 0) % n


def diff_lanes(a):
    n = a.shape[-1]
    return pltpu.roll(a, n - 1, a.ndim - 1) - pltpu.roll(a, 1, a.ndim - 1)


def diff_rows(a, n, lo, hi):
    rows = a.shape[0]
    row = row_of(a.shape, n)
    return jnp.where(row == n - 1, hi, pltpu.roll(a, rows - 1, 0)) - jnp.where(row == 0, lo, pltpu.roll(a, 1, 0))


UNROLL = 4


def main_kernel(pick, amp, lw, u_hbm, q_hbm, out, u_buf, q_buf, acc, c0, u_sem, q_sem):
    nx, nm, nv, ny, nz = u_buf.shape
    rows = nv * ny

    def u_copy(p):
        return pltpu.make_async_copy(u_hbm.at[:, :, p], u_buf.at[p], u_sem.at[p])

    def q_copy(p):
        return pltpu.make_async_copy(q_hbm.at[:, :, p], q_buf.at[p], q_sem.at[p])

    for p in range(nx):
        u_copy(p).start()
        q_copy(p).start()
    c0[0] = jnp.zeros((rows, nz), F32)
    c0[nx + 1] = jnp.zeros((rows, nz), F32)
    u_copy(0).wait()

    def plane(p, carry):
        @pl.when(p < nx - 1)
        def _():
            u_copy(p + 1).wait()

        q_copy(p).wait()
        acc[...] = jnp.zeros_like(acc)
        below, above = jnp.maximum(p - 1, 0), jnp.minimum(p + 1, nx - 1)

        def body(step, carry):
            parts = [None] * 4
            for k in range(UNROLL):
                m = step * UNROLL + k
                qm = q_buf[p, pick[m]].reshape(rows, nz)
                u = u_buf[p, m].reshape(rows, nz)
                w = jnp.dot(lw[...], jnp.concatenate([qm, qm, u], axis=0), preferred_element_type=F32)
                w0, w1, w2, dy = (w[n * rows : (n + 1) * rows] for n in range(4))
                dx = u_buf[above, m].reshape(rows, nz).astype(F32) - u_buf[below, m].reshape(rows, nz).astype(F32)
                a = amp[m]
                uf = u.astype(F32)
                dz = diff_lanes(uf)
                uf = uf * a
                terms = [(dx * w0 + dy * w1 + dz * w2) * a, uf * w0, uf * w1, uf * w2]
                parts = [t if v is None else v + t for v, t in zip(parts, terms)]
            for n in range(4):
                acc[n] += parts[n]
            return carry

        lax.fori_loop(0, nm // UNROLL, body, 0)
        ends = jnp.where(p == 0, 1.0, 0.0) - jnp.where(p == nx - 1, 1.0, 0.0)
        c0[p + 1] = acc[1]
        h = acc[0] - diff_lanes(acc[3]) + ends * acc[1] - diff_rows(acc[2], ny, 0.0, 0.0)
        out[p] = h
        return carry

    lax.fori_loop(0, nx, plane, 0)

    def finish(p, carry):
        out[p] = out[p] - c0[p + 2] + c0[p]
        return carry

    lax.fori_loop(0, nx, finish, 0)


def main(pick, amp, lw, direct, adjoint):
    nm, nv, nx, ny, nz = direct.shape
    rows = nv * ny
    buf = pltpu.VMEM((nx, nm, nv, ny, nz), BF16)
    return pl.pallas_call(
        main_kernel,
        in_specs=[in_smem(), in_smem(), in_vmem(), in_hbm(), in_hbm()],
        out_specs=in_vmem(),
        out_shape=sds((nx, rows, nz), F32),
        scratch_shapes=[
            buf,
            buf,
            pltpu.VMEM((4, rows, nz), F32),
            pltpu.VMEM((nx + 2, rows, nz), F32),
            pltpu.SemaphoreType.DMA((nx,)),
            pltpu.SemaphoreType.DMA((nx,)),
        ],
        compiler_params=params(36),
        cost_estimate=pl.CostEstimate(flops=2 * nm * nx * 480 * 256 * 256, bytes_accessed=4 * direct.size, transcendentals=0),
        name="main",
    )(pick, amp, lw, direct, adjoint)


def weight_of(cells):
    return jnp.where(cells == 0, 1.0, jnp.where(cells == 1, 0.5, 0.0)).astype(F32)


def spread(ref, x, n):
    nv, _, nz = ref.shape
    return jnp.concatenate([jnp.broadcast_to(ref[j, pl.ds(x, 1), :], (n, nz)) for j in range(nv)], axis=0)


def write_lines(values, x, n, lo, hi):
    for j in range(lo.shape[0]):
        lo[j, pl.ds(x, 1), :] = values[j * n : j * n + 1]
        hi[j, pl.ds(x, 1), :] = values[(j + 1) * n - 1 : (j + 1) * n]


def boundary_kernel(scale, pick, amp, lw_x, lw_y, local, cell, *refs):
    own = refs[0:4]
    got = refs[4:8]
    field, xlo, xhi, ylo, yhi = refs[8:13]
    add = refs[13:17]
    nx, rows, nz = local.shape
    nm = (own[0].shape[0] - GROUP) // 2
    nv = own[0].shape[1]
    ny = rows // nv
    for f in range(4):
        add[f][...] = jnp.zeros_like(add[f])

    def body(step, carry):
        for k in range(2):
            m = step * 2 + k
            at = pick[m] + nm
            for f in range(4):
                n = nv * own[f].shape[2]
                outer = got[f][at].reshape(n, nz)
                inner = own[f][at].reshape(n, nz)
                lw = lw_x if f < 2 else lw_y
                diff = jnp.dot(lw[...], jnp.concatenate([outer, outer, inner, inner], axis=0), preferred_element_type=F32)
                add[f][...] += (amp[m] * got[f][m].reshape(n, nz).astype(F32) * diff).reshape(add[f].shape)
        return carry

    lax.fori_loop(0, nm // 2, body, 0)

    row = row_of((rows, nz), ny)

    def plane(x, carry):
        lo, hi = spread(add[2], x, ny), spread(add[3], x, ny)
        field[x] = local[x] + jnp.where(row == 0, lo, 0.0) - jnp.where(row == ny - 1, hi, 0.0)
        return carry

    lax.fori_loop(0, nx, plane, 0)
    field[0] += add[0][...].reshape(rows, nz)
    field[nx - 1] -= add[1][...].reshape(rows, nz)

    def weigh(x, carry):
        weight = weight_of(cell[x]) * scale
        g = field[x] * jnp.concatenate([weight] * nv, axis=0)
        field[x] = g
        write_lines(g, x, ny, ylo, yhi)
        return carry

    lax.fori_loop(0, nx, weigh, 0)
    xlo[...] = field[0].reshape(xlo.shape)
    xhi[...] = field[nx - 1].reshape(xhi.shape)


def boundary(scale, pick, amp, lw_x, lw_y, local, cell, own, got):
    nx, rows, nz = local.shape
    nv, ny = own[0].shape[1:3]
    face = [sds((nv, n, nz), F32) for n in (ny, ny, nx, nx)]
    return pl.pallas_call(
        lambda *refs: boundary_kernel(scale, *refs),
        in_specs=[in_smem()] * 2 + [in_vmem()] * 12,
        out_specs=[in_vmem()] * 5,
        out_shape=[sds(local.shape, F32)] + face,
        scratch_shapes=[pltpu.VMEM(f.shape, F32) for f in face],
        compiler_params=params(28),
        name="boundary",
    )(pick, amp, lw_x, lw_y, local, cell, *own, *got)


def mix_rows(lw, values):
    hi = values.astype(BF16)
    lo = (values - hi.astype(F32)).astype(BF16)
    return jnp.dot(lw, jnp.concatenate([hi, lo, hi], axis=0), preferred_element_type=F32)


def base_part(ref):
    n = ref.shape[0] - GROUP
    return ref[n].astype(F32) + (ref[n + 1].astype(F32) + ref[n + 2].astype(F32))


def step_kernel(last, lw, lw_y, base, cell, field, *refs):
    got_base = refs[0:4]
    got = refs[4:8]
    out = refs[8]
    faces = refs[9:13]
    b_pad, c0, bh_lo, bh_hi, ch_lo, ch_hi = refs[-6:]
    nv, nx, ny, nz = base.shape
    rows = nv * ny
    for f, at in ((0, 0), (1, nx + 1)):
        b = base_part(got_base[f]).reshape(rows, nz)
        b_pad[at] = b
        c0[at] = b * mix_rows(lw[:rows], got[f][...].reshape(rows, nz))
    for f, bh, ch in ((2, bh_lo, ch_lo), (3, bh_hi, ch_hi)):
        b = base_part(got_base[f])
        bh[...] = b
        ch[...] = b * mix_rows(lw_y[...], got[f][...].reshape(nv * nx, nz)).reshape(nv, nx, nz)

    def fill(x, carry):
        b_pad[x + 1] = base[:, x].reshape(rows, nz)
        return carry

    lax.fori_loop(0, nx, fill, 0)

    def plane(x, carry):
        w = mix_rows(lw[...], field[x])
        w0, w1, w2 = (w[n * rows : (n + 1) * rows] for n in range(3))
        b = b_pad[x + 1]
        c0[x + 1] = b * w0
        h = (b_pad[x + 2] - b_pad[x]) * w0
        h = h + diff_rows(b, ny, spread(bh_lo, x, ny), spread(bh_hi, x, ny)) * w1
        h = h - diff_rows(b * w1, ny, spread(ch_lo, x, ny), spread(ch_hi, x, ny))
        h = h + diff_lanes(b) * w2 - diff_lanes(b * w2)
        if last:
            out[:, x] = h.reshape(nv, ny, nz)
        else:
            out[x] = h
        return carry

    lax.fori_loop(0, nx, plane, 0)

    def finish(x, carry):
        change = c0[x] - c0[x + 2]
        if last:
            out[:, x] = out[:, x] + change.reshape(nv, ny, nz)
        else:
            g = (out[x] + change) * jnp.concatenate([weight_of(cell[x])] * nv, axis=0)
            out[x] = g
            write_lines(g, x, ny, faces[2], faces[3])
        return carry

    lax.fori_loop(0, nx, finish, 0)
    if not last:
        faces[0][...] = out[0].reshape(nv, ny, nz)
        faces[1][...] = out[nx - 1].reshape(nv, ny, nz)


def apply_step(last, lw, lw_y, base, cell, field, got_base, got):
    nv, nx, ny, nz = base.shape
    rows = nv * ny
    face = [] if last else [sds((nv, n, nz), F32) for n in (ny, ny, nx, nx)]
    line = pltpu.VMEM((nv, nx, nz), F32)
    padded = pltpu.VMEM((nx + 2, rows, nz), F32)
    return pl.pallas_call(
        lambda *refs: step_kernel(last, *refs),
        in_specs=[in_vmem()] * 13,
        out_specs=[in_vmem()] * (1 + len(face)),
        out_shape=[sds(base.shape if last else field.shape, F32)] + face,
        scratch_shapes=[padded, padded, line, line, line, line],
        compiler_params=params(28),
        name="step_two" if last else "step_one",
    )(lw, lw_y, base, cell, field, *got_base, *got)


def exchange(arrays):
    out = []
    for k, axis in enumerate(("chord", "normal")):
        count = lax.axis_size(axis)
        up = [(i, i + 1) for i in range(count - 1)]
        down = [(i + 1, i) for i in range(count - 1)]
        out.append(lax.ppermute(arrays[2 * k + 1], axis, up))
        out.append(lax.ppermute(arrays[2 * k], axis, down))
    return out


def sum_everywhere(values):
    for axis in ("chord", "normal"):
        count = lax.axis_size(axis)
        if count & (count - 1):
            values = lax.psum(values, axis)
            continue
        bit = 1
        while bit < count:
            values = values + lax.ppermute(values, axis, [(i, i ^ bit) for i in range(count)])
            bit *= 2
    return values


def kron_rows(mix, n):
    nv = mix.shape[1]
    hi = lax.reduce_precision(mix, 8, 7)
    lo = lax.reduce_precision(mix - hi, 8, 7)
    small = jnp.concatenate([hi.transpose(0, 2, 1), lo.transpose(0, 2, 1)], axis=2)
    rows, cols = np.arange(nv * n), np.arange(2 * nv * n)
    left = jnp.asarray((rows[:, None] // n == np.arange(nv)[None]).astype(np.float32))
    right = jnp.asarray((cols[None] // n == np.arange(2 * nv)[:, None]).astype(np.float32))
    mask = jnp.asarray((rows[:, None] % n == cols[None] % n).astype(np.float32))
    wide = jnp.einsum("rj,djc,ck->drk", left, small, right, precision=lax.Precision.HIGHEST)
    return (wide * mask).astype(BF16)


def main_rows(lw, nv, ny):
    dy = np.kron(np.eye(nv, dtype=np.float32), np.eye(ny, k=1, dtype=np.float32) - np.eye(ny, k=-1, dtype=np.float32))
    rows = nv * ny
    top = jnp.pad(lw.reshape(3 * rows, 2 * rows), ((0, 0), (0, rows)))
    return jnp.concatenate([top, jnp.pad(jnp.asarray(dy, BF16), ((0, 0), (2 * rows, 0)))], axis=0)


def step_rows(lw):
    half = lw.shape[-1] // 2
    return jnp.concatenate([lw[..., :half], lw[..., :half], lw[..., half:]], axis=-1)


def per_device(direct, adjoint, base, cell, pick, mix):
    nm, nv, nx, ny, nz = direct.shape
    cells_all = nv * nx * ny * nz * lax.axis_size("chord") * lax.axis_size("normal")
    own, sums = pack(direct, adjoint, base)
    energy = sum_everywhere(jnp.sum(sums, axis=1)) / cells_all
    got = exchange(own)
    amp = lax.rsqrt(energy + 1e-06)
    lw_y = kron_rows(mix, ny)
    lw_x = lw_y if nx == ny else kron_rows(mix, nx)
    local = main(pick, amp, main_rows(lw_y, nv, ny), direct, adjoint)
    across = [jnp.concatenate([lw, -lw], axis=1) for lw in (lw_y[0], lw_x[1])]
    field, *sides = boundary(1.0 / nm, pick, amp, *across, local, cell, own, got)
    lw_step = step_rows(lw_y.reshape(3 * nv * ny, -1))
    lw_line = step_rows(lw_x[1])
    field, *sides = apply_step(False, lw_step, lw_line, base, cell, field, got, exchange(sides))
    return apply_step(True, lw_step, lw_line, base, cell, field, got, exchange(sides))[0]


def solution(mesh):
    return jax.shard_map(
        per_device,
        mesh=mesh,
        in_specs=(
            P(None, None, "chord", "normal", None),
            P(None, None, "chord", "normal", None),
            P(None, "chord", "normal", None),
            P("chord", "normal", None),
            P(),
            P(),
        ),
        out_specs=P(None, "chord", "normal", None),
        check_vma=False,
    )
```

```python
import jax
import jax.numpy as jnp
import numpy as np
from jax import lax
from jax.experimental import pallas as pl
from jax.experimental.pallas import tpu as pltpu
from jax.sharding import PartitionSpec as P

F32 = jnp.float32
BF16 = jnp.bfloat16
LANES = 128
MIB = 1024 * 1024
GROUP = 4
TAIL = 4


def in_vmem():
    return pl.BlockSpec(memory_space=pltpu.VMEM)


def in_smem():
    return pl.BlockSpec(memory_space=pltpu.SMEM)


def in_hbm():
    return pl.BlockSpec(memory_space=pl.ANY)


def sds(shape, dtype):
    return jax.ShapeDtypeStruct(shape, dtype)


def params(mib):
    return pltpu.CompilerParams(vmem_limit_bytes=mib * MIB)


def edge_lines(cells, scratch):
    nx, ny, nz = cells.shape
    flat = cells.reshape(nx * ny, nz)
    out = ([], [])
    for h in range(nz // LANES):
        scratch[h] = flat[:, h * LANES : (h + 1) * LANES]
        for side, first in enumerate((0, ny - 1)):
            out[side].append(scratch[h, pl.ds(first, nx, stride=ny), :])
    return [jnp.concatenate(o, axis=1) for o in out]


def direct_kernel(half, src, xlo, xhi, ylo_a, yhi_a, ylo_b, yhi_b, energy, scratch):
    group, nv, nx, ny, nz = src.shape
    step = pl.program_id(0)

    def body(m, carry):
        xlo[m] = src[m, :, 0]
        xhi[m] = src[m, :, nx - 1]
        total = jnp.zeros((ny, nz), F32)
        for i in range(nv):
            cells = src[m, i].astype(F32)
            lo, hi = (line.astype(BF16) for line in edge_lines(cells, scratch.at[i]))

            @pl.when(step < half)
            def _():
                ylo_a[m, i] = lo
                yhi_a[m, i] = hi

            @pl.when(step >= half)
            def _():
                ylo_b[m, i] = lo
                yhi_b[m, i] = hi

            total = total + jnp.sum(cells * cells, axis=0)
        line = jnp.sum(total, axis=0, keepdims=True)
        line = sum(line[:, h : h + LANES] for h in range(0, nz, LANES))
        energy[pl.ds(step * group + m, 1), :] = line
        return carry

    lax.fori_loop(0, group, body, 0)


def pack(direct):
    nm, nv, nx, ny, nz = direct.shape
    steps = nm // GROUP
    half = steps // 2
    kinds = [(ny, nm + TAIL, lambda s: s)] * 2
    kinds += [(nx, half * GROUP, lambda s: jnp.minimum(s, half - 1))] * 2
    kinds += [(nx, nm - half * GROUP + TAIL, lambda s: jnp.maximum(s - half, 0))] * 2
    face_spec = lambda n, at: pl.BlockSpec((GROUP, nv, n, nz), lambda s: (at(s), 0, 0, 0))
    return pl.pallas_call(
        lambda *refs: direct_kernel(half, *refs),
        grid=(steps,),
        in_specs=[pl.BlockSpec((GROUP, nv, nx, ny, nz), lambda s: (s, 0, 0, 0, 0))],
        out_specs=[face_spec(n, at) for n, _, at in kinds] + [pl.BlockSpec((nm, LANES), lambda s: (0, 0))],
        out_shape=[sds((count, nv, n, nz), BF16) for n, count, _ in kinds] + [sds((nm, LANES), F32)],
        scratch_shapes=[pltpu.VMEM((nv, nz // LANES, nx * ny, LANES), F32)],
        compiler_params=params(56),
        cost_estimate=pl.CostEstimate(flops=3 * direct.size, bytes_accessed=2 * direct.size, transcendentals=0),
        name="pack_direct",
    )(direct)


def mix_chord_kernel(lw, lo, hi, w_lo, w_hi):
    nm, nv, _, ny, nz = lo.shape
    rows = nv * ny

    def body(m, carry):
        for src, out in ((lo, w_lo), (hi, w_hi)):
            face = src[m, :, 0].reshape(rows, nz)
            out[m] = jnp.dot(lw[...], jnp.concatenate([face, face], axis=0), preferred_element_type=F32)
        return carry

    lax.fori_loop(0, nm, body, 0, unroll=4)


def mix_chord(lw, modes):
    nm, nv, nx, ny, nz = modes.shape
    block = (nm, nv, 1, ny, nz)
    w = sds((nm, nv * ny, nz), F32)
    whole = pl.BlockSpec(w.shape, lambda s: (0, 0, 0))
    return pl.pallas_call(
        mix_chord_kernel,
        grid=(1,),
        in_specs=[
            pl.BlockSpec(lw.shape, lambda s: (0, 0)),
            pl.BlockSpec(block, lambda s: (0, 0, 0, 0, 0)),
            pl.BlockSpec(block, lambda s: (0, 0, nx - 1, 0, 0)),
        ],
        out_specs=[whole, whole],
        out_shape=[w, w],
        compiler_params=params(56),
        cost_estimate=pl.CostEstimate(flops=10**8, bytes_accessed=6 * 10**6, transcendentals=0),
        name="mix_chord",
    )(lw, modes, modes)


def mix_normal_kernel(lw, src, w_lo, w_hi, scratch):
    group, nv, nx, ny, nz = src.shape

    def body(m, carry):
        lines = [edge_lines(src[m, i].astype(F32), scratch.at[i]) for i in range(nv)]
        for side, out in enumerate((w_lo, w_hi)):
            face = jnp.concatenate([line[side] for line in lines], axis=0).astype(BF16)
            out[m] = jnp.dot(lw[...], jnp.concatenate([face, face], axis=0), preferred_element_type=F32)
        return carry

    lax.fori_loop(0, group, body, 0)


def mix_normal(lw, modes):
    nm, nv, nx, ny, nz = modes.shape
    w = sds((nm, nv * nx, nz), F32)
    out = pl.BlockSpec((GROUP, nv * nx, nz), lambda s: (s, 0, 0))
    return pl.pallas_call(
        mix_normal_kernel,
        grid=(nm // GROUP,),
        in_specs=[
            pl.BlockSpec(lw.shape, lambda s: (0, 0)),
            pl.BlockSpec((GROUP, nv, nx, ny, nz), lambda s: (s, 0, 0, 0, 0)),
        ],
        out_specs=[out, out],
        out_shape=[w, w],
        scratch_shapes=[pltpu.VMEM((nv, nz // LANES, nx * ny, LANES), F32)],
        compiler_params=params(56),
        cost_estimate=pl.CostEstimate(flops=3 * modes.size, bytes_accessed=3 * modes.size, transcendentals=0),
        name="mix_normal",
    )(lw, modes)


def summed(pick, amp, parts, w, j):
    nm = w.shape[0]
    n, nz = parts[0][0].shape[2:]
    total = jnp.zeros((n, nz), F32)
    m = 0
    for u, count in parts:
        for k in range(count):
            total = total + amp[m] * (u[k, j].astype(F32) * w[pick[m], pl.ds(pl.multiple_of(j * n, n), n), :])
            m += 1
    return total


def by_face(refs):
    modes = [ref.shape[0] - TAIL for ref in refs]
    parts = [[(refs[f], modes[f])] for f in range(2)]
    parts += [[(refs[f], refs[f].shape[0]), (refs[f + 2], modes[f + 2])] for f in (2, 3)]
    return parts, [refs[0], refs[1], refs[4], refs[5]]


def whole_of(ref, part):
    n = ref.shape[0] - TAIL + 2 * part
    return ref[n].astype(F32) + ref[n + 1].astype(F32)


def faces_kernel(pick, amp, base, *refs):
    u = refs[0:6]
    w = refs[6:10]
    tails = refs[10:14]
    scratch = refs[14]
    nv, nx, ny, nz = base.shape
    parts, _ = by_face(u)

    def body(j, carry):
        lines = [base[j, 0], base[j, nx - 1], *edge_lines(base[j], scratch)]
        for f in range(4):
            for n, value in enumerate((summed(pick, amp, parts[f], w[f], j), lines[f])):
                hi = value.astype(BF16)
                tails[f][2 * n, j] = hi
                tails[f][2 * n + 1, j] = (value - hi.astype(F32)).astype(BF16)
        return carry

    lax.fori_loop(0, nv, body, 0)


def faces(pick, amp, base, u_faces, w_faces):
    nv, nx, ny, nz = base.shape
    whole = lambda a: pl.BlockSpec(a.shape, lambda s: (0,) * a.ndim)
    tailed = [u_faces[f] for f in (0, 1, 4, 5)]
    at = [a.shape[0] // TAIL - 1 for a in tailed]
    return pl.pallas_call(
        faces_kernel,
        grid=(1,),
        in_specs=[in_smem()] * 2 + [whole(a) for a in (base, *u_faces, *w_faces)],
        out_specs=[pl.BlockSpec((TAIL,) + a.shape[1:], lambda s, n=n: (n, 0, 0, 0)) for a, n in zip(tailed, at)],
        out_shape=[sds(a.shape, BF16) for a in tailed],
        input_output_aliases={3: 0, 4: 1, 7: 2, 8: 3},
        scratch_shapes=[pltpu.VMEM((nz // LANES, nx * ny, LANES), F32)],
        compiler_params=params(40),
        name="faces",
    )(pick, amp, base, *u_faces, *w_faces)


def row_of(shape, n):
    return lax.broadcasted_iota(jnp.int32, shape, 0) % n


def diff_lanes(a):
    n = a.shape[-1]
    return pltpu.roll(a, n - 1, a.ndim - 1) - pltpu.roll(a, 1, a.ndim - 1)


def diff_rows(a, n, lo, hi):
    rows = a.shape[0]
    row = row_of(a.shape, n)
    return jnp.where(row == n - 1, hi, pltpu.roll(a, rows - 1, 0)) - jnp.where(row == 0, lo, pltpu.roll(a, 1, 0))


def main_kernel(pick, amp, lw, u_hbm, q_hbm, out, u_buf, q_buf, even, odd, acc, c0, u_sem, q_sem):
    nx, nm, nv, ny, nz = u_buf.shape
    rows = nv * ny

    def u_copy(p):
        return pltpu.make_async_copy(u_hbm.at[:, :, p], u_buf.at[p], u_sem.at[p])

    def q_copy(p):
        return pltpu.make_async_copy(q_hbm.at[:, :, p], q_buf.at[p], q_sem.at[p])

    for p in range(nx):
        u_copy(p).start()
        q_copy(p).start()
    c0[0] = jnp.zeros((rows, nz), F32)
    c0[nx + 1] = jnp.zeros((rows, nz), F32)

    def products(p, m, dest):
        qm = q_buf[p, pick[m]].reshape(rows, nz)
        u = u_buf[p, m].reshape(rows, nz)
        dest[m] = jnp.dot(lw[...], jnp.concatenate([qm, qm, u], axis=0), preferred_element_type=F32)

    def plane(p, src, dest):
        after = jnp.minimum(p + 1, nx - 1)

        @pl.when(p < nx - 1)
        def _():
            u_copy(after).wait()
            q_copy(after).wait()

        acc[...] = jnp.zeros_like(acc)
        before = jnp.maximum(p - 1, 0)

        def body(step, carry):
            for k in range(GROUP):
                products(after, step * GROUP + k, dest)
            for j in range(nv):
                at = slice(j * ny, (j + 1) * ny)
                sums = [acc[n, at] for n in range(4)]
                for k in range(GROUP):
                    m = step * GROUP + k
                    a = amp[m]
                    w0, w1, w2, dy = (src[m, n * rows + j * ny : n * rows + (j + 1) * ny] for n in range(4))
                    dx = u_buf[after, m, j].astype(F32) - u_buf[before, m, j].astype(F32)
                    uf = u_buf[p, m, j].astype(F32)
                    dz = diff_lanes(uf)
                    uf = uf * a
                    terms = [(dx * w0 + dy * w1 + dz * w2) * a, uf * w0, uf * w1, uf * w2]
                    sums = [v + t for v, t in zip(sums, terms)]
                for n in range(4):
                    acc[n, at] = sums[n]
            return carry

        lax.fori_loop(0, nm // GROUP, body, 0)
        ends = jnp.where(p == 0, 1.0, 0.0) - jnp.where(p == nx - 1, 1.0, 0.0)
        c0[p + 1] = acc[1]
        out[p] = acc[0] - diff_lanes(acc[3]) + ends * acc[1] - diff_rows(acc[2], ny, 0.0, 0.0)

    u_copy(0).wait()
    q_copy(0).wait()

    def first(m, carry):
        products(0, m, even)
        return carry

    lax.fori_loop(0, nm, first, 0, unroll=GROUP)

    def pair(i, carry):
        plane(2 * i, even, odd)
        plane(2 * i + 1, odd, even)
        return carry

    lax.fori_loop(0, nx // 2, pair, 0)

    def finish(p, carry):
        out[p] = out[p] - c0[p + 2] + c0[p]
        return carry

    lax.fori_loop(0, nx, finish, 0)


def main(pick, amp, lw, direct, adjoint):
    nm, nv, nx, ny, nz = direct.shape
    rows = nv * ny
    buf = pltpu.VMEM((nx, nm, nv, ny, nz), BF16)
    return pl.pallas_call(
        main_kernel,
        in_specs=[in_smem(), in_smem(), in_vmem(), in_hbm(), in_hbm()],
        out_specs=in_vmem(),
        out_shape=sds((nx, rows, nz), F32),
        scratch_shapes=[
            buf,
            buf,
            pltpu.VMEM((nm, 4 * rows, nz), F32),
            pltpu.VMEM((nm, 4 * rows, nz), F32),
            pltpu.VMEM((4, rows, nz), F32),
            pltpu.VMEM((nx + 2, rows, nz), F32),
            pltpu.SemaphoreType.DMA((nx,)),
            pltpu.SemaphoreType.DMA((nx,)),
        ],
        compiler_params=params(56),
        cost_estimate=pl.CostEstimate(flops=10**6, bytes_accessed=10**5, transcendentals=0),
        name="main",
    )(pick, amp, lw, direct, adjoint)


def weight_of(cells):
    return jnp.where(cells == 0, 1.0, jnp.where(cells == 1, 0.5, 0.0)).astype(F32)


def spread(ref, x, n):
    nv, _, nz = ref.shape
    return jnp.concatenate([jnp.broadcast_to(ref[j, pl.ds(x, 1), :], (n, nz)) for j in range(nv)], axis=0)


def write_lines(values, x, n, lo, hi):
    for j in range(lo.shape[0]):
        lo[j, pl.ds(x, 1), :] = values[j * n : j * n + 1]
        hi[j, pl.ds(x, 1), :] = values[(j + 1) * n - 1 : (j + 1) * n]


def boundary_kernel(scale, pick, amp, local, cell, *refs):
    w = refs[0:4]
    parts, tailed = by_face(refs[4:10])
    field, xlo, xhi, ylo, yhi = refs[10:15]
    add = refs[15:19]
    nx, rows, nz = local.shape
    nv = add[0].shape[0]
    ny = rows // nv
    for f in range(4):
        add[f][...] = whole_of(tailed[f], 0)

    def face(j, carry):
        for f in range(4):
            add[f][j] -= summed(pick, amp, parts[f], w[f], j)
        return carry

    lax.fori_loop(0, nv, face, 0)

    row = row_of((rows, nz), ny)

    def plane(x, carry):
        lo, hi = spread(add[2], x, ny), spread(add[3], x, ny)
        field[x] = local[x] + jnp.where(row == 0, lo, 0.0) - jnp.where(row == ny - 1, hi, 0.0)
        return carry

    lax.fori_loop(0, nx, plane, 0)
    field[0] += add[0][...].reshape(rows, nz)
    field[nx - 1] -= add[1][...].reshape(rows, nz)

    def weigh(x, carry):
        weight = weight_of(cell[x]) * scale
        g = field[x] * jnp.concatenate([weight] * nv, axis=0)
        field[x] = g
        write_lines(g, x, ny, ylo, yhi)
        return carry

    lax.fori_loop(0, nx, weigh, 0)
    xlo[...] = field[0].reshape(xlo.shape)
    xhi[...] = field[nx - 1].reshape(xhi.shape)


def boundary(scale, pick, amp, local, cell, w_faces, halo):
    nx, rows, nz = local.shape
    face = [sds(halo[f].shape[1:], F32) for f in range(4)]
    return pl.pallas_call(
        lambda *refs: boundary_kernel(scale, *refs),
        in_specs=[in_smem()] * 2 + [in_vmem()] * 12,
        out_specs=[in_vmem()] * 5,
        out_shape=[sds(local.shape, F32)] + face,
        scratch_shapes=[pltpu.VMEM(f.shape, F32) for f in face],
        compiler_params=params(28),
        name="boundary",
    )(pick, amp, local, cell, *w_faces, *halo)


def mix_rows(lw, values):
    hi = values.astype(BF16)
    lo = (values - hi.astype(F32)).astype(BF16)
    return jnp.dot(lw, jnp.concatenate([hi, lo, hi], axis=0), preferred_element_type=F32)


def step_kernel(last, lw, lw_y, base, cell, field, *refs):
    got_base = refs[0:4]
    got = refs[4:8]
    out = refs[8]
    faces = refs[9:13]
    b_pad, c0, bh_lo, bh_hi, ch_lo, ch_hi = refs[-6:]
    nv, nx, ny, nz = base.shape
    rows = nv * ny
    for f, at in ((0, 0), (1, nx + 1)):
        b = whole_of(got_base[f], 1).reshape(rows, nz)
        b_pad[at] = b
        c0[at] = b * mix_rows(lw[:rows], got[f][...].reshape(rows, nz))
    for f, bh, ch in ((2, bh_lo, ch_lo), (3, bh_hi, ch_hi)):
        b = whole_of(got_base[f], 1)
        bh[...] = b
        ch[...] = b * mix_rows(lw_y[...], got[f][...].reshape(nv * nx, nz)).reshape(nv, nx, nz)

    def fill(x, carry):
        b_pad[x + 1] = base[:, x].reshape(rows, nz)
        return carry

    lax.fori_loop(0, nx, fill, 0)

    def plane(x, carry):
        w = mix_rows(lw[...], field[x])
        w0, w1, w2 = (w[n * rows : (n + 1) * rows] for n in range(3))
        b = b_pad[x + 1]
        c0[x + 1] = b * w0
        h = (b_pad[x + 2] - b_pad[x]) * w0
        h = h + diff_rows(b, ny, spread(bh_lo, x, ny), spread(bh_hi, x, ny)) * w1
        h = h - diff_rows(b * w1, ny, spread(ch_lo, x, ny), spread(ch_hi, x, ny))
        h = h + diff_lanes(b) * w2 - diff_lanes(b * w2)
        if last:
            out[:, x] = h.reshape(nv, ny, nz)
        else:
            out[x] = h
        return carry

    lax.fori_loop(0, nx, plane, 0)

    def finish(x, carry):
        change = c0[x] - c0[x + 2]
        if last:
            out[:, x] = out[:, x] + change.reshape(nv, ny, nz)
        else:
            g = (out[x] + change) * jnp.concatenate([weight_of(cell[x])] * nv, axis=0)
            out[x] = g
            write_lines(g, x, ny, faces[2], faces[3])
        return carry

    lax.fori_loop(0, nx, finish, 0)
    if not last:
        faces[0][...] = out[0].reshape(nv, ny, nz)
        faces[1][...] = out[nx - 1].reshape(nv, ny, nz)


def apply_step(last, lw, lw_y, base, cell, field, got_base, got):
    nv, nx, ny, nz = base.shape
    rows = nv * ny
    face = [] if last else [sds((nv, n, nz), F32) for n in (ny, ny, nx, nx)]
    line = pltpu.VMEM((nv, nx, nz), F32)
    padded = pltpu.VMEM((nx + 2, rows, nz), F32)
    return pl.pallas_call(
        lambda *refs: step_kernel(last, *refs),
        in_specs=[in_vmem()] * 13,
        out_specs=[in_vmem()] * (1 + len(face)),
        out_shape=[sds(base.shape if last else field.shape, F32)] + face,
        scratch_shapes=[padded, padded, line, line, line, line],
        compiler_params=params(28),
        name="step_two" if last else "step_one",
    )(lw, lw_y, base, cell, field, *got_base, *got)


def exchange_axis(axis, lo, hi):
    count = lax.axis_size(axis)
    up = [(i, i + 1) for i in range(count - 1)]
    down = [(i + 1, i) for i in range(count - 1)]
    return [lax.ppermute(hi, axis, up), lax.ppermute(lo, axis, down)]


def exchange(arrays):
    return exchange_axis("chord", *arrays[:2]) + exchange_axis("normal", *arrays[2:])


def sum_over(axis, values):
    count = lax.axis_size(axis)
    if count & (count - 1):
        return lax.psum(values, axis)
    bit = 1
    while bit < count:
        values = values + lax.ppermute(values, axis, [(i, i ^ bit) for i in range(count)])
        bit *= 2
    return values


def kron_rows(mix, n):
    nv = mix.shape[1]
    hi = lax.reduce_precision(mix, 8, 7)
    lo = lax.reduce_precision(mix - hi, 8, 7)
    small = jnp.concatenate([hi.transpose(0, 2, 1), lo.transpose(0, 2, 1)], axis=2)
    rows, cols = np.arange(nv * n), np.arange(2 * nv * n)
    left = jnp.asarray((rows[:, None] // n == np.arange(nv)[None]).astype(np.float32))
    right = jnp.asarray((cols[None] // n == np.arange(2 * nv)[:, None]).astype(np.float32))
    mask = jnp.asarray((rows[:, None] % n == cols[None] % n).astype(np.float32))
    wide = jnp.einsum("rj,djc,ck->drk", left, small, right, precision=lax.Precision.HIGHEST)
    return (wide * mask).astype(BF16)


def main_rows(lw, nv, ny):
    dy = np.kron(np.eye(nv, dtype=np.float32), np.eye(ny, k=1, dtype=np.float32) - np.eye(ny, k=-1, dtype=np.float32))
    rows = nv * ny
    top = jnp.pad(lw.reshape(3 * rows, 2 * rows), ((0, 0), (0, rows)))
    return jnp.concatenate([top, jnp.pad(jnp.asarray(dy, BF16), ((0, 0), (2 * rows, 0)))], axis=0)


def step_rows(lw):
    half = lw.shape[-1] // 2
    return jnp.concatenate([lw[..., :half], lw[..., :half], lw[..., half:]], axis=-1)


def per_device(direct, adjoint, base, cell, pick, mix):
    nm, nv, nx, ny, nz = direct.shape
    cells_all = nv * nx * ny * nz * lax.axis_size("chord") * lax.axis_size("normal")
    *own, sums = pack(direct)
    early = exchange_axis("normal", *own[2:4])
    sums = sum_over("chord", jnp.sum(sums, axis=1))
    lw_y = kron_rows(mix, ny)
    lw_x = lw_y if nx == ny else kron_rows(mix, nx)
    w_faces = [*mix_chord(lw_y[0], adjoint), *mix_normal(lw_x[1], adjoint)]
    *early, sums = lax.optimization_barrier((*early, sums, *w_faces))[:3]
    sums = sum_over("normal", sums)
    amp = lax.rsqrt(sums / cells_all + 1e-06)
    late = exchange(faces(pick, amp, base, own, w_faces))
    halo = late[:2] + early + late[2:]
    local = main(pick, amp, main_rows(lw_y, nv, ny), direct, adjoint)
    field, *sides = boundary(1.0 / nm, pick, amp, local, cell, w_faces, halo)
    lw_step = step_rows(lw_y.reshape(3 * nv * ny, -1))
    lw_line = step_rows(lw_x[1])
    field, *sides = apply_step(False, lw_step, lw_line, base, cell, field, late, exchange(sides))
    return apply_step(True, lw_step, lw_line, base, cell, field, late, exchange(sides))[0]


def solution(mesh):
    return jax.shard_map(
        per_device,
        mesh=mesh,
        in_specs=(
            P(None, None, "chord", "normal", None),
            P(None, None, "chord", "normal", None),
            P(None, "chord", "normal", None),
            P("chord", "normal", None),
            P(),
            P(),
        ),
        out_specs=P(None, "chord", "normal", None),
        check_vma=False,
    )
```

```python
import jax
import jax.numpy as jnp
import numpy as np
from jax import lax
from jax.experimental import pallas as pl
from jax.experimental.pallas import tpu as pltpu
from jax.sharding import PartitionSpec as P

F32 = jnp.float32
BF16 = jnp.bfloat16
LANES = 128
MIB = 1024 * 1024
GROUP = 4
TAIL = 4


def in_vmem():
    return pl.BlockSpec(memory_space=pltpu.VMEM)


def in_smem():
    return pl.BlockSpec(memory_space=pltpu.SMEM)


def in_hbm():
    return pl.BlockSpec(memory_space=pl.ANY)


def sds(shape, dtype):
    return jax.ShapeDtypeStruct(shape, dtype)


def params(mib):
    return pltpu.CompilerParams(vmem_limit_bytes=mib * MIB)


def edge_lines(cells, scratch):
    nx, ny, nz = cells.shape
    flat = cells.reshape(nx * ny, nz)
    out = ([], [])
    for h in range(nz // LANES):
        scratch[h] = flat[:, h * LANES : (h + 1) * LANES]
        for side, first in enumerate((0, ny - 1)):
            out[side].append(scratch[h, pl.ds(first, nx, stride=ny), :])
    return [jnp.concatenate(o, axis=1) for o in out]


def direct_kernel(half, src, xlo, xhi, ylo_a, yhi_a, ylo_b, yhi_b, energy, scratch):
    group, nv, nx, ny, nz = src.shape
    step = pl.program_id(0)

    def body(m, carry):
        xlo[m] = src[m, :, 0]
        xhi[m] = src[m, :, nx - 1]
        total = jnp.zeros((ny, nz), F32)
        for i in range(nv):
            cells = src[m, i].astype(F32)
            lo, hi = (line.astype(BF16) for line in edge_lines(cells, scratch.at[i]))

            @pl.when(step < half)
            def _():
                ylo_a[m, i] = lo
                yhi_a[m, i] = hi

            @pl.when(step >= half)
            def _():
                ylo_b[m, i] = lo
                yhi_b[m, i] = hi

            total = total + jnp.sum(cells * cells, axis=0)
        line = jnp.sum(total, axis=0, keepdims=True)
        line = sum(line[:, h : h + LANES] for h in range(0, nz, LANES))
        energy[pl.ds(step * group + m, 1), :] = line
        return carry

    lax.fori_loop(0, group, body, 0)


def pack(direct):
    nm, nv, nx, ny, nz = direct.shape
    steps = nm // GROUP
    half = steps // 2
    kinds = [(ny, nm + TAIL, lambda s: s)] * 2
    kinds += [(nx, half * GROUP, lambda s: jnp.minimum(s, half - 1))] * 2
    kinds += [(nx, nm - half * GROUP + TAIL, lambda s: jnp.maximum(s - half, 0))] * 2
    face_spec = lambda n, at: pl.BlockSpec((GROUP, nv, n, nz), lambda s: (at(s), 0, 0, 0))
    return pl.pallas_call(
        lambda *refs: direct_kernel(half, *refs),
        grid=(steps,),
        in_specs=[pl.BlockSpec((GROUP, nv, nx, ny, nz), lambda s: (s, 0, 0, 0, 0))],
        out_specs=[face_spec(n, at) for n, _, at in kinds] + [pl.BlockSpec((nm, LANES), lambda s: (0, 0))],
        out_shape=[sds((count, nv, n, nz), BF16) for n, count, _ in kinds] + [sds((nm, LANES), F32)],
        scratch_shapes=[pltpu.VMEM((nv, nz // LANES, nx * ny, LANES), F32)],
        compiler_params=params(56),
        cost_estimate=pl.CostEstimate(flops=3 * direct.size, bytes_accessed=2 * direct.size, transcendentals=0),
        name="pack_direct",
    )(direct)


def mix_chord_kernel(lw, lo, hi, w_lo, w_hi):
    nm, nv, _, ny, nz = lo.shape
    rows = nv * ny

    def body(m, carry):
        for src, out in ((lo, w_lo), (hi, w_hi)):
            face = src[m, :, 0].reshape(rows, nz)
            out[m] = jnp.dot(lw[...], jnp.concatenate([face, face], axis=0), preferred_element_type=F32)
        return carry

    lax.fori_loop(0, nm, body, 0, unroll=4)


def mix_chord(lw, modes):
    nm, nv, nx, ny, nz = modes.shape
    block = (nm, nv, 1, ny, nz)
    w = sds((nm, nv * ny, nz), F32)
    whole = pl.BlockSpec(w.shape, lambda s: (0, 0, 0))
    return pl.pallas_call(
        mix_chord_kernel,
        grid=(1,),
        in_specs=[
            pl.BlockSpec(lw.shape, lambda s: (0, 0)),
            pl.BlockSpec(block, lambda s: (0, 0, 0, 0, 0)),
            pl.BlockSpec(block, lambda s: (0, 0, nx - 1, 0, 0)),
        ],
        out_specs=[whole, whole],
        out_shape=[w, w],
        compiler_params=params(56),
        cost_estimate=pl.CostEstimate(flops=10**8, bytes_accessed=6 * 10**6, transcendentals=0),
        name="mix_chord",
    )(lw, modes, modes)


def mix_normal_kernel(lw, src, w_lo, w_hi, scratch):
    group, nv, nx, ny, nz = src.shape

    def body(m, carry):
        lines = [edge_lines(src[m, i].astype(F32), scratch.at[i]) for i in range(nv)]
        for side, out in enumerate((w_lo, w_hi)):
            face = jnp.concatenate([line[side] for line in lines], axis=0).astype(BF16)
            out[m] = jnp.dot(lw[...], jnp.concatenate([face, face], axis=0), preferred_element_type=F32)
        return carry

    lax.fori_loop(0, group, body, 0)


def mix_normal(lw, modes):
    nm, nv, nx, ny, nz = modes.shape
    w = sds((nm, nv * nx, nz), F32)
    out = pl.BlockSpec((GROUP, nv * nx, nz), lambda s: (s, 0, 0))
    return pl.pallas_call(
        mix_normal_kernel,
        grid=(nm // GROUP,),
        in_specs=[
            pl.BlockSpec(lw.shape, lambda s: (0, 0)),
            pl.BlockSpec((GROUP, nv, nx, ny, nz), lambda s: (s, 0, 0, 0, 0)),
        ],
        out_specs=[out, out],
        out_shape=[w, w],
        scratch_shapes=[pltpu.VMEM((nv, nz // LANES, nx * ny, LANES), F32)],
        compiler_params=params(56),
        cost_estimate=pl.CostEstimate(flops=3 * modes.size, bytes_accessed=3 * modes.size, transcendentals=0),
        name="mix_normal",
    )(lw, modes)


def summed(pick, amp, parts, w):
    n, nz = w.shape[1:]
    total = jnp.zeros((n, nz), F32)
    m = 0
    for u, count in parts:
        for k in range(count):
            total = total + amp[m] * (u[k, 0].astype(F32) * w[pick[m]])
            m += 1
    return total


def by_face(refs, nm):
    first = refs[2].shape[0]
    return [[(refs[f], nm)] for f in range(2)] + [[(refs[f], first), (refs[f + 2], nm - first)] for f in (2, 3)]


def whole_of(ref, part):
    n = ref.shape[0] - TAIL + 2 * part
    return ref[n].astype(F32) + ref[n + 1].astype(F32)


def of_variable(shape, dim):
    block = tuple(1 if i == dim else size for i, size in enumerate(shape))
    return pl.BlockSpec(block, lambda j: tuple(j if i == dim else 0 for i in range(len(shape))))


def rows_of_variable(shape, nv):
    return pl.BlockSpec((shape[0], shape[1] // nv, shape[2]), lambda j: (0, j, 0))


def faces_kernel(pick, amp, base, *refs):
    u = refs[0:6]
    w = refs[6:10]
    tails = refs[10:14]
    scratch = refs[14]
    nx = base.shape[1]
    parts = by_face(u, w[0].shape[0])
    lines = [base[0, 0], base[0, nx - 1], *edge_lines(base[0], scratch)]
    for f in range(4):
        for n, value in enumerate((summed(pick, amp, parts[f], w[f]), lines[f])):
            hi = value.astype(BF16)
            tails[f][2 * n, 0] = hi
            tails[f][2 * n + 1, 0] = (value - hi.astype(F32)).astype(BF16)


def faces(pick, amp, base, u_faces, w_faces):
    nv, nx, ny, nz = base.shape
    first = u_faces[2].shape[0]
    nm = w_faces[0].shape[0]
    counts = [nm, nm, first, first, nm - first, nm - first]
    tailed = [u_faces[f] for f in (0, 1, 4, 5)]
    at = [a.shape[0] // TAIL - 1 for a in tailed]
    return pl.pallas_call(
        faces_kernel,
        grid=(nv,),
        in_specs=[in_smem()] * 2
        + [of_variable(base.shape, 0)]
        + [of_variable((count,) + a.shape[1:], 1) for a, count in zip(u_faces, counts)]
        + [rows_of_variable(a.shape, nv) for a in w_faces],
        out_specs=[pl.BlockSpec((TAIL, 1) + a.shape[2:], lambda j, n=n: (n, j, 0, 0)) for a, n in zip(tailed, at)],
        out_shape=[sds(a.shape, BF16) for a in tailed],
        input_output_aliases={3: 0, 4: 1, 7: 2, 8: 3},
        scratch_shapes=[pltpu.VMEM((nz // LANES, nx * ny, LANES), F32)],
        compiler_params=params(56),
        name="faces",
    )(pick, amp, base, *u_faces, *w_faces)


def row_of(shape, n):
    return lax.broadcasted_iota(jnp.int32, shape, 0) % n


def diff_lanes(a):
    n = a.shape[-1]
    return pltpu.roll(a, n - 1, a.ndim - 1) - pltpu.roll(a, 1, a.ndim - 1)


def diff_rows(a, n, lo, hi):
    rows = a.shape[0]
    row = row_of(a.shape, n)
    return jnp.where(row == n - 1, hi, pltpu.roll(a, rows - 1, 0)) - jnp.where(row == 0, lo, pltpu.roll(a, 1, 0))


def main_kernel(pick, amp, lw, u_hbm, q_hbm, out, u_buf, q_buf, even, odd, u_even, u_odd, acc, c0, u_sem, q_sem):
    nx, nm, nv, ny, nz = u_buf.shape
    rows = nv * ny

    def u_copy(p):
        return pltpu.make_async_copy(u_hbm.at[:, :, p], u_buf.at[p], u_sem.at[p])

    def q_copy(p):
        return pltpu.make_async_copy(q_hbm.at[:, :, p], q_buf.at[p], q_sem.at[p])

    for p in range(nx):
        u_copy(p).start()
        q_copy(p).start()
    c0[0] = jnp.zeros((rows, nz), F32)
    c0[nx + 1] = jnp.zeros((rows, nz), F32)

    def products(p, m, dest):
        qm = q_buf[p, pick[m]].reshape(rows, nz)
        dest[m] = jnp.dot(lw[...], jnp.concatenate([qm, qm], axis=0), preferred_element_type=F32)

    def plane(p, src, dest, u_src, u_dest):
        after = jnp.minimum(p + 1, nx - 1)

        @pl.when(p < nx - 1)
        def _():
            u_copy(after).wait()
            q_copy(after).wait()

        acc[...] = jnp.zeros_like(acc)

        def body(step, carry):
            for k in range(GROUP):
                products(after, step * GROUP + k, dest)
            for j in range(nv):
                at = slice(j * ny, (j + 1) * ny)
                sums = [acc[n, at] for n in range(5)]
                for k in range(GROUP):
                    m = step * GROUP + k
                    w0, down, up, w2 = (src[m, n * rows + j * ny : n * rows + (j + 1) * ny] for n in range(4))
                    u = u_src[m, at]
                    following = u_buf[after, m, j].astype(F32) * amp[m]
                    dx = following - u_dest[m, at]
                    u_dest[m, at] = following
                    terms = [dx * w0 + diff_lanes(u) * w2, u * w0, u * down, u * up, u * w2]
                    sums = [v + t for v, t in zip(sums, terms)]
                for n in range(5):
                    acc[n, at] = sums[n]
            return carry

        lax.fori_loop(0, nm // GROUP, body, 0)
        last = jnp.where(p == nx - 1, 1.0, 0.0)
        c0[p + 1] = acc[1]
        row = row_of((rows, nz), ny)
        h = acc[0] - diff_lanes(acc[4]) - last * acc[1]
        h = h + jnp.where(row == ny - 1, 0.0, pltpu.roll(acc[2], rows - 1, 0))
        out[p] = h + jnp.where(row == 0, 0.0, pltpu.roll(acc[3], 1, 0))

    u_copy(0).wait()
    q_copy(0).wait()
    u_odd[...] = jnp.zeros_like(u_odd)

    def first(m, carry):
        products(0, m, even)
        u_even[m] = u_buf[0, m].reshape(rows, nz).astype(F32) * amp[m]
        return carry

    lax.fori_loop(0, nm, first, 0, unroll=GROUP)

    def pair(i, carry):
        plane(2 * i, even, odd, u_even, u_odd)
        plane(2 * i + 1, odd, even, u_odd, u_even)
        return carry

    lax.fori_loop(0, nx // 2, pair, 0)

    def finish(p, carry):
        out[p] = out[p] - c0[p + 2] + c0[p]
        return carry

    lax.fori_loop(0, nx, finish, 0, unroll=4)


def main(pick, amp, lw, direct, adjoint):
    nm, nv, nx, ny, nz = direct.shape
    rows = nv * ny
    buf = pltpu.VMEM((nx, nm, nv, ny, nz), BF16)
    return pl.pallas_call(
        main_kernel,
        in_specs=[in_smem(), in_smem(), in_vmem(), in_hbm(), in_hbm()],
        out_specs=in_vmem(),
        out_shape=sds((nx, rows, nz), F32),
        scratch_shapes=[
            buf,
            buf,
            pltpu.VMEM((nm, 4 * rows, nz), F32),
            pltpu.VMEM((nm, 4 * rows, nz), F32),
            pltpu.VMEM((nm, rows, nz), F32),
            pltpu.VMEM((nm, rows, nz), F32),
            pltpu.VMEM((5, rows, nz), F32),
            pltpu.VMEM((nx + 2, rows, nz), F32),
            pltpu.SemaphoreType.DMA((nx,)),
            pltpu.SemaphoreType.DMA((nx,)),
        ],
        compiler_params=params(56),
        cost_estimate=pl.CostEstimate(flops=10**6, bytes_accessed=10**5, transcendentals=0),
        name="main",
    )(pick, amp, lw, direct, adjoint)


def weight_of(cells):
    return jnp.where(cells == 0, 1.0, jnp.where(cells == 1, 0.5, 0.0)).astype(F32)


def spread(ref, x, n):
    nv, _, nz = ref.shape
    return jnp.concatenate([jnp.broadcast_to(ref[j, pl.ds(x, 1), :], (n, nz)) for j in range(nv)], axis=0)


def write_lines(values, x, n, lo, hi):
    for j in range(lo.shape[0]):
        lo[j, pl.ds(x, 1), :] = values[j * n : j * n + 1]
        hi[j, pl.ds(x, 1), :] = values[(j + 1) * n - 1 : (j + 1) * n]


def boundary_kernel(scale, pick, amp, local, cell, *refs):
    w = refs[0:4]
    halo = [refs[4 + f] for f in (4, 5, 2, 3, 0, 1)]
    field, xlo, xhi, ylo, yhi = refs[10:15]
    base_halo = refs[15:19]
    add = refs[19:23]
    nx, ny, nz = local.shape
    parts = by_face(halo, w[0].shape[0])
    tailed = [halo[f] for f in (0, 1, 4, 5)]
    for f in range(4):
        sign = 1.0 if f % 2 == 0 else -1.0
        add[f][...] = sign * (whole_of(tailed[f], 0)[0] - summed(pick, amp, parts[f], w[f]))
        base_halo[f][...] = whole_of(tailed[f], 1)
    row = lax.broadcasted_iota(jnp.int32, (ny, nz), 0)

    def plane(x, carry):
        lo, hi = add[2][pl.ds(x, 1), :], add[3][pl.ds(x, 1), :]
        g = local[x] + jnp.where(row == 0, lo, 0.0) + jnp.where(row == ny - 1, hi, 0.0)
        g = g + jnp.where(x == 0, 1.0, 0.0) * add[0][...] + jnp.where(x == nx - 1, 1.0, 0.0) * add[1][...]
        g = g * (weight_of(cell[x]) * scale)
        field[x] = g
        write_lines(g, x, ny, ylo, yhi)
        return carry

    lax.fori_loop(0, nx, plane, 0, unroll=4)
    xlo[0] = field[0]
    xhi[0] = field[nx - 1]


def boundary(scale, pick, amp, local, cell, w_faces, halo):
    nx, rows, nz = local.shape
    nv = halo[0].shape[1]
    face = [sds(halo[f].shape[1:], F32) for f in range(4)]
    ordered = [halo[f] for f in (4, 5, 2, 3, 0, 1)]
    return pl.pallas_call(
        lambda *refs: boundary_kernel(scale, *refs),
        grid=(nv,),
        in_specs=[in_smem()] * 2
        + [rows_of_variable(local.shape, nv), pl.BlockSpec(cell.shape, lambda j: (0, 0, 0))]
        + [rows_of_variable(a.shape, nv) for a in w_faces]
        + [of_variable(a.shape, 1) for a in ordered],
        out_specs=[rows_of_variable(local.shape, nv)] + [of_variable(f.shape, 0) for f in face * 2],
        out_shape=[sds(local.shape, F32)] + face * 2,
        scratch_shapes=[pltpu.VMEM(f.shape[1:], F32) for f in face],
        compiler_params=params(56),
        name="boundary",
    )(pick, amp, local, cell, *w_faces, *ordered)


def mix_rows(lw, values):
    hi = values.astype(BF16)
    lo = (values - hi.astype(F32)).astype(BF16)
    return jnp.dot(lw, jnp.concatenate([hi, lo, hi], axis=0), preferred_element_type=F32)


def step_kernel(last, lw, lw_y, base, cell, field, *refs):
    got = [refs[f] for f in (2, 3, 0, 1)]
    got_base = refs[4:8]
    out = refs[8]
    faces = refs[9:13]
    b_pad, c0, bh_lo, bh_hi, ch_lo, ch_hi = refs[-6:]
    nv, nx, ny, nz = base.shape
    rows = nv * ny
    for f, at in ((0, 0), (1, nx + 1)):
        b = got_base[f][...].reshape(rows, nz)
        b_pad[at] = b
        c0[at] = b * mix_rows(lw[:rows], got[f][...].reshape(rows, nz))
    for f, bh, ch in ((2, bh_lo, ch_lo), (3, bh_hi, ch_hi)):
        b = got_base[f][...]
        bh[...] = b
        ch[...] = b * mix_rows(lw_y[...], got[f][...].reshape(nv * nx, nz)).reshape(nv, nx, nz)

    def fill(x, carry):
        b_pad[x + 1] = base[:, x].reshape(rows, nz)
        return carry

    lax.fori_loop(0, nx, fill, 0, unroll=4)

    def plane(x, carry):
        w = mix_rows(lw[...], field[x])
        w0, w1, w2 = (w[n * rows : (n + 1) * rows] for n in range(3))
        b = b_pad[x + 1]
        c0[x + 1] = b * w0
        h = (b_pad[x + 2] - b_pad[x]) * w0
        h = h + diff_rows(b, ny, spread(bh_lo, x, ny), spread(bh_hi, x, ny)) * w1
        h = h - diff_rows(b * w1, ny, spread(ch_lo, x, ny), spread(ch_hi, x, ny))
        h = h + diff_lanes(b) * w2 - diff_lanes(b * w2)
        if last:
            out[:, x] = h.reshape(nv, ny, nz)
        else:
            out[x] = h
        return carry

    lax.fori_loop(0, nx, plane, 0, unroll=4)

    def finish(x, carry):
        change = c0[x] - c0[x + 2]
        if last:
            out[:, x] = out[:, x] + change.reshape(nv, ny, nz)
        else:
            g = (out[x] + change) * jnp.concatenate([weight_of(cell[x])] * nv, axis=0)
            out[x] = g
            write_lines(g, x, ny, faces[2], faces[3])
        return carry

    lax.fori_loop(0, nx, finish, 0, unroll=4)
    if not last:
        faces[0][...] = out[0].reshape(nv, ny, nz)
        faces[1][...] = out[nx - 1].reshape(nv, ny, nz)


def apply_step(last, lw, lw_y, base, cell, field, got_base, got):
    nv, nx, ny, nz = base.shape
    rows = nv * ny
    face = [] if last else [sds((nv, n, nz), F32) for n in (ny, ny, nx, nx)]
    line = pltpu.VMEM((nv, nx, nz), F32)
    padded = pltpu.VMEM((nx + 2, rows, nz), F32)
    return pl.pallas_call(
        lambda *refs: step_kernel(last, *refs),
        in_specs=[in_vmem()] * 13,
        out_specs=[in_vmem()] * (1 + len(face)),
        out_shape=[sds(base.shape if last else field.shape, F32)] + face,
        scratch_shapes=[padded, padded, line, line, line, line],
        compiler_params=params(28),
        name="step_two" if last else "step_one",
    )(lw, lw_y, base, cell, field, *got[2:], *got[:2], *got_base)


def exchange_axis(axis, lo, hi):
    count = lax.axis_size(axis)
    up = [(i, i + 1) for i in range(count - 1)]
    down = [(i + 1, i) for i in range(count - 1)]
    return [lax.ppermute(hi, axis, up), lax.ppermute(lo, axis, down)]


def exchange(arrays):
    normal = exchange_axis("normal", *arrays[2:])
    return exchange_axis("chord", *arrays[:2]) + normal


def sum_over(axis, values):
    count = lax.axis_size(axis)
    if count & (count - 1):
        return lax.psum(values, axis)
    bit = 1
    while bit < count:
        values = values + lax.ppermute(values, axis, [(i, i ^ bit) for i in range(count)])
        bit *= 2
    return values


def kron_rows(mix, n):
    nv = mix.shape[1]
    hi = lax.reduce_precision(mix, 8, 7)
    lo = lax.reduce_precision(mix - hi, 8, 7)
    small = jnp.concatenate([hi.transpose(0, 2, 1), lo.transpose(0, 2, 1)], axis=2)
    rows, cols = np.arange(nv * n), np.arange(2 * nv * n)
    left = jnp.asarray((rows[:, None] // n == np.arange(nv)[None]).astype(np.float32))
    right = jnp.asarray((cols[None] // n == np.arange(2 * nv)[:, None]).astype(np.float32))
    return jnp.einsum("rj,djc,ck->drk", left, small, right, precision=lax.Precision.HIGHEST)


def within(wide, n, cells):
    return (wide * jnp.asarray(np.tile(cells, (wide.shape[-2] // n, wide.shape[-1] // n)))).astype(BF16)


def main_rows(wide, n):
    eye, below, above = (np.eye(n, k=k, dtype=np.float32) for k in (0, -1, 1))
    return jnp.concatenate([within(wide[d], n, c) for d, c in ((0, eye), (1, below - eye), (1, eye - above), (2, eye))], axis=0)


def step_rows(lw):
    half = lw.shape[-1] // 2
    return jnp.concatenate([lw[..., :half], lw[..., :half], lw[..., half:]], axis=-1)


def per_device(direct, adjoint, base, cell, pick, mix):
    nm, nv, nx, ny, nz = direct.shape
    cells_all = nv * nx * ny * nz * lax.axis_size("chord") * lax.axis_size("normal")
    *own, sums = pack(direct)
    early = exchange_axis("normal", *own[2:4])
    sums = sum_over("chord", jnp.sum(sums, axis=1))
    wide = kron_rows(mix, ny)
    lw_y = within(wide, ny, np.eye(ny, dtype=np.float32))
    lw_x = lw_y if nx == ny else within(kron_rows(mix, nx), nx, np.eye(nx, dtype=np.float32))
    w_faces = [*mix_chord(lw_y[0], adjoint), *mix_normal(lw_x[1], adjoint)]
    *early, sums = lax.optimization_barrier((*early, sums, *w_faces))[:3]
    sums = sum_over("normal", sums)
    amp = lax.rsqrt(sums / cells_all + 1e-06)
    late = exchange(faces(pick, amp, base, own, w_faces))
    halo = late[:2] + early + late[2:]
    local = main(pick, amp, main_rows(wide, ny), direct, adjoint)
    field, *sides = boundary(1.0 / nm, pick, amp, local, cell, w_faces, halo)
    sides, base_halo = sides[:4], sides[4:]
    lw_step = step_rows(lw_y.reshape(3 * nv * ny, -1))
    lw_line = step_rows(lw_x[1])
    field, *sides = apply_step(False, lw_step, lw_line, base, cell, field, base_halo, exchange(sides))
    return apply_step(True, lw_step, lw_line, base, cell, field, base_halo, exchange(sides))[0]


def solution(mesh):
    return jax.shard_map(
        per_device,
        mesh=mesh,
        in_specs=(
            P(None, None, "chord", "normal", None),
            P(None, None, "chord", "normal", None),
            P(None, "chord", "normal", None),
            P("chord", "normal", None),
            P(),
            P(),
        ),
        out_specs=P(None, "chord", "normal", None),
        check_vma=False,
    )
```

```python
import jax
import jax.numpy as jnp
import numpy as np
from jax import lax
from jax.experimental import pallas as pl
from jax.experimental.pallas import tpu as pltpu
from jax.sharding import PartitionSpec as P

F32 = jnp.float32
BF16 = jnp.bfloat16
LANES = 128
MIB = 1024 * 1024
GROUP = 4
TAIL = 4
LARGE = 51


def in_vmem():
    return pl.BlockSpec(memory_space=pltpu.VMEM)


def in_smem():
    return pl.BlockSpec(memory_space=pltpu.SMEM)


def in_hbm():
    return pl.BlockSpec(memory_space=pl.ANY)


def sds(shape, dtype):
    return jax.ShapeDtypeStruct(shape, dtype)


def params(mib):
    return pltpu.CompilerParams(vmem_limit_bytes=mib * MIB)


def edge_lines(cells, scratch):
    nx, ny, nz = cells.shape
    flat = cells.reshape(nx * ny, nz)
    out = ([], [])
    for h in range(nz // LANES):
        scratch[h] = flat[:, h * LANES : (h + 1) * LANES]
        for side, first in enumerate((0, ny - 1)):
            out[side].append(scratch[h, pl.ds(first, nx, stride=ny), :])
    return [jnp.concatenate(o, axis=1) for o in out]


def direct_kernel(src, xlo, xhi, ylo, yhi, energy, scratch):
    group, nv, nx, ny, nz = src.shape

    def body(m, carry):
        xlo[m] = src[m, :, 0]
        xhi[m] = src[m, :, nx - 1]
        total = jnp.zeros((ny, nz), F32)
        for i in range(nv):
            cells = src[m, i].astype(F32)
            lo, hi = edge_lines(cells, scratch.at[i])
            ylo[m, i] = lo.astype(BF16)
            yhi[m, i] = hi.astype(BF16)
            total = total + jnp.sum(cells * cells, axis=0)
        line = jnp.sum(total, axis=0, keepdims=True)
        line = sum(line[:, h : h + LANES] for h in range(0, nz, LANES))
        energy[pl.ds(pl.program_id(0) * group + m, 1), :] = line
        return carry

    lax.fori_loop(0, group, body, 0, unroll=2)


def pack(direct):
    nm, nv, nx, ny, nz = direct.shape
    sizes = (ny, ny, nx, nx)
    return pl.pallas_call(
        direct_kernel,
        grid=(nm // GROUP,),
        in_specs=[pl.BlockSpec((GROUP, nv, nx, ny, nz), lambda s: (s, 0, 0, 0, 0))],
        out_specs=[pl.BlockSpec((GROUP, nv, n, nz), lambda s: (s, 0, 0, 0)) for n in sizes]
        + [pl.BlockSpec((nm, LANES), lambda s: (0, 0))],
        out_shape=[sds((nm + TAIL, nv, n, nz), BF16) for n in sizes] + [sds((nm, LANES), F32)],
        scratch_shapes=[pltpu.VMEM((nv, nz // LANES, nx * ny, LANES), F32)],
        compiler_params=params(LARGE),
        cost_estimate=pl.CostEstimate(flops=3 * direct.size, bytes_accessed=2 * direct.size, transcendentals=0),
        name="pack_direct",
    )(direct)


def mix_chord_kernel(lw, lo, hi, w_lo, w_hi):
    nm, nv, _, ny, nz = lo.shape
    rows = nv * ny

    def body(m, carry):
        for src, out in ((lo, w_lo), (hi, w_hi)):
            face = src[m, :, 0].reshape(rows, nz)
            out[m] = jnp.dot(lw[...], jnp.concatenate([face, face], axis=0), preferred_element_type=F32)
        return carry

    lax.fori_loop(0, nm, body, 0, unroll=4)


def mix_chord(lw, modes):
    nm, nv, nx, ny, nz = modes.shape
    block = (nm, nv, 1, ny, nz)
    w = sds((nm, nv * ny, nz), F32)
    whole = pl.BlockSpec(w.shape, lambda s: (0, 0, 0))
    return pl.pallas_call(
        mix_chord_kernel,
        grid=(1,),
        in_specs=[
            pl.BlockSpec(lw.shape, lambda s: (0, 0)),
            pl.BlockSpec(block, lambda s: (0, 0, 0, 0, 0)),
            pl.BlockSpec(block, lambda s: (0, 0, nx - 1, 0, 0)),
        ],
        out_specs=[whole, whole],
        out_shape=[w, w],
        compiler_params=params(LARGE),
        cost_estimate=pl.CostEstimate(flops=10**8, bytes_accessed=6 * 10**6, transcendentals=0),
        name="mix_chord",
    )(lw, modes, modes)


def mix_normal_kernel(lw, src, w_lo, w_hi, scratch):
    group, nv, nx, ny, nz = src.shape

    def body(m, carry):
        lines = [edge_lines(src[m, i].astype(F32), scratch.at[i]) for i in range(nv)]
        for side, out in enumerate((w_lo, w_hi)):
            face = jnp.concatenate([line[side] for line in lines], axis=0).astype(BF16)
            out[m] = jnp.dot(lw[...], jnp.concatenate([face, face], axis=0), preferred_element_type=F32)
        return carry

    lax.fori_loop(0, group, body, 0, unroll=2)


def mix_normal(lw, modes):
    nm, nv, nx, ny, nz = modes.shape
    w = sds((nm, nv * nx, nz), F32)
    out = pl.BlockSpec((GROUP, nv * nx, nz), lambda s: (s, 0, 0))
    return pl.pallas_call(
        mix_normal_kernel,
        grid=(nm // GROUP,),
        in_specs=[
            pl.BlockSpec(lw.shape, lambda s: (0, 0)),
            pl.BlockSpec((GROUP, nv, nx, ny, nz), lambda s: (s, 0, 0, 0, 0)),
        ],
        out_specs=[out, out],
        out_shape=[w, w],
        scratch_shapes=[pltpu.VMEM((nv, nz // LANES, nx * ny, LANES), F32)],
        compiler_params=params(LARGE),
        cost_estimate=pl.CostEstimate(flops=3 * modes.size, bytes_accessed=3 * modes.size, transcendentals=0),
        name="mix_normal",
    )(lw, modes)


def summed(pick, amp, u, w, j):
    nm = w.shape[0]
    n, nz = u.shape[2:]
    total = jnp.zeros((n, nz), F32)
    for m in range(nm):
        total = total + amp[m] * (u[m, j].astype(F32) * w[pick[m], pl.ds(pl.multiple_of(j * n, n), n), :])
    return total


def whole_of(ref, part):
    n = ref.shape[0] - TAIL + 2 * part
    return ref[n].astype(F32) + ref[n + 1].astype(F32)


def faces_kernel(pick, amp, base, *refs):
    u = refs[0:4]
    w = refs[4:8]
    tails = refs[8:12]
    scratch = refs[12]
    nv, nx, ny, nz = base.shape

    def body(j, carry):
        lines = [base[j, 0], base[j, nx - 1], *edge_lines(base[j], scratch)]
        for f in range(4):
            for n, value in enumerate((summed(pick, amp, u[f], w[f], j), lines[f])):
                hi = value.astype(BF16)
                tails[f][2 * n, j] = hi
                tails[f][2 * n + 1, j] = (value - hi.astype(F32)).astype(BF16)
        return carry

    lax.fori_loop(0, nv, body, 0)


def faces(pick, amp, base, u_faces, w_faces):
    nv, nx, ny, nz = base.shape
    whole = lambda a: pl.BlockSpec(a.shape, lambda s: (0,) * a.ndim)
    return pl.pallas_call(
        faces_kernel,
        grid=(1,),
        in_specs=[in_smem()] * 2 + [whole(a) for a in (base, *u_faces, *w_faces)],
        out_specs=[pl.BlockSpec((TAIL,) + a.shape[1:], lambda s: (a.shape[0] // TAIL - 1, 0, 0, 0)) for a in u_faces],
        out_shape=[sds(a.shape, BF16) for a in u_faces],
        input_output_aliases={3: 0, 4: 1, 5: 2, 6: 3},
        scratch_shapes=[pltpu.VMEM((nz // LANES, nx * ny, LANES), F32)],
        compiler_params=params(36),
        name="faces",
    )(pick, amp, base, *u_faces, *w_faces)


def row_of(shape, n):
    return lax.broadcasted_iota(jnp.int32, shape, 0) % n


def diff_lanes(a):
    n = a.shape[-1]
    return pltpu.roll(a, n - 1, a.ndim - 1) - pltpu.roll(a, 1, a.ndim - 1)


def diff_rows(a, n, lo, hi):
    rows = a.shape[0]
    row = row_of(a.shape, n)
    return jnp.where(row == n - 1, hi, pltpu.roll(a, rows - 1, 0)) - jnp.where(row == 0, lo, pltpu.roll(a, 1, 0))


def main_kernel(pick, amp, lw, rz, u_hbm, q_hbm, out, u_buf, q_buf, even, odd, dz_even, dz_odd, u_even, u_odd, acc, c0, u_sem, q_sem):
    nx, nm, nv, ny, nz = u_buf.shape
    rows = nv * ny

    def u_copy(p):
        return pltpu.make_async_copy(u_hbm.at[:, :, p], u_buf.at[p], u_sem.at[p])

    def q_copy(p):
        return pltpu.make_async_copy(q_hbm.at[:, :, p], q_buf.at[p], q_sem.at[p])

    for p in range(nx):
        u_copy(p).start()
        q_copy(p).start()
    c0[0] = jnp.zeros((rows, nz), F32)
    c0[nx + 1] = jnp.zeros((rows, nz), F32)

    def products(p, m, dest):
        qm = q_buf[p, pick[m]].reshape(rows, nz)
        dest[m] = jnp.dot(lw[...], jnp.concatenate([qm, qm], axis=0), preferred_element_type=F32)

    def span_differences(p, step, dest):
        u = u_buf[p, pl.ds(step * GROUP, GROUP)].reshape(GROUP * rows, nz)
        dz = jnp.dot(u, rz[...], preferred_element_type=F32)
        dest[pl.ds(step * GROUP, GROUP)] = dz.reshape(GROUP, rows, nz)

    def plane(p, src, dest, dz_src, dz_dest, u_src, u_dest):
        after = jnp.minimum(p + 1, nx - 1)

        @pl.when(p < nx - 1)
        def _():
            u_copy(after).wait()
            q_copy(after).wait()

        acc[...] = jnp.zeros_like(acc)

        def body(step, carry):
            for k in range(GROUP):
                products(after, step * GROUP + k, dest)
            span_differences(after, step, dz_dest)
            for j in range(nv):
                at = slice(j * ny, (j + 1) * ny)
                sums = [acc[n, at] for n in range(5)]
                for k in range(GROUP):
                    m = step * GROUP + k
                    w0, down, up, w2 = (src[m, n * rows + j * ny : n * rows + (j + 1) * ny] for n in range(4))
                    u = u_src[m, at]
                    a = amp[m]
                    following = u_buf[after, m, j].astype(F32) * a
                    dx = following - u_dest[m, at]
                    u_dest[m, at] = following
                    terms = [dx * w0 + (dz_src[m, at] * a) * w2, u * w0, u * down, u * up, u * w2]
                    sums = [v + t for v, t in zip(sums, terms)]
                for n in range(5):
                    acc[n, at] = sums[n]
            return carry

        lax.fori_loop(0, nm // GROUP, body, 0)
        last = jnp.where(p == nx - 1, 1.0, 0.0)
        c0[p + 1] = acc[1]
        row = row_of((rows, nz), ny)
        h = acc[0] - diff_lanes(acc[4]) - last * acc[1]
        h = h + jnp.where(row == ny - 1, 0.0, pltpu.roll(acc[2], rows - 1, 0))
        out[p] = h + jnp.where(row == 0, 0.0, pltpu.roll(acc[3], 1, 0))

    u_copy(0).wait()
    q_copy(0).wait()
    u_odd[...] = jnp.zeros_like(u_odd)

    def first(m, carry):
        products(0, m, even)
        u_even[m] = u_buf[0, m].reshape(rows, nz).astype(F32) * amp[m]
        return carry

    lax.fori_loop(0, nm, first, 0, unroll=GROUP)
    for step in range(nm // GROUP):
        span_differences(0, step, dz_even)

    def pair(i, carry):
        plane(2 * i, even, odd, dz_even, dz_odd, u_even, u_odd)
        plane(2 * i + 1, odd, even, dz_odd, dz_even, u_odd, u_even)
        return carry

    lax.fori_loop(0, nx // 2, pair, 0)

    def finish(p, carry):
        out[p] = out[p] - c0[p + 2] + c0[p]
        return carry

    lax.fori_loop(0, nx, finish, 0, unroll=4)


def main(pick, amp, lw, rz, direct, adjoint):
    nm, nv, nx, ny, nz = direct.shape
    rows = nv * ny
    buf = pltpu.VMEM((nx, nm, nv, ny, nz), BF16)
    return pl.pallas_call(
        main_kernel,
        in_specs=[in_smem(), in_smem(), in_vmem(), in_vmem(), in_hbm(), in_hbm()],
        out_specs=in_vmem(),
        out_shape=sds((nx, rows, nz), F32),
        scratch_shapes=[
            buf,
            buf,
            pltpu.VMEM((nm, 4 * rows, nz), F32),
            pltpu.VMEM((nm, 4 * rows, nz), F32),
            pltpu.VMEM((nm, rows, nz), F32),
            pltpu.VMEM((nm, rows, nz), F32),
            pltpu.VMEM((nm, rows, nz), F32),
            pltpu.VMEM((nm, rows, nz), F32),
            pltpu.VMEM((5, rows, nz), F32),
            pltpu.VMEM((nx + 2, rows, nz), F32),
            pltpu.SemaphoreType.DMA((nx,)),
            pltpu.SemaphoreType.DMA((nx,)),
        ],
        compiler_params=params(LARGE),
        cost_estimate=pl.CostEstimate(flops=10**6, bytes_accessed=10**5, transcendentals=0),
        name="main",
    )(pick, amp, lw, rz, direct, adjoint)


def weight_of(cells):
    return jnp.where(cells == 0, 1.0, jnp.where(cells == 1, 0.5, 0.0)).astype(F32)


def spread(ref, x, n):
    nv, _, nz = ref.shape
    return jnp.concatenate([jnp.broadcast_to(ref[j, pl.ds(x, 1), :], (n, nz)) for j in range(nv)], axis=0)


def write_lines(values, x, n, lo, hi):
    for j in range(lo.shape[0]):
        lo[j, pl.ds(x, 1), :] = values[j * n : j * n + 1]
        hi[j, pl.ds(x, 1), :] = values[(j + 1) * n - 1 : (j + 1) * n]


def boundary_kernel(scale, pick, amp, local, cell, *refs):
    w = refs[0:4]
    halo = refs[4:8]
    field, xlo, xhi, ylo, yhi = refs[8:13]
    base_halo = refs[13:17]
    add = refs[17:21]
    nx, rows, nz = local.shape
    nv = add[0].shape[0]
    ny = rows // nv
    for f in range(4):
        add[f][...] = whole_of(halo[f], 0)
        base_halo[f][...] = whole_of(halo[f], 1)

    def face(j, carry):
        for f in range(4):
            add[f][j] -= summed(pick, amp, halo[f], w[f], j)
        return carry

    lax.fori_loop(0, nv, face, 0)
    row = row_of((rows, nz), ny)

    def plane(x, carry):
        lo, hi = spread(add[2], x, ny), spread(add[3], x, ny)
        g = local[x] + jnp.where(row == 0, lo, 0.0) - jnp.where(row == ny - 1, hi, 0.0)
        g = g + jnp.where(x == 0, 1.0, 0.0) * add[0][...].reshape(rows, nz)
        g = g - jnp.where(x == nx - 1, 1.0, 0.0) * add[1][...].reshape(rows, nz)
        g = g * jnp.concatenate([weight_of(cell[x]) * scale] * nv, axis=0)
        field[x] = g
        write_lines(g, x, ny, ylo, yhi)
        return carry

    lax.fori_loop(0, nx, plane, 0, unroll=2)
    xlo[...] = field[0].reshape(xlo.shape)
    xhi[...] = field[nx - 1].reshape(xhi.shape)


def boundary(scale, pick, amp, local, cell, w_faces, halo):
    nx, rows, nz = local.shape
    face = [sds(a.shape[1:], F32) for a in halo]
    return pl.pallas_call(
        lambda *refs: boundary_kernel(scale, *refs),
        in_specs=[in_smem()] * 2 + [in_vmem()] * 10,
        out_specs=[in_vmem()] * 9,
        out_shape=[sds(local.shape, F32)] + face * 2,
        scratch_shapes=[pltpu.VMEM(f.shape, F32) for f in face],
        compiler_params=params(28),
        name="boundary",
    )(pick, amp, local, cell, *w_faces, *halo)


def mix_rows(lw, values):
    hi = values.astype(BF16)
    lo = (values - hi.astype(F32)).astype(BF16)
    return jnp.dot(lw, jnp.concatenate([hi, lo, hi], axis=0), preferred_element_type=F32)


def step_kernel(last, lw, lw_y, base, cell, field, *refs):
    got = [refs[f] for f in (2, 3, 0, 1)]
    got_base = refs[4:8]
    out = refs[8]
    faces = refs[9:13]
    b_pad, c0, bh_lo, bh_hi, ch_lo, ch_hi = refs[-6:]
    nv, nx, ny, nz = base.shape
    rows = nv * ny
    for f, at in ((0, 0), (1, nx + 1)):
        b = got_base[f][...].reshape(rows, nz)
        b_pad[at] = b
        c0[at] = b * mix_rows(lw[:rows], got[f][...].reshape(rows, nz))
    for f, bh, ch in ((2, bh_lo, ch_lo), (3, bh_hi, ch_hi)):
        b = got_base[f][...]
        bh[...] = b
        ch[...] = b * mix_rows(lw_y[...], got[f][...].reshape(nv * nx, nz)).reshape(nv, nx, nz)

    def fill(x, carry):
        b_pad[x + 1] = base[:, x].reshape(rows, nz)
        return carry

    lax.fori_loop(0, nx, fill, 0, unroll=4)

    def plane(x, carry):
        w = mix_rows(lw[...], field[x])
        w0, w1, w2 = (w[n * rows : (n + 1) * rows] for n in range(3))
        b = b_pad[x + 1]
        c0[x + 1] = b * w0
        h = (b_pad[x + 2] - b_pad[x]) * w0
        h = h + diff_rows(b, ny, spread(bh_lo, x, ny), spread(bh_hi, x, ny)) * w1
        h = h - diff_rows(b * w1, ny, spread(ch_lo, x, ny), spread(ch_hi, x, ny))
        h = h + diff_lanes(b) * w2 - diff_lanes(b * w2)
        if last:
            out[:, x] = h.reshape(nv, ny, nz)
        else:
            out[x] = h
        return carry

    lax.fori_loop(0, nx, plane, 0, unroll=4)

    def finish(x, carry):
        change = c0[x] - c0[x + 2]
        if last:
            out[:, x] = out[:, x] + change.reshape(nv, ny, nz)
        else:
            g = (out[x] + change) * jnp.concatenate([weight_of(cell[x])] * nv, axis=0)
            out[x] = g
            write_lines(g, x, ny, faces[2], faces[3])
        return carry

    lax.fori_loop(0, nx, finish, 0, unroll=4)
    if not last:
        faces[0][...] = out[0].reshape(nv, ny, nz)
        faces[1][...] = out[nx - 1].reshape(nv, ny, nz)


def apply_step(last, lw, lw_y, base, cell, field, got_base, got):
    nv, nx, ny, nz = base.shape
    rows = nv * ny
    face = [] if last else [sds((nv, n, nz), F32) for n in (ny, ny, nx, nx)]
    line = pltpu.VMEM((nv, nx, nz), F32)
    padded = pltpu.VMEM((nx + 2, rows, nz), F32)
    return pl.pallas_call(
        lambda *refs: step_kernel(last, *refs),
        in_specs=[in_vmem()] * 13,
        out_specs=[in_vmem()] * (1 + len(face)),
        out_shape=[sds(base.shape if last else field.shape, F32)] + face,
        scratch_shapes=[padded, padded, line, line, line, line],
        compiler_params=params(28),
        name="step_two" if last else "step_one",
    )(lw, lw_y, base, cell, field, *got[2:], *got[:2], *got_base)


def exchange_axis(axis, lo, hi):
    count = lax.axis_size(axis)
    up = [(i, i + 1) for i in range(count - 1)]
    down = [(i + 1, i) for i in range(count - 1)]
    return [lax.ppermute(hi, axis, up), lax.ppermute(lo, axis, down)]


def exchange(arrays):
    normal = exchange_axis("normal", *arrays[2:])
    return exchange_axis("chord", *arrays[:2]) + normal


def sum_over(axis, values):
    count = lax.axis_size(axis)
    if count & (count - 1):
        return lax.psum(values, axis)
    bit = 1
    while bit < count:
        values = values + lax.ppermute(values, axis, [(i, i ^ bit) for i in range(count)])
        bit *= 2
    return values


def kron_rows(mix, n):
    nv = mix.shape[1]
    hi = lax.reduce_precision(mix, 8, 7)
    lo = lax.reduce_precision(mix - hi, 8, 7)
    small = jnp.concatenate([hi.transpose(0, 2, 1), lo.transpose(0, 2, 1)], axis=2)
    rows, cols = np.arange(nv * n), np.arange(2 * nv * n)
    left = jnp.asarray((rows[:, None] // n == np.arange(nv)[None]).astype(np.float32))
    right = jnp.asarray((cols[None] // n == np.arange(2 * nv)[:, None]).astype(np.float32))
    return jnp.einsum("rj,djc,ck->drk", left, small, right, precision=lax.Precision.HIGHEST)


def within(wide, n, cells):
    return (wide * jnp.asarray(np.tile(cells, (wide.shape[-2] // n, wide.shape[-1] // n)))).astype(BF16)


def main_rows(wide, n):
    eye, below, above = (np.eye(n, k=k, dtype=np.float32) for k in (0, -1, 1))
    return jnp.concatenate([within(wide[d], n, c) for d, c in ((0, eye), (1, below - eye), (1, eye - above), (2, eye))], axis=0)


def span_difference(nz):
    eye = np.eye(nz, dtype=np.float32)
    return jnp.asarray(np.roll(eye, -1, 1) - np.roll(eye, 1, 1), BF16)


def step_rows(lw):
    half = lw.shape[-1] // 2
    return jnp.concatenate([lw[..., :half], lw[..., :half], lw[..., half:]], axis=-1)


def per_device(direct, adjoint, base, cell, pick, mix):
    nm, nv, nx, ny, nz = direct.shape
    cells_all = nv * nx * ny * nz * lax.axis_size("chord") * lax.axis_size("normal")
    *own, sums = pack(direct)
    sums = sum_over("chord", sum_over("normal", jnp.sum(sums, axis=1)))
    amp = lax.rsqrt(sums / cells_all + 1e-06)
    wide = kron_rows(mix, ny)
    lw_y = within(wide, ny, np.eye(ny, dtype=np.float32))
    lw_x = lw_y if nx == ny else within(kron_rows(mix, nx), nx, np.eye(nx, dtype=np.float32))
    w_faces = [*mix_chord(lw_y[0], adjoint), *mix_normal(lw_x[1], adjoint)]
    halo = exchange(faces(pick, amp, base, own, w_faces))
    local = main(pick, amp, main_rows(wide, ny), span_difference(nz), direct, adjoint)
    field, *sides = boundary(1.0 / nm, pick, amp, local, cell, w_faces, halo)
    sides, base_halo = sides[:4], sides[4:]
    lw_step = step_rows(lw_y.reshape(3 * nv * ny, -1))
    lw_line = step_rows(lw_x[1])
    field, *sides = apply_step(False, lw_step, lw_line, base, cell, field, base_halo, exchange(sides))
    return apply_step(True, lw_step, lw_line, base, cell, field, base_halo, exchange(sides))[0]


def solution(mesh):
    return jax.shard_map(
        per_device,
        mesh=mesh,
        in_specs=(
            P(None, None, "chord", "normal", None),
            P(None, None, "chord", "normal", None),
            P(None, "chord", "normal", None),
            P("chord", "normal", None),
            P(),
            P(),
        ),
        out_specs=P(None, "chord", "normal", None),
        check_vma=False,
    )
```

```python
import jax
import jax.numpy as jnp
import numpy as np
from jax import lax
from jax.experimental import pallas as pl
from jax.experimental.pallas import tpu as pltpu
from jax.sharding import PartitionSpec as P

F32 = jnp.float32
BF16 = jnp.bfloat16
LANES = 128
MIB = 1024 * 1024
GROUP = 4
TAIL = 4
LARGE = 51


def in_vmem():
    return pl.BlockSpec(memory_space=pltpu.VMEM)


def in_smem():
    return pl.BlockSpec(memory_space=pltpu.SMEM)


def in_hbm():
    return pl.BlockSpec(memory_space=pl.ANY)


def sds(shape, dtype):
    return jax.ShapeDtypeStruct(shape, dtype)


def params(mib):
    return pltpu.CompilerParams(vmem_limit_bytes=mib * MIB)


def edge_lines(cells, scratch):
    nx, ny, nz = cells.shape
    flat = cells.reshape(nx * ny, nz)
    out = ([], [])
    for h in range(nz // LANES):
        scratch[h] = flat[:, h * LANES : (h + 1) * LANES]
        for side, first in enumerate((0, ny - 1)):
            out[side].append(scratch[h, pl.ds(first, nx, stride=ny), :])
    return [jnp.concatenate(o, axis=1) for o in out]


def direct_kernel(src, xlo, xhi, ylo, yhi, energy, scratch):
    group, nv, nx, ny, nz = src.shape

    def body(m, carry):
        xlo[m] = src[m, :, 0]
        xhi[m] = src[m, :, nx - 1]
        total = jnp.zeros((ny, nz), F32)
        for i in range(nv):
            cells = src[m, i].astype(F32)
            lo, hi = edge_lines(cells, scratch.at[i])
            ylo[m, i] = lo.astype(BF16)
            yhi[m, i] = hi.astype(BF16)
            total = total + jnp.sum(cells * cells, axis=0)
        line = jnp.sum(total, axis=0, keepdims=True)
        line = sum(line[:, h : h + LANES] for h in range(0, nz, LANES))
        energy[pl.ds(pl.program_id(0) * group + m, 1), :] = line
        return carry

    lax.fori_loop(0, group, body, 0, unroll=2)


def pack(direct):
    nm, nv, nx, ny, nz = direct.shape
    sizes = (ny, ny, nx, nx)
    return pl.pallas_call(
        direct_kernel,
        grid=(nm // GROUP,),
        in_specs=[pl.BlockSpec((GROUP, nv, nx, ny, nz), lambda s: (s, 0, 0, 0, 0))],
        out_specs=[pl.BlockSpec((GROUP, nv, n, nz), lambda s: (s, 0, 0, 0)) for n in sizes]
        + [pl.BlockSpec((nm, LANES), lambda s: (0, 0))],
        out_shape=[sds((nm + TAIL, nv, n, nz), BF16) for n in sizes] + [sds((nm, LANES), F32)],
        scratch_shapes=[pltpu.VMEM((nv, nz // LANES, nx * ny, LANES), F32)],
        compiler_params=params(LARGE),
        cost_estimate=pl.CostEstimate(flops=3 * direct.size, bytes_accessed=2 * direct.size, transcendentals=0),
        name="pack_direct",
    )(direct)


def mix_chord_kernel(lw, lo, hi, w_lo, w_hi):
    nm, nv, _, ny, nz = lo.shape
    rows = nv * ny

    def body(m, carry):
        for src, out in ((lo, w_lo), (hi, w_hi)):
            face = src[m, :, 0].reshape(rows, nz)
            out[m] = jnp.dot(lw[...], jnp.concatenate([face, face], axis=0), preferred_element_type=F32)
        return carry

    lax.fori_loop(0, nm, body, 0, unroll=4)


def mix_chord(lw, modes):
    nm, nv, nx, ny, nz = modes.shape
    block = (nm, nv, 1, ny, nz)
    w = sds((nm, nv * ny, nz), F32)
    whole = pl.BlockSpec(w.shape, lambda s: (0, 0, 0))
    return pl.pallas_call(
        mix_chord_kernel,
        grid=(1,),
        in_specs=[
            pl.BlockSpec(lw.shape, lambda s: (0, 0)),
            pl.BlockSpec(block, lambda s: (0, 0, 0, 0, 0)),
            pl.BlockSpec(block, lambda s: (0, 0, nx - 1, 0, 0)),
        ],
        out_specs=[whole, whole],
        out_shape=[w, w],
        compiler_params=params(LARGE),
        cost_estimate=pl.CostEstimate(flops=10**8, bytes_accessed=6 * 10**6, transcendentals=0),
        name="mix_chord",
    )(lw, modes, modes)


def mix_normal_kernel(lw, src, w_lo, w_hi, scratch):
    group, nv, nx, ny, nz = src.shape

    def body(m, carry):
        lines = [edge_lines(src[m, i].astype(F32), scratch.at[i]) for i in range(nv)]
        for side, out in enumerate((w_lo, w_hi)):
            face = jnp.concatenate([line[side] for line in lines], axis=0).astype(BF16)
            out[m] = jnp.dot(lw[...], jnp.concatenate([face, face], axis=0), preferred_element_type=F32)
        return carry

    lax.fori_loop(0, group, body, 0, unroll=2)


def mix_normal(lw, modes):
    nm, nv, nx, ny, nz = modes.shape
    w = sds((nm, nv * nx, nz), F32)
    out = pl.BlockSpec((GROUP, nv * nx, nz), lambda s: (s, 0, 0))
    return pl.pallas_call(
        mix_normal_kernel,
        grid=(nm // GROUP,),
        in_specs=[
            pl.BlockSpec(lw.shape, lambda s: (0, 0)),
            pl.BlockSpec((GROUP, nv, nx, ny, nz), lambda s: (s, 0, 0, 0, 0)),
        ],
        out_specs=[out, out],
        out_shape=[w, w],
        scratch_shapes=[pltpu.VMEM((nv, nz // LANES, nx * ny, LANES), F32)],
        compiler_params=params(LARGE),
        cost_estimate=pl.CostEstimate(flops=3 * modes.size, bytes_accessed=3 * modes.size, transcendentals=0),
        name="mix_normal",
    )(lw, modes)


def summed(pick, amp, u, w, j):
    nm = w.shape[0]
    n, nz = u.shape[2:]
    total = jnp.zeros((n, nz), F32)
    for m in range(nm):
        total = total + amp[m] * (u[m, j].astype(F32) * w[pick[m], pl.ds(pl.multiple_of(j * n, n), n), :])
    return total


def whole_of(ref, part):
    n = ref.shape[0] - TAIL + 2 * part
    return ref[n].astype(F32) + ref[n + 1].astype(F32)


def faces_kernel(pick, amp, base, *refs):
    u = refs[0:4]
    w = refs[4:8]
    tails = refs[8:12]
    scratch = refs[12]
    nv, nx, ny, nz = base.shape

    def body(j, carry):
        lines = [base[j, 0], base[j, nx - 1], *edge_lines(base[j], scratch)]
        for f in range(4):
            for n, value in enumerate((summed(pick, amp, u[f], w[f], j), lines[f])):
                hi = value.astype(BF16)
                tails[f][2 * n, j] = hi
                tails[f][2 * n + 1, j] = (value - hi.astype(F32)).astype(BF16)
        return carry

    lax.fori_loop(0, nv, body, 0)


def faces(pick, amp, base, u_faces, w_faces):
    nv, nx, ny, nz = base.shape
    whole = lambda a: pl.BlockSpec(a.shape, lambda s: (0,) * a.ndim)
    return pl.pallas_call(
        faces_kernel,
        grid=(1,),
        in_specs=[in_smem()] * 2 + [whole(a) for a in (base, *u_faces, *w_faces)],
        out_specs=[pl.BlockSpec((TAIL,) + a.shape[1:], lambda s: (a.shape[0] // TAIL - 1, 0, 0, 0)) for a in u_faces],
        out_shape=[sds(a.shape, BF16) for a in u_faces],
        input_output_aliases={3: 0, 4: 1, 5: 2, 6: 3},
        scratch_shapes=[pltpu.VMEM((nz // LANES, nx * ny, LANES), F32)],
        compiler_params=params(36),
        name="faces",
    )(pick, amp, base, *u_faces, *w_faces)


def row_of(shape, n):
    return lax.broadcasted_iota(jnp.int32, shape, 0) % n


def diff_lanes(a):
    n = a.shape[-1]
    return pltpu.roll(a, n - 1, a.ndim - 1) - pltpu.roll(a, 1, a.ndim - 1)


def diff_rows(a, n, lo, hi):
    rows = a.shape[0]
    row = row_of(a.shape, n)
    return jnp.where(row == n - 1, hi, pltpu.roll(a, rows - 1, 0)) - jnp.where(row == 0, lo, pltpu.roll(a, 1, 0))


def main_kernel(pick, amp, lw, u_hbm, q_hbm, out, u_buf, q_buf, even, odd, u_even, u_odd, acc, c0, u_sem, q_sem):
    nx, nm, nv, ny, nz = u_buf.shape
    rows = nv * ny

    def u_copy(p):
        return pltpu.make_async_copy(u_hbm.at[:, :, p], u_buf.at[p], u_sem.at[p])

    def q_copy(p):
        return pltpu.make_async_copy(q_hbm.at[:, :, p], q_buf.at[p], q_sem.at[p])

    for p in range(nx):
        u_copy(p).start()
        q_copy(p).start()
    c0[0] = jnp.zeros((rows, nz), F32)
    c0[nx + 1] = jnp.zeros((rows, nz), F32)

    def products(p, m, dest):
        qm = q_buf[p, pick[m]].reshape(rows, nz)
        dest[m] = jnp.dot(lw[...], jnp.concatenate([qm, qm], axis=0), preferred_element_type=F32)

    def plane(p, src, dest, u_src, u_dest):
        after = jnp.minimum(p + 1, nx - 1)

        @pl.when(p < nx - 1)
        def _():
            u_copy(after).wait()
            q_copy(after).wait()

        acc[...] = jnp.zeros_like(acc)

        def body(step, carry):
            for k in range(GROUP):
                products(after, step * GROUP + k, dest)
            for j in range(nv):
                at = slice(j * ny, (j + 1) * ny)
                sums = [acc[n, at] for n in range(6)]
                for k in range(GROUP):
                    m = step * GROUP + k
                    w0, w1, w2 = (src[m, n * rows + j * ny : n * rows + (j + 1) * ny] for n in range(3))
                    u = u_src[m, at]
                    following = u_buf[after, m, j].astype(F32) * amp[m]
                    dx = following - u_dest[m, at]
                    u_dest[m, at] = following
                    down1 = pltpu.roll(w1, 1, 0) - w1
                    down2 = pltpu.roll(w2, 1, 1) - w2
                    up1 = pltpu.roll(down1, ny - 1, 0)
                    up2 = pltpu.roll(down2, nz - 1, 1)
                    terms = [dx * w0, u * w0, u * down1, u * up1, u * down2, u * up2]
                    sums = [v + t for v, t in zip(sums, terms)]
                for n in range(6):
                    acc[n, at] = sums[n]
            return carry

        lax.fori_loop(0, nm // GROUP, body, 0)
        last = jnp.where(p == nx - 1, 1.0, 0.0)
        c0[p + 1] = acc[1]
        row = row_of((rows, nz), ny)
        h = acc[0] - last * acc[1] + pltpu.roll(acc[4], nz - 1, 1) + pltpu.roll(acc[5], 1, 1)
        h = h + jnp.where(row == ny - 1, 0.0, pltpu.roll(acc[2], rows - 1, 0))
        out[p] = h + jnp.where(row == 0, 0.0, pltpu.roll(acc[3], 1, 0))

    u_copy(0).wait()
    q_copy(0).wait()
    u_odd[...] = jnp.zeros_like(u_odd)

    def first(m, carry):
        products(0, m, even)
        u_even[m] = u_buf[0, m].reshape(rows, nz).astype(F32) * amp[m]
        return carry

    lax.fori_loop(0, nm, first, 0, unroll=GROUP)

    def pair(i, carry):
        plane(2 * i, even, odd, u_even, u_odd)
        plane(2 * i + 1, odd, even, u_odd, u_even)
        return carry

    lax.fori_loop(0, nx // 2, pair, 0)

    def finish(p, carry):
        out[p] = out[p] - c0[p + 2] + c0[p]
        return carry

    lax.fori_loop(0, nx, finish, 0, unroll=4)


def main(pick, amp, lw, direct, adjoint):
    nm, nv, nx, ny, nz = direct.shape
    rows = nv * ny
    buf = pltpu.VMEM((nx, nm, nv, ny, nz), BF16)
    return pl.pallas_call(
        main_kernel,
        in_specs=[in_smem(), in_smem(), in_vmem(), in_hbm(), in_hbm()],
        out_specs=in_vmem(),
        out_shape=sds((nx, rows, nz), F32),
        scratch_shapes=[
            buf,
            buf,
            pltpu.VMEM((nm, 3 * rows, nz), F32),
            pltpu.VMEM((nm, 3 * rows, nz), F32),
            pltpu.VMEM((nm, rows, nz), F32),
            pltpu.VMEM((nm, rows, nz), F32),
            pltpu.VMEM((6, rows, nz), F32),
            pltpu.VMEM((nx + 2, rows, nz), F32),
            pltpu.SemaphoreType.DMA((nx,)),
            pltpu.SemaphoreType.DMA((nx,)),
        ],
        compiler_params=params(LARGE),
        cost_estimate=pl.CostEstimate(flops=10**6, bytes_accessed=10**5, transcendentals=0),
        name="main",
    )(pick, amp, lw, direct, adjoint)


def weight_of(cells):
    return jnp.where(cells == 0, 1.0, jnp.where(cells == 1, 0.5, 0.0)).astype(F32)


def spread(ref, x, n):
    nv, _, nz = ref.shape
    return jnp.concatenate([jnp.broadcast_to(ref[j, pl.ds(x, 1), :], (n, nz)) for j in range(nv)], axis=0)


def write_lines(values, x, n, lo, hi):
    for j in range(lo.shape[0]):
        lo[j, pl.ds(x, 1), :] = values[j * n : j * n + 1]
        hi[j, pl.ds(x, 1), :] = values[(j + 1) * n - 1 : (j + 1) * n]


def boundary_kernel(scale, pick, amp, local, cell, *refs):
    w = refs[0:4]
    halo = [refs[4 + f] for f in (2, 3, 0, 1)]
    field, xlo, xhi, ylo, yhi = refs[8:13]
    base_halo = refs[13:17]
    add = refs[17:21]
    nx, rows, nz = local.shape
    nv = add[0].shape[0]
    ny = rows // nv
    for f in range(4):
        add[f][...] = whole_of(halo[f], 0)
        base_halo[f][...] = whole_of(halo[f], 1)

    def face(j, carry):
        for f in range(4):
            add[f][j] -= summed(pick, amp, halo[f], w[f], j)
        return carry

    lax.fori_loop(0, nv, face, 0)
    row = row_of((rows, nz), ny)

    def plane(x, carry):
        lo, hi = spread(add[2], x, ny), spread(add[3], x, ny)
        g = local[x] + jnp.where(row == 0, lo, 0.0) - jnp.where(row == ny - 1, hi, 0.0)
        g = g + jnp.where(x == 0, 1.0, 0.0) * add[0][...].reshape(rows, nz)
        g = g - jnp.where(x == nx - 1, 1.0, 0.0) * add[1][...].reshape(rows, nz)
        g = g * jnp.concatenate([weight_of(cell[x]) * scale] * nv, axis=0)
        field[x] = g
        write_lines(g, x, ny, ylo, yhi)
        return carry

    lax.fori_loop(0, nx, plane, 0, unroll=2)
    xlo[...] = field[0].reshape(xlo.shape)
    xhi[...] = field[nx - 1].reshape(xhi.shape)


def boundary(scale, pick, amp, local, cell, w_faces, halo):
    nx, rows, nz = local.shape
    face = [sds(a.shape[1:], F32) for a in halo]
    return pl.pallas_call(
        lambda *refs: boundary_kernel(scale, *refs),
        in_specs=[in_smem()] * 2 + [in_vmem()] * 10,
        out_specs=[in_vmem()] * 9,
        out_shape=[sds(local.shape, F32)] + face * 2,
        scratch_shapes=[pltpu.VMEM(f.shape, F32) for f in face],
        compiler_params=params(28),
        name="boundary",
    )(pick, amp, local, cell, *w_faces, *halo[2:], *halo[:2])


def mix_rows(lw, values):
    hi = values.astype(BF16)
    lo = (values - hi.astype(F32)).astype(BF16)
    return jnp.dot(lw, jnp.concatenate([hi, lo, hi], axis=0), preferred_element_type=F32)


def step_kernel(last, lw, lw_y, base, cell, field, *refs):
    got = [refs[f] for f in (2, 3, 0, 1)]
    got_base = refs[4:8]
    out = refs[8]
    faces = refs[9:13]
    b_pad, c0, bh_lo, bh_hi, ch_lo, ch_hi = refs[-6:]
    nv, nx, ny, nz = base.shape
    rows = nv * ny
    for f, at in ((0, 0), (1, nx + 1)):
        b = got_base[f][...].reshape(rows, nz)
        b_pad[at] = b
        c0[at] = b * mix_rows(lw[:rows], got[f][...].reshape(rows, nz))
    for f, bh, ch in ((2, bh_lo, ch_lo), (3, bh_hi, ch_hi)):
        b = got_base[f][...]
        bh[...] = b
        ch[...] = b * mix_rows(lw_y[...], got[f][...].reshape(nv * nx, nz)).reshape(nv, nx, nz)

    def fill(x, carry):
        b_pad[x + 1] = base[:, x].reshape(rows, nz)
        return carry

    lax.fori_loop(0, nx, fill, 0, unroll=4)

    def plane(x, carry):
        w = mix_rows(lw[...], field[x])
        w0, w1, w2 = (w[n * rows : (n + 1) * rows] for n in range(3))
        b = b_pad[x + 1]
        c0[x + 1] = b * w0
        h = (b_pad[x + 2] - b_pad[x]) * w0
        h = h + diff_rows(b, ny, spread(bh_lo, x, ny), spread(bh_hi, x, ny)) * w1
        h = h - diff_rows(b * w1, ny, spread(ch_lo, x, ny), spread(ch_hi, x, ny))
        h = h + diff_lanes(b) * w2 - diff_lanes(b * w2)
        if last:
            out[:, x] = h.reshape(nv, ny, nz)
        else:
            out[x] = h
        return carry

    lax.fori_loop(0, nx, plane, 0, unroll=4)

    def finish(x, carry):
        change = c0[x] - c0[x + 2]
        if last:
            out[:, x] = out[:, x] + change.reshape(nv, ny, nz)
        else:
            g = (out[x] + change) * jnp.concatenate([weight_of(cell[x])] * nv, axis=0)
            out[x] = g
            write_lines(g, x, ny, faces[2], faces[3])
        return carry

    lax.fori_loop(0, nx, finish, 0, unroll=4)
    if not last:
        faces[0][...] = out[0].reshape(nv, ny, nz)
        faces[1][...] = out[nx - 1].reshape(nv, ny, nz)


def apply_step(last, lw, lw_y, base, cell, field, got_base, got):
    nv, nx, ny, nz = base.shape
    rows = nv * ny
    face = [] if last else [sds((nv, n, nz), F32) for n in (ny, ny, nx, nx)]
    line = pltpu.VMEM((nv, nx, nz), F32)
    padded = pltpu.VMEM((nx + 2, rows, nz), F32)
    return pl.pallas_call(
        lambda *refs: step_kernel(last, *refs),
        in_specs=[in_vmem()] * 13,
        out_specs=[in_vmem()] * (1 + len(face)),
        out_shape=[sds(base.shape if last else field.shape, F32)] + face,
        scratch_shapes=[padded, padded, line, line, line, line],
        compiler_params=params(28),
        name="step_two" if last else "step_one",
    )(lw, lw_y, base, cell, field, *got[2:], *got[:2], *got_base)


def exchange_axis(axis, lo, hi):
    count = lax.axis_size(axis)
    up = [(i, i + 1) for i in range(count - 1)]
    down = [(i + 1, i) for i in range(count - 1)]
    return [lax.ppermute(hi, axis, up), lax.ppermute(lo, axis, down)]


def exchange(arrays):
    normal = exchange_axis("normal", *arrays[2:])
    return exchange_axis("chord", *arrays[:2]) + normal


def sum_over(axis, values):
    count = lax.axis_size(axis)
    if count & (count - 1):
        return lax.psum(values, axis)
    bit = 1
    while bit < count:
        values = values + lax.ppermute(values, axis, [(i, i ^ bit) for i in range(count)])
        bit *= 2
    return values


def kron_rows(mix, n):
    nv = mix.shape[1]
    hi = lax.reduce_precision(mix, 8, 7)
    lo = lax.reduce_precision(mix - hi, 8, 7)
    small = jnp.concatenate([hi.transpose(0, 2, 1), lo.transpose(0, 2, 1)], axis=2)
    rows, cols = np.arange(nv * n), np.arange(2 * nv * n)
    left = jnp.asarray((rows[:, None] // n == np.arange(nv)[None]).astype(np.float32))
    right = jnp.asarray((cols[None] // n == np.arange(2 * nv)[:, None]).astype(np.float32))
    return jnp.einsum("rj,djc,ck->drk", left, small, right, precision=lax.Precision.HIGHEST)


def within(wide, n, cells):
    return (wide * jnp.asarray(np.tile(cells, (wide.shape[-2] // n, wide.shape[-1] // n)))).astype(BF16)


def step_rows(lw):
    half = lw.shape[-1] // 2
    return jnp.concatenate([lw[..., :half], lw[..., :half], lw[..., half:]], axis=-1)


def per_device(direct, adjoint, base, cell, pick, mix):
    nm, nv, nx, ny, nz = direct.shape
    cells_all = nv * nx * ny * nz * lax.axis_size("chord") * lax.axis_size("normal")
    *own, sums = pack(direct)
    sums = sum_over("chord", sum_over("normal", jnp.sum(sums, axis=1)))
    amp = lax.rsqrt(sums / cells_all + 1e-06)
    wide = kron_rows(mix, ny)
    lw_y = within(wide, ny, np.eye(ny, dtype=np.float32))
    lw_x = lw_y if nx == ny else within(kron_rows(mix, nx), nx, np.eye(nx, dtype=np.float32))
    w_faces = [*mix_chord(lw_y[0], adjoint), *mix_normal(lw_x[1], adjoint)]
    halo = exchange(faces(pick, amp, base, own, w_faces))
    local = main(pick, amp, lw_y.reshape(3 * nv * ny, -1), direct, adjoint)
    field, *sides = boundary(1.0 / nm, pick, amp, local, cell, w_faces, halo)
    sides, base_halo = sides[:4], sides[4:]
    lw_step = step_rows(lw_y.reshape(3 * nv * ny, -1))
    lw_line = step_rows(lw_x[1])
    field, *sides = apply_step(False, lw_step, lw_line, base, cell, field, base_halo, exchange(sides))
    return apply_step(True, lw_step, lw_line, base, cell, field, base_halo, exchange(sides))[0]


def solution(mesh):
    return jax.shard_map(
        per_device,
        mesh=mesh,
        in_specs=(
            P(None, None, "chord", "normal", None),
            P(None, None, "chord", "normal", None),
            P(None, "chord", "normal", None),
            P("chord", "normal", None),
            P(),
            P(),
        ),
        out_specs=P(None, "chord", "normal", None),
        check_vma=False,
    )
```

```python
import jax
import jax.numpy as jnp
import numpy as np
from jax import lax
from jax.experimental import pallas as pl
from jax.experimental.pallas import tpu as pltpu
from jax.sharding import PartitionSpec as P

F32 = jnp.float32
BF16 = jnp.bfloat16
LANES = 128
MIB = 1024 * 1024
GROUP = 4
TAIL = 4
LARGE = 51


def in_vmem():
    return pl.BlockSpec(memory_space=pltpu.VMEM)


def in_smem():
    return pl.BlockSpec(memory_space=pltpu.SMEM)


def in_hbm():
    return pl.BlockSpec(memory_space=pl.ANY)


def sds(shape, dtype):
    return jax.ShapeDtypeStruct(shape, dtype)


def params(mib):
    return pltpu.CompilerParams(vmem_limit_bytes=mib * MIB)


def edge_lines(cells, scratch):
    nx, ny, nz = cells.shape
    flat = cells.reshape(nx * ny, nz)
    out = ([], [])
    for h in range(nz // LANES):
        scratch[h] = flat[:, h * LANES : (h + 1) * LANES]
        for side, first in enumerate((0, ny - 1)):
            out[side].append(scratch[h, pl.ds(first, nx, stride=ny), :])
    return [jnp.concatenate(o, axis=1) for o in out]


def direct_kernel(src, xlo, xhi, ylo, yhi, energy, scratch):
    group, nv, nx, ny, nz = src.shape

    def body(m, carry):
        xlo[m] = src[m, :, 0]
        xhi[m] = src[m, :, nx - 1]
        total = jnp.zeros((ny, nz), F32)
        for i in range(nv):
            cells = src[m, i].astype(F32)
            lo, hi = edge_lines(cells, scratch.at[i])
            ylo[m, i] = lo.astype(BF16)
            yhi[m, i] = hi.astype(BF16)
            total = total + jnp.sum(cells * cells, axis=0)
        line = jnp.sum(total, axis=0, keepdims=True)
        line = sum(line[:, h : h + LANES] for h in range(0, nz, LANES))
        energy[pl.ds(pl.program_id(0) * group + m, 1), :] = line
        return carry

    lax.fori_loop(0, group, body, 0, unroll=2)


def pack(direct):
    nm, nv, nx, ny, nz = direct.shape
    sizes = (ny, ny, nx, nx)
    return pl.pallas_call(
        direct_kernel,
        grid=(nm // GROUP,),
        in_specs=[pl.BlockSpec((GROUP, nv, nx, ny, nz), lambda s: (s, 0, 0, 0, 0))],
        out_specs=[pl.BlockSpec((GROUP, nv, n, nz), lambda s: (s, 0, 0, 0)) for n in sizes]
        + [pl.BlockSpec((nm, LANES), lambda s: (0, 0))],
        out_shape=[sds((nm + TAIL, nv, n, nz), BF16) for n in sizes] + [sds((nm, LANES), F32)],
        scratch_shapes=[pltpu.VMEM((nv, nz // LANES, nx * ny, LANES), F32)],
        compiler_params=params(LARGE),
        cost_estimate=pl.CostEstimate(flops=3 * direct.size, bytes_accessed=2 * direct.size, transcendentals=0),
        name="pack_direct",
    )(direct)


def mix_chord_kernel(lw, lo, hi, w_lo, w_hi):
    nm, nv, _, ny, nz = lo.shape
    rows = nv * ny

    def body(m, carry):
        for src, out in ((lo, w_lo), (hi, w_hi)):
            face = src[m, :, 0].reshape(rows, nz)
            out[m] = jnp.dot(lw[...], jnp.concatenate([face, face], axis=0), preferred_element_type=F32)
        return carry

    lax.fori_loop(0, nm, body, 0, unroll=4)


def mix_chord(lw, modes):
    nm, nv, nx, ny, nz = modes.shape
    block = (nm, nv, 1, ny, nz)
    w = sds((nm, nv * ny, nz), F32)
    whole = pl.BlockSpec(w.shape, lambda s: (0, 0, 0))
    return pl.pallas_call(
        mix_chord_kernel,
        grid=(1,),
        in_specs=[
            pl.BlockSpec(lw.shape, lambda s: (0, 0)),
            pl.BlockSpec(block, lambda s: (0, 0, 0, 0, 0)),
            pl.BlockSpec(block, lambda s: (0, 0, nx - 1, 0, 0)),
        ],
        out_specs=[whole, whole],
        out_shape=[w, w],
        compiler_params=params(LARGE),
        cost_estimate=pl.CostEstimate(flops=10**8, bytes_accessed=6 * 10**6, transcendentals=0),
        name="mix_chord",
    )(lw, modes, modes)


def mix_normal_kernel(lw, src, w_lo, w_hi, scratch):
    group, nv, nx, ny, nz = src.shape

    def body(m, carry):
        lines = [edge_lines(src[m, i].astype(F32), scratch.at[i]) for i in range(nv)]
        for side, out in enumerate((w_lo, w_hi)):
            face = jnp.concatenate([line[side] for line in lines], axis=0).astype(BF16)
            out[m] = jnp.dot(lw[...], jnp.concatenate([face, face], axis=0), preferred_element_type=F32)
        return carry

    lax.fori_loop(0, group, body, 0, unroll=2)


def mix_normal(lw, modes):
    nm, nv, nx, ny, nz = modes.shape
    w = sds((nm, nv * nx, nz), F32)
    out = pl.BlockSpec((GROUP, nv * nx, nz), lambda s: (s, 0, 0))
    return pl.pallas_call(
        mix_normal_kernel,
        grid=(nm // GROUP,),
        in_specs=[
            pl.BlockSpec(lw.shape, lambda s: (0, 0)),
            pl.BlockSpec((GROUP, nv, nx, ny, nz), lambda s: (s, 0, 0, 0, 0)),
        ],
        out_specs=[out, out],
        out_shape=[w, w],
        scratch_shapes=[pltpu.VMEM((nv, nz // LANES, nx * ny, LANES), F32)],
        compiler_params=params(LARGE),
        cost_estimate=pl.CostEstimate(flops=3 * modes.size, bytes_accessed=3 * modes.size, transcendentals=0),
        name="mix_normal",
    )(lw, modes)


def summed(pick, amp, u, w, j):
    nm = w.shape[0]
    n, nz = u.shape[2:]
    total = jnp.zeros((n, nz), F32)
    for m in range(nm):
        total = total + amp[m] * (u[m, j].astype(F32) * w[pick[m], pl.ds(pl.multiple_of(j * n, n), n), :])
    return total


def whole_of(ref, part):
    n = ref.shape[0] - TAIL + 2 * part
    return ref[n].astype(F32) + ref[n + 1].astype(F32)


def faces_kernel(pick, amp, base, *refs):
    u = refs[0:4]
    w = refs[4:8]
    tails = refs[8:12]
    scratch = refs[12]
    nv, nx, ny, nz = base.shape

    def body(j, carry):
        lines = [base[j, 0], base[j, nx - 1], *edge_lines(base[j], scratch)]
        for f in range(4):
            for n, value in enumerate((summed(pick, amp, u[f], w[f], j), lines[f])):
                hi = value.astype(BF16)
                tails[f][2 * n, j] = hi
                tails[f][2 * n + 1, j] = (value - hi.astype(F32)).astype(BF16)
        return carry

    lax.fori_loop(0, nv, body, 0)


def faces(pick, amp, base, u_faces, w_faces):
    nv, nx, ny, nz = base.shape
    whole = lambda a: pl.BlockSpec(a.shape, lambda s: (0,) * a.ndim)
    return pl.pallas_call(
        faces_kernel,
        grid=(1,),
        in_specs=[in_smem()] * 2 + [whole(a) for a in (base, *u_faces, *w_faces)],
        out_specs=[pl.BlockSpec((TAIL,) + a.shape[1:], lambda s: (a.shape[0] // TAIL - 1, 0, 0, 0)) for a in u_faces],
        out_shape=[sds(a.shape, BF16) for a in u_faces],
        input_output_aliases={3: 0, 4: 1, 5: 2, 6: 3},
        scratch_shapes=[pltpu.VMEM((nz // LANES, nx * ny, LANES), F32)],
        compiler_params=params(36),
        name="faces",
    )(pick, amp, base, *u_faces, *w_faces)


def row_of(shape, n):
    return lax.broadcasted_iota(jnp.int32, shape, 0) % n


def diff_lanes(a):
    n = a.shape[-1]
    return pltpu.roll(a, n - 1, a.ndim - 1) - pltpu.roll(a, 1, a.ndim - 1)


def diff_rows(a, n, lo, hi):
    rows = a.shape[0]
    row = row_of(a.shape, n)
    return jnp.where(row == n - 1, hi, pltpu.roll(a, rows - 1, 0)) - jnp.where(row == 0, lo, pltpu.roll(a, 1, 0))


def main_kernel(pick, amp, lw, u_hbm, q_hbm, out, u_buf, q_buf, even, odd, u_even, u_odd, acc, c0, u_sem, q_sem):
    nx, nm, nv, ny, nz = u_buf.shape
    rows = nv * ny

    def u_copy(p):
        return pltpu.make_async_copy(u_hbm.at[:, :, p], u_buf.at[p], u_sem.at[p])

    def q_copy(p):
        return pltpu.make_async_copy(q_hbm.at[:, :, p], q_buf.at[p], q_sem.at[p])

    for p in range(nx):
        u_copy(p).start()
        q_copy(p).start()
    c0[0] = jnp.zeros((rows, nz), F32)
    c0[nx + 1] = jnp.zeros((rows, nz), F32)

    def products(p, m, dest):
        qm = q_buf[p, pick[m]].reshape(rows, nz)
        dest[m] = jnp.dot(lw[...], jnp.concatenate([qm, qm], axis=0), preferred_element_type=F32)

    def plane(p, src, dest, u_src, u_dest):
        after = jnp.minimum(p + 1, nx - 1)

        @pl.when(p < nx - 1)
        def _():
            u_copy(after).wait()
            q_copy(after).wait()

        acc[...] = jnp.zeros_like(acc)

        def body(step, carry):
            for j in range(nv):
                if j < GROUP:
                    products(after, step * GROUP + j, dest)
                at = slice(j * ny, (j + 1) * ny)
                sums = [acc[n, at] for n in range(5)]
                for k in range(GROUP):
                    m = step * GROUP + k
                    w0, down, up, w2 = (src[m, n * rows + j * ny : n * rows + (j + 1) * ny] for n in range(4))
                    u = u_src[m, at]
                    following = u_buf[after, m, j].astype(F32) * amp[m]
                    dx = following - u_dest[m, at]
                    u_dest[m, at] = following
                    terms = [dx * w0 + diff_lanes(u) * w2, u * w0, u * down, u * up, u * w2]
                    sums = [v + t for v, t in zip(sums, terms)]
                for n in range(5):
                    acc[n, at] = sums[n]
            for k in range(nv, GROUP):
                products(after, step * GROUP + k, dest)
            return carry

        lax.fori_loop(0, nm // GROUP, body, 0)
        last = jnp.where(p == nx - 1, 1.0, 0.0)
        c0[p + 1] = acc[1]
        row = row_of((rows, nz), ny)
        h = acc[0] - diff_lanes(acc[4]) - last * acc[1]
        h = h + jnp.where(row == ny - 1, 0.0, pltpu.roll(acc[2], rows - 1, 0))
        out[p] = h + jnp.where(row == 0, 0.0, pltpu.roll(acc[3], 1, 0))

    u_copy(0).wait()
    q_copy(0).wait()
    u_odd[...] = jnp.zeros_like(u_odd)

    def first(m, carry):
        products(0, m, even)
        u_even[m] = u_buf[0, m].reshape(rows, nz).astype(F32) * amp[m]
        return carry

    lax.fori_loop(0, nm, first, 0, unroll=GROUP)

    def pair(i, carry):
        plane(2 * i, even, odd, u_even, u_odd)
        plane(2 * i + 1, odd, even, u_odd, u_even)
        return carry

    lax.fori_loop(0, nx // 2, pair, 0)

    def finish(p, carry):
        out[p] = out[p] - c0[p + 2] + c0[p]
        return carry

    lax.fori_loop(0, nx, finish, 0, unroll=4)


def main(pick, amp, lw, direct, adjoint):
    nm, nv, nx, ny, nz = direct.shape
    rows = nv * ny
    buf = pltpu.VMEM((nx, nm, nv, ny, nz), BF16)
    return pl.pallas_call(
        main_kernel,
        in_specs=[in_smem(), in_smem(), in_vmem(), in_hbm(), in_hbm()],
        out_specs=in_vmem(),
        out_shape=sds((nx, rows, nz), F32),
        scratch_shapes=[
            buf,
            buf,
            pltpu.VMEM((nm, 4 * rows, nz), F32),
            pltpu.VMEM((nm, 4 * rows, nz), F32),
            pltpu.VMEM((nm, rows, nz), F32),
            pltpu.VMEM((nm, rows, nz), F32),
            pltpu.VMEM((5, rows, nz), F32),
            pltpu.VMEM((nx + 2, rows, nz), F32),
            pltpu.SemaphoreType.DMA((nx,)),
            pltpu.SemaphoreType.DMA((nx,)),
        ],
        compiler_params=params(LARGE),
        cost_estimate=pl.CostEstimate(flops=10**6, bytes_accessed=10**5, transcendentals=0),
        name="main",
    )(pick, amp, lw, direct, adjoint)


def weight_of(cells):
    return jnp.where(cells == 0, 1.0, jnp.where(cells == 1, 0.5, 0.0)).astype(F32)


def spread(ref, x, n):
    nv, _, nz = ref.shape
    return jnp.concatenate([jnp.broadcast_to(ref[j, pl.ds(x, 1), :], (n, nz)) for j in range(nv)], axis=0)


def write_lines(values, x, n, lo, hi):
    for j in range(lo.shape[0]):
        lo[j, pl.ds(x, 1), :] = values[j * n : j * n + 1]
        hi[j, pl.ds(x, 1), :] = values[(j + 1) * n - 1 : (j + 1) * n]


def boundary_kernel(scale, pick, amp, local, cell, *refs):
    w = refs[0:4]
    halo = [refs[4 + f] for f in (2, 3, 0, 1)]
    field, xlo, xhi, ylo, yhi = refs[8:13]
    base_halo = refs[13:17]
    add = refs[17:21]
    nx, rows, nz = local.shape
    nv = add[0].shape[0]
    ny = rows // nv
    for f in range(4):
        add[f][...] = whole_of(halo[f], 0)
        base_halo[f][...] = whole_of(halo[f], 1)

    def face(j, carry):
        for f in range(4):
            add[f][j] -= summed(pick, amp, halo[f], w[f], j)
        return carry

    lax.fori_loop(0, nv, face, 0)
    row = row_of((rows, nz), ny)

    def plane(x, carry):
        lo, hi = spread(add[2], x, ny), spread(add[3], x, ny)
        g = local[x] + jnp.where(row == 0, lo, 0.0) - jnp.where(row == ny - 1, hi, 0.0)
        g = g + jnp.where(x == 0, 1.0, 0.0) * add[0][...].reshape(rows, nz)
        g = g - jnp.where(x == nx - 1, 1.0, 0.0) * add[1][...].reshape(rows, nz)
        g = g * jnp.concatenate([weight_of(cell[x]) * scale] * nv, axis=0)
        field[x] = g
        write_lines(g, x, ny, ylo, yhi)
        return carry

    lax.fori_loop(0, nx, plane, 0, unroll=2)
    xlo[...] = field[0].reshape(xlo.shape)
    xhi[...] = field[nx - 1].reshape(xhi.shape)


def boundary(scale, pick, amp, local, cell, w_faces, halo):
    nx, rows, nz = local.shape
    face = [sds(a.shape[1:], F32) for a in halo]
    return pl.pallas_call(
        lambda *refs: boundary_kernel(scale, *refs),
        in_specs=[in_smem()] * 2 + [in_vmem()] * 10,
        out_specs=[in_vmem()] * 9,
        out_shape=[sds(local.shape, F32)] + face * 2,
        scratch_shapes=[pltpu.VMEM(f.shape, F32) for f in face],
        compiler_params=params(28),
        name="boundary",
    )(pick, amp, local, cell, *w_faces, *halo[2:], *halo[:2])


def mix_rows(lw, values):
    hi = values.astype(BF16)
    lo = (values - hi.astype(F32)).astype(BF16)
    return jnp.dot(lw, jnp.concatenate([hi, lo, hi], axis=0), preferred_element_type=F32)


def step_kernel(last, lw, lw_y, base, cell, field, *refs):
    got = [refs[f] for f in (2, 3, 0, 1)]
    got_base = refs[4:8]
    out = refs[8]
    faces = refs[9:13]
    b_pad, c0, bh_lo, bh_hi, ch_lo, ch_hi = refs[-6:]
    nv, nx, ny, nz = base.shape
    rows = nv * ny
    for f, at in ((0, 0), (1, nx + 1)):
        b = got_base[f][...].reshape(rows, nz)
        b_pad[at] = b
        c0[at] = b * mix_rows(lw[:rows], got[f][...].reshape(rows, nz))
    for f, bh, ch in ((2, bh_lo, ch_lo), (3, bh_hi, ch_hi)):
        b = got_base[f][...]
        bh[...] = b
        ch[...] = b * mix_rows(lw_y[...], got[f][...].reshape(nv * nx, nz)).reshape(nv, nx, nz)

    def fill(x, carry):
        b_pad[x + 1] = base[:, x].reshape(rows, nz)
        return carry

    lax.fori_loop(0, nx, fill, 0, unroll=4)

    def plane(x, carry):
        w = mix_rows(lw[...], field[x])
        w0, w1, w2 = (w[n * rows : (n + 1) * rows] for n in range(3))
        b = b_pad[x + 1]
        c0[x + 1] = b * w0
        h = (b_pad[x + 2] - b_pad[x]) * w0
        h = h + diff_rows(b, ny, spread(bh_lo, x, ny), spread(bh_hi, x, ny)) * w1
        h = h - diff_rows(b * w1, ny, spread(ch_lo, x, ny), spread(ch_hi, x, ny))
        h = h + diff_lanes(b) * w2 - diff_lanes(b * w2)
        if last:
            out[:, x] = h.reshape(nv, ny, nz)
        else:
            out[x] = h
        return carry

    lax.fori_loop(0, nx, plane, 0, unroll=4)

    def finish(x, carry):
        change = c0[x] - c0[x + 2]
        if last:
            out[:, x] = out[:, x] + change.reshape(nv, ny, nz)
        else:
            g = (out[x] + change) * jnp.concatenate([weight_of(cell[x])] * nv, axis=0)
            out[x] = g
            write_lines(g, x, ny, faces[2], faces[3])
        return carry

    lax.fori_loop(0, nx, finish, 0, unroll=4)
    if not last:
        faces[0][...] = out[0].reshape(nv, ny, nz)
        faces[1][...] = out[nx - 1].reshape(nv, ny, nz)


def apply_step(last, lw, lw_y, base, cell, field, got_base, got):
    nv, nx, ny, nz = base.shape
    rows = nv * ny
    face = [] if last else [sds((nv, n, nz), F32) for n in (ny, ny, nx, nx)]
    line = pltpu.VMEM((nv, nx, nz), F32)
    padded = pltpu.VMEM((nx + 2, rows, nz), F32)
    return pl.pallas_call(
        lambda *refs: step_kernel(last, *refs),
        in_specs=[in_vmem()] * 13,
        out_specs=[in_vmem()] * (1 + len(face)),
        out_shape=[sds(base.shape if last else field.shape, F32)] + face,
        scratch_shapes=[padded, padded, line, line, line, line],
        compiler_params=params(28),
        name="step_two" if last else "step_one",
    )(lw, lw_y, base, cell, field, *got[2:], *got[:2], *got_base)


def exchange_axis(axis, lo, hi):
    count = lax.axis_size(axis)
    up = [(i, i + 1) for i in range(count - 1)]
    down = [(i + 1, i) for i in range(count - 1)]
    return [lax.ppermute(hi, axis, up), lax.ppermute(lo, axis, down)]


def exchange(arrays):
    normal = exchange_axis("normal", *arrays[2:])
    return exchange_axis("chord", *arrays[:2]) + normal


def sum_over(axis, values):
    count = lax.axis_size(axis)
    if count & (count - 1):
        return lax.psum(values, axis)
    bit = 1
    while bit < count:
        values = values + lax.ppermute(values, axis, [(i, i ^ bit) for i in range(count)])
        bit *= 2
    return values


def kron_rows(mix, n):
    nv = mix.shape[1]
    hi = lax.reduce_precision(mix, 8, 7)
    lo = lax.reduce_precision(mix - hi, 8, 7)
    small = jnp.concatenate([hi.transpose(0, 2, 1), lo.transpose(0, 2, 1)], axis=2)
    rows, cols = np.arange(nv * n), np.arange(2 * nv * n)
    left = jnp.asarray((rows[:, None] // n == np.arange(nv)[None]).astype(np.float32))
    right = jnp.asarray((cols[None] // n == np.arange(2 * nv)[:, None]).astype(np.float32))
    return jnp.einsum("rj,djc,ck->drk", left, small, right, precision=lax.Precision.HIGHEST)


def within(wide, n, cells):
    return (wide * jnp.asarray(np.tile(cells, (wide.shape[-2] // n, wide.shape[-1] // n)))).astype(BF16)


def main_rows(wide, n):
    eye, below, above = (np.eye(n, k=k, dtype=np.float32) for k in (0, -1, 1))
    return jnp.concatenate([within(wide[d], n, c) for d, c in ((0, eye), (1, below - eye), (1, eye - above), (2, eye))], axis=0)


def step_rows(lw):
    half = lw.shape[-1] // 2
    return jnp.concatenate([lw[..., :half], lw[..., :half], lw[..., half:]], axis=-1)


def per_device(direct, adjoint, base, cell, pick, mix):
    nm, nv, nx, ny, nz = direct.shape
    cells_all = nv * nx * ny * nz * lax.axis_size("chord") * lax.axis_size("normal")
    *own, sums = pack(direct)
    sums = sum_over("chord", sum_over("normal", jnp.sum(sums, axis=1)))
    amp = lax.rsqrt(sums / cells_all + 1e-06)
    wide = kron_rows(mix, ny)
    lw_y = within(wide, ny, np.eye(ny, dtype=np.float32))
    lw_x = lw_y if nx == ny else within(kron_rows(mix, nx), nx, np.eye(nx, dtype=np.float32))
    w_faces = [*mix_chord(lw_y[0], adjoint), *mix_normal(lw_x[1], adjoint)]
    halo = exchange(faces(pick, amp, base, own, w_faces))
    local = main(pick, amp, main_rows(wide, ny), direct, adjoint)
    field, *sides = boundary(1.0 / nm, pick, amp, local, cell, w_faces, halo)
    sides, base_halo = sides[:4], sides[4:]
    lw_step = step_rows(lw_y.reshape(3 * nv * ny, -1))
    lw_line = step_rows(lw_x[1])
    field, *sides = apply_step(False, lw_step, lw_line, base, cell, field, base_halo, exchange(sides))
    return apply_step(True, lw_step, lw_line, base, cell, field, base_halo, exchange(sides))[0]


def solution(mesh):
    return jax.shard_map(
        per_device,
        mesh=mesh,
        in_specs=(
            P(None, None, "chord", "normal", None),
            P(None, None, "chord", "normal", None),
            P(None, "chord", "normal", None),
            P("chord", "normal", None),
            P(),
            P(),
        ),
        out_specs=P(None, "chord", "normal", None),
        check_vma=False,
    )
```

```python
import jax
import jax.numpy as jnp
import numpy as np
from jax import lax
from jax.experimental import pallas as pl
from jax.experimental.pallas import tpu as pltpu
from jax.sharding import PartitionSpec as P

F32 = jnp.float32
BF16 = jnp.bfloat16
LANES = 128
MIB = 1024 * 1024
GROUP = 4
TAIL = 4
TURN = 8
LARGE = 51


def in_vmem():
    return pl.BlockSpec(memory_space=pltpu.VMEM)


def in_smem():
    return pl.BlockSpec(memory_space=pltpu.SMEM)


def in_hbm():
    return pl.BlockSpec(memory_space=pl.ANY)


def sds(shape, dtype):
    return jax.ShapeDtypeStruct(shape, dtype)


def params(mib):
    return pltpu.CompilerParams(vmem_limit_bytes=mib * MIB)


def edge_lines(cells, scratch):
    nx, ny, nz = cells.shape
    flat = cells.reshape(nx * ny, nz)
    out = ([], [])
    for h in range(nz // LANES):
        scratch[h] = flat[:, h * LANES : (h + 1) * LANES]
        for side, first in enumerate((0, ny - 1)):
            out[side].append(scratch[h, pl.ds(first, nx, stride=ny), :])
    return [jnp.concatenate(o, axis=1) for o in out]


def direct_kernel(src, xlo, xhi, ylo, yhi, energy, scratch):
    group, nv, nx, ny, nz = src.shape

    def body(m, carry):
        xlo[m] = src[m, :, 0]
        xhi[m] = src[m, :, nx - 1]
        total = jnp.zeros((ny, nz), F32)
        for i in range(nv):
            cells = src[m, i].astype(F32)
            lo, hi = edge_lines(cells, scratch.at[i])
            ylo[m, i] = lo.astype(BF16)
            yhi[m, i] = hi.astype(BF16)
            total = total + jnp.sum(cells * cells, axis=0)
        line = jnp.sum(total, axis=0, keepdims=True)
        line = sum(line[:, h : h + LANES] for h in range(0, nz, LANES))
        energy[pl.ds(pl.program_id(0) * group + m, 1), :] = line
        return carry

    lax.fori_loop(0, group, body, 0, unroll=2)


def pack(direct):
    nm, nv, nx, ny, nz = direct.shape
    sizes = (ny, ny, nx, nx)
    return pl.pallas_call(
        direct_kernel,
        grid=(nm // GROUP,),
        in_specs=[pl.BlockSpec((GROUP, nv, nx, ny, nz), lambda s: (s, 0, 0, 0, 0))],
        out_specs=[pl.BlockSpec((GROUP, nv, n, nz), lambda s: (s, 0, 0, 0)) for n in sizes]
        + [pl.BlockSpec((nm, LANES), lambda s: (0, 0))],
        out_shape=[sds((nm + TAIL, nv, n, nz), BF16) for n in sizes] + [sds((nm, LANES), F32)],
        scratch_shapes=[pltpu.VMEM((nv, nz // LANES, nx * ny, LANES), F32)],
        compiler_params=params(LARGE),
        cost_estimate=pl.CostEstimate(flops=3 * direct.size, bytes_accessed=2 * direct.size, transcendentals=0),
        name="pack_direct",
    )(direct)


def mix_chord_kernel(lw, lo, hi, w_lo, w_hi):
    nm, nv, _, ny, nz = lo.shape
    rows = nv * ny

    def body(m, carry):
        for src, out in ((lo, w_lo), (hi, w_hi)):
            face = src[m, :, 0].reshape(rows, nz)
            out[m] = jnp.dot(lw[...], jnp.concatenate([face, face], axis=0), preferred_element_type=F32)
        return carry

    lax.fori_loop(0, nm, body, 0, unroll=4)


def mix_chord(lw, modes):
    nm, nv, nx, ny, nz = modes.shape
    block = (nm, nv, 1, ny, nz)
    w = sds((nm, nv * ny, nz), F32)
    whole = pl.BlockSpec(w.shape, lambda s: (0, 0, 0))
    return pl.pallas_call(
        mix_chord_kernel,
        grid=(1,),
        in_specs=[
            pl.BlockSpec(lw.shape, lambda s: (0, 0)),
            pl.BlockSpec(block, lambda s: (0, 0, 0, 0, 0)),
            pl.BlockSpec(block, lambda s: (0, 0, nx - 1, 0, 0)),
        ],
        out_specs=[whole, whole],
        out_shape=[w, w],
        compiler_params=params(LARGE),
        cost_estimate=pl.CostEstimate(flops=10**8, bytes_accessed=6 * 10**6, transcendentals=0),
        name="mix_chord",
    )(lw, modes, modes)


def mix_normal_kernel(lw, src, w_lo, w_hi, scratch):
    group, nv, nx, ny, nz = src.shape

    def body(m, carry):
        lines = [edge_lines(src[m, i].astype(F32), scratch.at[i]) for i in range(nv)]
        for side, out in enumerate((w_lo, w_hi)):
            face = jnp.concatenate([line[side] for line in lines], axis=0).astype(BF16)
            out[m] = jnp.dot(lw[...], jnp.concatenate([face, face], axis=0), preferred_element_type=F32)
        return carry

    lax.fori_loop(0, group, body, 0, unroll=2)


def mix_normal(lw, modes):
    nm, nv, nx, ny, nz = modes.shape
    w = sds((nm, nv * nx, nz), F32)
    out = pl.BlockSpec((GROUP, nv * nx, nz), lambda s: (s, 0, 0))
    return pl.pallas_call(
        mix_normal_kernel,
        grid=(nm // GROUP,),
        in_specs=[
            pl.BlockSpec(lw.shape, lambda s: (0, 0)),
            pl.BlockSpec((GROUP, nv, nx, ny, nz), lambda s: (s, 0, 0, 0, 0)),
        ],
        out_specs=[out, out],
        out_shape=[w, w],
        scratch_shapes=[pltpu.VMEM((nv, nz // LANES, nx * ny, LANES), F32)],
        compiler_params=params(LARGE),
        cost_estimate=pl.CostEstimate(flops=3 * modes.size, bytes_accessed=3 * modes.size, transcendentals=0),
        name="mix_normal",
    )(lw, modes)


def summed(pick, amp, u, w, j):
    nm = w.shape[0]
    n, nz = u.shape[2:]
    total = jnp.zeros((n, nz), F32)
    for m in range(nm):
        total = total + amp[m] * (u[m, j].astype(F32) * w[pick[m], pl.ds(pl.multiple_of(j * n, n), n), :])
    return total


def whole_of(ref, part):
    n = ref.shape[0] - TAIL + 2 * part
    return ref[n].astype(F32) + ref[n + 1].astype(F32)


def faces_kernel(pick, amp, base, *refs):
    u = refs[0:4]
    w = refs[4:8]
    tails = refs[8:12]
    scratch = refs[12]
    nv, nx, ny, nz = base.shape

    def body(j, carry):
        lines = [base[j, 0], base[j, nx - 1], *edge_lines(base[j], scratch)]
        for f in range(4):
            for n, value in enumerate((summed(pick, amp, u[f], w[f], j), lines[f])):
                hi = value.astype(BF16)
                tails[f][2 * n, j] = hi
                tails[f][2 * n + 1, j] = (value - hi.astype(F32)).astype(BF16)
        return carry

    lax.fori_loop(0, nv, body, 0)


def faces(pick, amp, base, u_faces, w_faces):
    nv, nx, ny, nz = base.shape
    whole = lambda a: pl.BlockSpec(a.shape, lambda s: (0,) * a.ndim)
    return pl.pallas_call(
        faces_kernel,
        grid=(1,),
        in_specs=[in_smem()] * 2 + [whole(a) for a in (base, *u_faces, *w_faces)],
        out_specs=[pl.BlockSpec((TAIL,) + a.shape[1:], lambda s: (a.shape[0] // TAIL - 1, 0, 0, 0)) for a in u_faces],
        out_shape=[sds(a.shape, BF16) for a in u_faces],
        input_output_aliases={3: 0, 4: 1, 5: 2, 6: 3},
        scratch_shapes=[pltpu.VMEM((nz // LANES, nx * ny, LANES), F32)],
        compiler_params=params(36),
        name="faces",
    )(pick, amp, base, *u_faces, *w_faces)


def row_of(shape, n):
    return lax.broadcasted_iota(jnp.int32, shape, 0) % n


def diff_lanes(a):
    n = a.shape[-1]
    return pltpu.roll(a, n - 1, a.ndim - 1) - pltpu.roll(a, 1, a.ndim - 1)


def diff_rows(a, n, lo, hi):
    rows = a.shape[0]
    row = row_of(a.shape, n)
    return jnp.where(row == n - 1, hi, pltpu.roll(a, rows - 1, 0)) - jnp.where(row == 0, lo, pltpu.roll(a, 1, 0))


def main_kernel(pick, amp, lw, u_hbm, q_hbm, out, u_buf, q_buf, even, odd, u_even, u_odd, acc, c0, u_sem, q_sem):
    nx, nm, nv, ny, nz = u_buf.shape
    rows = nv * ny

    def u_copy(p):
        return pltpu.make_async_copy(u_hbm.at[:, :, p], u_buf.at[p], u_sem.at[p])

    def q_copy(p):
        return pltpu.make_async_copy(q_hbm.at[:, :, p], q_buf.at[p], q_sem.at[p])

    for p in range(nx):
        u_copy(p).start()
        q_copy(p).start()
    c0[0] = jnp.zeros((rows, nz), F32)
    c0[nx + 1] = jnp.zeros((rows, nz), F32)

    def products(p, m, dest):
        qm = q_buf[p, pick[m]].reshape(rows, nz)
        dest[m] = jnp.dot(lw[...], jnp.concatenate([qm, qm], axis=0), preferred_element_type=F32)

    def plane(p, src, dest, u_src, u_dest):
        after = jnp.minimum(p + 1, nx - 1)

        @pl.when(p < nx - 1)
        def _():
            u_copy(after).wait()
            q_copy(after).wait()

        acc[...] = jnp.zeros_like(acc)

        def body(step, carry):
            for j in range(nv):
                for k in range(2 * j, min(2 * j + 2, TURN)):
                    products(after, step * TURN + k, dest)
                at = slice(j * ny, (j + 1) * ny)
                sums = [acc[n, at] for n in range(5)]
                for k in range(TURN):
                    m = step * TURN + k
                    w0, down, up, w2 = (src[m, n * rows + j * ny : n * rows + (j + 1) * ny] for n in range(4))
                    u = u_src[m, at]
                    following = u_buf[after, m, j].astype(F32) * amp[m]
                    dx = following - u_dest[m, at]
                    u_dest[m, at] = following
                    terms = [dx * w0 + diff_lanes(u) * w2, u * w0, u * down, u * up, u * w2]
                    sums = [v + t for v, t in zip(sums, terms)]
                for n in range(5):
                    acc[n, at] = sums[n]
            for k in range(2 * nv, TURN):
                products(after, step * TURN + k, dest)
            return carry

        lax.fori_loop(0, nm // TURN, body, 0)
        last = jnp.where(p == nx - 1, 1.0, 0.0)
        c0[p + 1] = acc[1]
        row = row_of((rows, nz), ny)
        h = acc[0] - diff_lanes(acc[4]) - last * acc[1]
        h = h + jnp.where(row == ny - 1, 0.0, pltpu.roll(acc[2], rows - 1, 0))
        out[p] = h + jnp.where(row == 0, 0.0, pltpu.roll(acc[3], 1, 0))

    u_copy(0).wait()
    q_copy(0).wait()
    u_odd[...] = jnp.zeros_like(u_odd)

    def first(m, carry):
        products(0, m, even)
        u_even[m] = u_buf[0, m].reshape(rows, nz).astype(F32) * amp[m]
        return carry

    lax.fori_loop(0, nm, first, 0, unroll=4)

    def pair(i, carry):
        plane(2 * i, even, odd, u_even, u_odd)
        plane(2 * i + 1, odd, even, u_odd, u_even)
        return carry

    lax.fori_loop(0, nx // 2, pair, 0)

    def finish(p, carry):
        out[p] = out[p] - c0[p + 2] + c0[p]
        return carry

    lax.fori_loop(0, nx, finish, 0, unroll=4)


def main(pick, amp, lw, direct, adjoint):
    nm, nv, nx, ny, nz = direct.shape
    rows = nv * ny
    buf = pltpu.VMEM((nx, nm, nv, ny, nz), BF16)
    return pl.pallas_call(
        main_kernel,
        in_specs=[in_smem(), in_smem(), in_vmem(), in_hbm(), in_hbm()],
        out_specs=in_vmem(),
        out_shape=sds((nx, rows, nz), F32),
        scratch_shapes=[
            buf,
            buf,
            pltpu.VMEM((nm, 4 * rows, nz), F32),
            pltpu.VMEM((nm, 4 * rows, nz), F32),
            pltpu.VMEM((nm, rows, nz), F32),
            pltpu.VMEM((nm, rows, nz), F32),
            pltpu.VMEM((5, rows, nz), F32),
            pltpu.VMEM((nx + 2, rows, nz), F32),
            pltpu.SemaphoreType.DMA((nx,)),
            pltpu.SemaphoreType.DMA((nx,)),
        ],
        compiler_params=params(LARGE),
        cost_estimate=pl.CostEstimate(flops=10**6, bytes_accessed=10**5, transcendentals=0),
        name="main",
    )(pick, amp, lw, direct, adjoint)


def weight_of(cells):
    return jnp.where(cells == 0, 1.0, jnp.where(cells == 1, 0.5, 0.0)).astype(F32)


def spread(ref, x, n):
    nv, _, nz = ref.shape
    return jnp.concatenate([jnp.broadcast_to(ref[j, pl.ds(x, 1), :], (n, nz)) for j in range(nv)], axis=0)


def write_lines(values, x, n, lo, hi):
    for j in range(lo.shape[0]):
        lo[j, pl.ds(x, 1), :] = values[j * n : j * n + 1]
        hi[j, pl.ds(x, 1), :] = values[(j + 1) * n - 1 : (j + 1) * n]


def boundary_kernel(scale, pick, amp, local, cell, *refs):
    w = refs[0:4]
    halo = [refs[4 + f] for f in (2, 3, 0, 1)]
    field, xlo, xhi, ylo, yhi = refs[8:13]
    base_halo = refs[13:17]
    add = refs[17:21]
    nx, rows, nz = local.shape
    nv = add[0].shape[0]
    ny = rows // nv
    for f in range(4):
        add[f][...] = whole_of(halo[f], 0)
        base_halo[f][...] = whole_of(halo[f], 1)

    def face(j, carry):
        for f in range(4):
            add[f][j] -= summed(pick, amp, halo[f], w[f], j)
        return carry

    lax.fori_loop(0, nv, face, 0)
    row = row_of((rows, nz), ny)

    def plane(x, carry):
        lo, hi = spread(add[2], x, ny), spread(add[3], x, ny)
        g = local[x] + jnp.where(row == 0, lo, 0.0) - jnp.where(row == ny - 1, hi, 0.0)
        g = g + jnp.where(x == 0, 1.0, 0.0) * add[0][...].reshape(rows, nz)
        g = g - jnp.where(x == nx - 1, 1.0, 0.0) * add[1][...].reshape(rows, nz)
        g = g * jnp.concatenate([weight_of(cell[x]) * scale] * nv, axis=0)
        field[x] = g
        write_lines(g, x, ny, ylo, yhi)
        return carry

    lax.fori_loop(0, nx, plane, 0, unroll=2)
    xlo[...] = field[0].reshape(xlo.shape)
    xhi[...] = field[nx - 1].reshape(xhi.shape)


def boundary(scale, pick, amp, local, cell, w_faces, halo):
    nx, rows, nz = local.shape
    face = [sds(a.shape[1:], F32) for a in halo]
    return pl.pallas_call(
        lambda *refs: boundary_kernel(scale, *refs),
        in_specs=[in_smem()] * 2 + [in_vmem()] * 10,
        out_specs=[in_vmem()] * 9,
        out_shape=[sds(local.shape, F32)] + face * 2,
        scratch_shapes=[pltpu.VMEM(f.shape, F32) for f in face],
        compiler_params=params(28),
        name="boundary",
    )(pick, amp, local, cell, *w_faces, *halo[2:], *halo[:2])


def mix_rows(lw, values):
    hi = values.astype(BF16)
    lo = (values - hi.astype(F32)).astype(BF16)
    return jnp.dot(lw, jnp.concatenate([hi, lo, hi], axis=0), preferred_element_type=F32)


def step_kernel(last, lw, lw_y, base, cell, field, *refs):
    got = [refs[f] for f in (2, 3, 0, 1)]
    got_base = refs[4:8]
    out = refs[8]
    faces = refs[9:13]
    b_pad, c0, bh_lo, bh_hi, ch_lo, ch_hi = refs[-6:]
    nv, nx, ny, nz = base.shape
    rows = nv * ny
    for f, at in ((0, 0), (1, nx + 1)):
        b = got_base[f][...].reshape(rows, nz)
        b_pad[at] = b
        c0[at] = b * mix_rows(lw[:rows], got[f][...].reshape(rows, nz))
    for f, bh, ch in ((2, bh_lo, ch_lo), (3, bh_hi, ch_hi)):
        b = got_base[f][...]
        bh[...] = b
        ch[...] = b * mix_rows(lw_y[...], got[f][...].reshape(nv * nx, nz)).reshape(nv, nx, nz)

    def fill(x, carry):
        b_pad[x + 1] = base[:, x].reshape(rows, nz)
        return carry

    lax.fori_loop(0, nx, fill, 0, unroll=4)

    def plane(x, carry):
        w = mix_rows(lw[...], field[x])
        w0, w1, w2 = (w[n * rows : (n + 1) * rows] for n in range(3))
        b = b_pad[x + 1]
        c0[x + 1] = b * w0
        h = (b_pad[x + 2] - b_pad[x]) * w0
        h = h + diff_rows(b, ny, spread(bh_lo, x, ny), spread(bh_hi, x, ny)) * w1
        h = h - diff_rows(b * w1, ny, spread(ch_lo, x, ny), spread(ch_hi, x, ny))
        h = h + diff_lanes(b) * w2 - diff_lanes(b * w2)
        if last:
            out[:, x] = h.reshape(nv, ny, nz)
        else:
            out[x] = h
        return carry

    lax.fori_loop(0, nx, plane, 0, unroll=4)

    def finish(x, carry):
        change = c0[x] - c0[x + 2]
        if last:
            out[:, x] = out[:, x] + change.reshape(nv, ny, nz)
        else:
            g = (out[x] + change) * jnp.concatenate([weight_of(cell[x])] * nv, axis=0)
            out[x] = g
            write_lines(g, x, ny, faces[2], faces[3])
        return carry

    lax.fori_loop(0, nx, finish, 0, unroll=4)
    if not last:
        faces[0][...] = out[0].reshape(nv, ny, nz)
        faces[1][...] = out[nx - 1].reshape(nv, ny, nz)


def apply_step(last, lw, lw_y, base, cell, field, got_base, got):
    nv, nx, ny, nz = base.shape
    rows = nv * ny
    face = [] if last else [sds((nv, n, nz), F32) for n in (ny, ny, nx, nx)]
    line = pltpu.VMEM((nv, nx, nz), F32)
    padded = pltpu.VMEM((nx + 2, rows, nz), F32)
    return pl.pallas_call(
        lambda *refs: step_kernel(last, *refs),
        in_specs=[in_vmem()] * 13,
        out_specs=[in_vmem()] * (1 + len(face)),
        out_shape=[sds(base.shape if last else field.shape, F32)] + face,
        scratch_shapes=[padded, padded, line, line, line, line],
        compiler_params=params(28),
        name="step_two" if last else "step_one",
    )(lw, lw_y, base, cell, field, *got[2:], *got[:2], *got_base)


def exchange_axis(axis, lo, hi):
    count = lax.axis_size(axis)
    up = [(i, i + 1) for i in range(count - 1)]
    down = [(i + 1, i) for i in range(count - 1)]
    return [lax.ppermute(hi, axis, up), lax.ppermute(lo, axis, down)]


def exchange(arrays):
    normal = exchange_axis("normal", *arrays[2:])
    return exchange_axis("chord", *arrays[:2]) + normal


def sum_over(axis, values):
    count = lax.axis_size(axis)
    if count & (count - 1):
        return lax.psum(values, axis)
    bit = 1
    while bit < count:
        values = values + lax.ppermute(values, axis, [(i, i ^ bit) for i in range(count)])
        bit *= 2
    return values


def kron_rows(mix, n):
    nv = mix.shape[1]
    hi = lax.reduce_precision(mix, 8, 7)
    lo = lax.reduce_precision(mix - hi, 8, 7)
    small = jnp.concatenate([hi.transpose(0, 2, 1), lo.transpose(0, 2, 1)], axis=2)
    rows, cols = np.arange(nv * n), np.arange(2 * nv * n)
    left = jnp.asarray((rows[:, None] // n == np.arange(nv)[None]).astype(np.float32))
    right = jnp.asarray((cols[None] // n == np.arange(2 * nv)[:, None]).astype(np.float32))
    return jnp.einsum("rj,djc,ck->drk", left, small, right, precision=lax.Precision.HIGHEST)


def within(wide, n, cells):
    return (wide * jnp.asarray(np.tile(cells, (wide.shape[-2] // n, wide.shape[-1] // n)))).astype(BF16)


def main_rows(wide, n):
    eye, below, above = (np.eye(n, k=k, dtype=np.float32) for k in (0, -1, 1))
    return jnp.concatenate([within(wide[d], n, c) for d, c in ((0, eye), (1, below - eye), (1, eye - above), (2, eye))], axis=0)


def step_rows(lw):
    half = lw.shape[-1] // 2
    return jnp.concatenate([lw[..., :half], lw[..., :half], lw[..., half:]], axis=-1)


def per_device(direct, adjoint, base, cell, pick, mix):
    nm, nv, nx, ny, nz = direct.shape
    cells_all = nv * nx * ny * nz * lax.axis_size("chord") * lax.axis_size("normal")
    *own, sums = pack(direct)
    sums = sum_over("chord", sum_over("normal", jnp.sum(sums, axis=1)))
    amp = lax.rsqrt(sums / cells_all + 1e-06)
    wide = kron_rows(mix, ny)
    lw_y = within(wide, ny, np.eye(ny, dtype=np.float32))
    lw_x = lw_y if nx == ny else within(kron_rows(mix, nx), nx, np.eye(nx, dtype=np.float32))
    w_faces = [*mix_chord(lw_y[0], adjoint), *mix_normal(lw_x[1], adjoint)]
    halo = exchange(faces(pick, amp, base, own, w_faces))
    local = main(pick, amp, main_rows(wide, ny), direct, adjoint)
    field, *sides = boundary(1.0 / nm, pick, amp, local, cell, w_faces, halo)
    sides, base_halo = sides[:4], sides[4:]
    lw_step = step_rows(lw_y.reshape(3 * nv * ny, -1))
    lw_line = step_rows(lw_x[1])
    field, *sides = apply_step(False, lw_step, lw_line, base, cell, field, base_halo, exchange(sides))
    return apply_step(True, lw_step, lw_line, base, cell, field, base_halo, exchange(sides))[0]


def solution(mesh):
    return jax.shard_map(
        per_device,
        mesh=mesh,
        in_specs=(
            P(None, None, "chord", "normal", None),
            P(None, None, "chord", "normal", None),
            P(None, "chord", "normal", None),
            P("chord", "normal", None),
            P(),
            P(),
        ),
        out_specs=P(None, "chord", "normal", None),
        check_vma=False,
    )
```

```python
import jax
import jax.numpy as jnp
import numpy as np
from jax import lax
from jax.experimental import pallas as pl
from jax.experimental.pallas import tpu as pltpu
from jax.sharding import PartitionSpec as P

F32 = jnp.float32
BF16 = jnp.bfloat16
LANES = 128
MIB = 1024 * 1024
GROUP = 4
TAIL = 4
TURN = 16
PACK = 2
LARGE = 51


def in_vmem():
    return pl.BlockSpec(memory_space=pltpu.VMEM)


def in_smem():
    return pl.BlockSpec(memory_space=pltpu.SMEM)


def in_hbm():
    return pl.BlockSpec(memory_space=pl.ANY)


def sds(shape, dtype):
    return jax.ShapeDtypeStruct(shape, dtype)


def params(mib):
    return pltpu.CompilerParams(vmem_limit_bytes=mib * MIB)


def edge_lines(cells, scratch):
    nx, ny, nz = cells.shape
    flat = cells.reshape(nx * ny, nz)
    out = ([], [])
    for h in range(nz // LANES):
        scratch[h] = flat[:, h * LANES : (h + 1) * LANES]
        for side, first in enumerate((0, ny - 1)):
            out[side].append(scratch[h, pl.ds(first, nx, stride=ny), :])
    return [jnp.concatenate(o, axis=1) for o in out]


def direct_kernel(src, xlo, xhi, ylo, yhi, energy, scratch):
    group, nv, nx, ny, nz = src.shape

    def body(m, carry):
        xlo[m] = src[m, :, 0]
        xhi[m] = src[m, :, nx - 1]
        total = jnp.zeros((ny, nz), F32)
        for i in range(nv):
            cells = src[m, i].astype(F32)
            lo, hi = edge_lines(cells, scratch.at[i])
            ylo[m, i] = lo.astype(BF16)
            yhi[m, i] = hi.astype(BF16)
            total = total + jnp.sum(cells * cells, axis=0)
        line = jnp.sum(total, axis=0, keepdims=True)
        line = sum(line[:, h : h + LANES] for h in range(0, nz, LANES))
        energy[pl.ds(pl.program_id(0) * group + m, 1), :] = line
        return carry

    lax.fori_loop(0, group, body, 0, unroll=2)


def pack(direct):
    nm, nv, nx, ny, nz = direct.shape
    sizes = (ny, ny, nx, nx)
    return pl.pallas_call(
        direct_kernel,
        grid=(nm // PACK,),
        in_specs=[pl.BlockSpec((PACK, nv, nx, ny, nz), lambda s: (s, 0, 0, 0, 0))],
        out_specs=[pl.BlockSpec((PACK, nv, n, nz), lambda s: (s, 0, 0, 0)) for n in sizes]
        + [pl.BlockSpec((nm, LANES), lambda s: (0, 0))],
        out_shape=[sds((nm + TAIL, nv, n, nz), BF16) for n in sizes] + [sds((nm, LANES), F32)],
        scratch_shapes=[pltpu.VMEM((nv, nz // LANES, nx * ny, LANES), F32)],
        compiler_params=params(LARGE),
        cost_estimate=pl.CostEstimate(flops=3 * direct.size, bytes_accessed=2 * direct.size, transcendentals=0),
        name="pack_direct",
    )(direct)


def mix_chord_kernel(lw, lo, hi, w_lo, w_hi):
    nm, nv, _, ny, nz = lo.shape
    rows = nv * ny

    def body(m, carry):
        for src, out in ((lo, w_lo), (hi, w_hi)):
            face = src[m, :, 0].reshape(rows, nz)
            out[m] = jnp.dot(lw[...], jnp.concatenate([face, face], axis=0), preferred_element_type=F32)
        return carry

    lax.fori_loop(0, nm, body, 0, unroll=4)


def mix_chord(lw, modes):
    nm, nv, nx, ny, nz = modes.shape
    block = (nm, nv, 1, ny, nz)
    w = sds((nm, nv * ny, nz), F32)
    whole = pl.BlockSpec(w.shape, lambda s: (0, 0, 0))
    return pl.pallas_call(
        mix_chord_kernel,
        grid=(1,),
        in_specs=[
            pl.BlockSpec(lw.shape, lambda s: (0, 0)),
            pl.BlockSpec(block, lambda s: (0, 0, 0, 0, 0)),
            pl.BlockSpec(block, lambda s: (0, 0, nx - 1, 0, 0)),
        ],
        out_specs=[whole, whole],
        out_shape=[w, w],
        compiler_params=params(LARGE),
        cost_estimate=pl.CostEstimate(flops=10**8, bytes_accessed=6 * 10**6, transcendentals=0),
        name="mix_chord",
    )(lw, modes, modes)


def mix_normal_kernel(lw, src, w_lo, w_hi, scratch):
    group, nv, nx, ny, nz = src.shape

    def body(m, carry):
        lines = [edge_lines(src[m, i].astype(F32), scratch.at[i]) for i in range(nv)]
        for side, out in enumerate((w_lo, w_hi)):
            face = jnp.concatenate([line[side] for line in lines], axis=0).astype(BF16)
            out[m] = jnp.dot(lw[...], jnp.concatenate([face, face], axis=0), preferred_element_type=F32)
        return carry

    lax.fori_loop(0, group, body, 0, unroll=2)


def mix_normal(lw, modes):
    nm, nv, nx, ny, nz = modes.shape
    w = sds((nm, nv * nx, nz), F32)
    out = pl.BlockSpec((PACK, nv * nx, nz), lambda s: (s, 0, 0))
    return pl.pallas_call(
        mix_normal_kernel,
        grid=(nm // PACK,),
        in_specs=[
            pl.BlockSpec(lw.shape, lambda s: (0, 0)),
            pl.BlockSpec((PACK, nv, nx, ny, nz), lambda s: (s, 0, 0, 0, 0)),
        ],
        out_specs=[out, out],
        out_shape=[w, w],
        scratch_shapes=[pltpu.VMEM((nv, nz // LANES, nx * ny, LANES), F32)],
        compiler_params=params(LARGE),
        cost_estimate=pl.CostEstimate(flops=3 * modes.size, bytes_accessed=3 * modes.size, transcendentals=0),
        name="mix_normal",
    )(lw, modes)


def summed(pick, amp, u, w, j):
    nm = w.shape[0]
    n, nz = u.shape[2:]
    total = jnp.zeros((n, nz), F32)
    for m in range(nm):
        total = total + amp[m] * (u[m, j].astype(F32) * w[pick[m], pl.ds(pl.multiple_of(j * n, n), n), :])
    return total


def whole_of(ref, part):
    n = ref.shape[0] - TAIL + 2 * part
    return ref[n].astype(F32) + ref[n + 1].astype(F32)


def faces_kernel(pick, amp, base, *refs):
    u = refs[0:4]
    w = refs[4:8]
    tails = refs[8:12]
    scratch = refs[12]
    nv, nx, ny, nz = base.shape

    def body(j, carry):
        lines = [base[j, 0], base[j, nx - 1], *edge_lines(base[j], scratch)]
        for f in range(4):
            for n, value in enumerate((summed(pick, amp, u[f], w[f], j), lines[f])):
                hi = value.astype(BF16)
                tails[f][2 * n, j] = hi
                tails[f][2 * n + 1, j] = (value - hi.astype(F32)).astype(BF16)
        return carry

    lax.fori_loop(0, nv, body, 0)


def faces(pick, amp, base, u_faces, w_faces):
    nv, nx, ny, nz = base.shape
    whole = lambda a: pl.BlockSpec(a.shape, lambda s: (0,) * a.ndim)
    return pl.pallas_call(
        faces_kernel,
        grid=(1,),
        in_specs=[in_smem()] * 2 + [whole(a) for a in (base, *u_faces, *w_faces)],
        out_specs=[pl.BlockSpec((TAIL,) + a.shape[1:], lambda s: (a.shape[0] // TAIL - 1, 0, 0, 0)) for a in u_faces],
        out_shape=[sds(a.shape, BF16) for a in u_faces],
        input_output_aliases={3: 0, 4: 1, 5: 2, 6: 3},
        scratch_shapes=[pltpu.VMEM((nz // LANES, nx * ny, LANES), F32)],
        compiler_params=params(36),
        name="faces",
    )(pick, amp, base, *u_faces, *w_faces)


def row_of(shape, n):
    return lax.broadcasted_iota(jnp.int32, shape, 0) % n


def diff_lanes(a):
    n = a.shape[-1]
    return pltpu.roll(a, n - 1, a.ndim - 1) - pltpu.roll(a, 1, a.ndim - 1)


def diff_rows(a, n, lo, hi):
    rows = a.shape[0]
    row = row_of(a.shape, n)
    return jnp.where(row == n - 1, hi, pltpu.roll(a, rows - 1, 0)) - jnp.where(row == 0, lo, pltpu.roll(a, 1, 0))


def main_kernel(pick, amp, lw, u_hbm, q_hbm, out, u_buf, q_buf, even, odd, u_even, u_odd, acc, c0, u_sem, q_sem):
    nx, nm, nv, ny, nz = u_buf.shape
    rows = nv * ny

    def u_copy(p):
        return pltpu.make_async_copy(u_hbm.at[:, :, p], u_buf.at[p], u_sem.at[p])

    def q_copy(p):
        return pltpu.make_async_copy(q_hbm.at[:, :, p], q_buf.at[p], q_sem.at[p])

    for p in range(nx):
        u_copy(p).start()
        q_copy(p).start()
    c0[0] = jnp.zeros((rows, nz), F32)
    c0[nx + 1] = jnp.zeros((rows, nz), F32)

    def products(p, m, dest):
        qm = q_buf[p, pick[m]].reshape(rows, nz)
        dest[m] = jnp.dot(lw[...], jnp.concatenate([qm, qm], axis=0), preferred_element_type=F32)

    def plane(p, src, dest, u_src, u_dest):
        after = jnp.minimum(p + 1, nx - 1)

        @pl.when(p < nx - 1)
        def _():
            u_copy(after).wait()
            q_copy(after).wait()

        acc[...] = jnp.zeros_like(acc)
        each = -(-TURN // nv)

        def body(step, carry):
            for j in range(nv):
                for k in range(each * j, min(each * (j + 1), TURN)):
                    products(after, step * TURN + k, dest)
                at = slice(j * ny, (j + 1) * ny)
                sums = [acc[n, at] for n in range(5)]
                for k in range(TURN):
                    m = step * TURN + k
                    w0, down, up, w2 = (src[m, n * rows + j * ny : n * rows + (j + 1) * ny] for n in range(4))
                    u = u_src[m, at]
                    following = u_buf[after, m, j].astype(F32) * amp[m]
                    dx = following - u_dest[m, at]
                    u_dest[m, at] = following
                    terms = [dx * w0 + diff_lanes(u) * w2, u * w0, u * down, u * up, u * w2]
                    sums = [v + t for v, t in zip(sums, terms)]
                for n in range(5):
                    acc[n, at] = sums[n]
            return carry

        lax.fori_loop(0, nm // TURN, body, 0)
        last = jnp.where(p == nx - 1, 1.0, 0.0)
        c0[p + 1] = acc[1]
        row = row_of((rows, nz), ny)
        h = acc[0] - diff_lanes(acc[4]) - last * acc[1]
        h = h + jnp.where(row == ny - 1, 0.0, pltpu.roll(acc[2], rows - 1, 0))
        out[p] = h + jnp.where(row == 0, 0.0, pltpu.roll(acc[3], 1, 0))

    u_copy(0).wait()
    q_copy(0).wait()
    u_odd[...] = jnp.zeros_like(u_odd)

    def first(m, carry):
        products(0, m, even)
        u_even[m] = u_buf[0, m].reshape(rows, nz).astype(F32) * amp[m]
        return carry

    lax.fori_loop(0, nm, first, 0, unroll=4)

    def pair(i, carry):
        plane(2 * i, even, odd, u_even, u_odd)
        plane(2 * i + 1, odd, even, u_odd, u_even)
        return carry

    lax.fori_loop(0, nx // 2, pair, 0)

    def finish(p, carry):
        out[p] = out[p] - c0[p + 2] + c0[p]
        return carry

    lax.fori_loop(0, nx, finish, 0, unroll=4)


def main(pick, amp, lw, direct, adjoint):
    nm, nv, nx, ny, nz = direct.shape
    rows = nv * ny
    buf = pltpu.VMEM((nx, nm, nv, ny, nz), BF16)
    return pl.pallas_call(
        main_kernel,
        in_specs=[in_smem(), in_smem(), in_vmem(), in_hbm(), in_hbm()],
        out_specs=in_vmem(),
        out_shape=sds((nx, rows, nz), F32),
        scratch_shapes=[
            buf,
            buf,
            pltpu.VMEM((nm, 4 * rows, nz), F32),
            pltpu.VMEM((nm, 4 * rows, nz), F32),
            pltpu.VMEM((nm, rows, nz), F32),
            pltpu.VMEM((nm, rows, nz), F32),
            pltpu.VMEM((5, rows, nz), F32),
            pltpu.VMEM((nx + 2, rows, nz), F32),
            pltpu.SemaphoreType.DMA((nx,)),
            pltpu.SemaphoreType.DMA((nx,)),
        ],
        compiler_params=params(LARGE),
        cost_estimate=pl.CostEstimate(flops=10**6, bytes_accessed=10**5, transcendentals=0),
        name="main",
    )(pick, amp, lw, direct, adjoint)


def weight_of(cells):
    return jnp.where(cells == 0, 1.0, jnp.where(cells == 1, 0.5, 0.0)).astype(F32)


def spread(ref, x, n):
    nv, _, nz = ref.shape
    return jnp.concatenate([jnp.broadcast_to(ref[j, pl.ds(x, 1), :], (n, nz)) for j in range(nv)], axis=0)


def write_lines(values, x, n, lo, hi):
    for j in range(lo.shape[0]):
        lo[j, pl.ds(x, 1), :] = values[j * n : j * n + 1]
        hi[j, pl.ds(x, 1), :] = values[(j + 1) * n - 1 : (j + 1) * n]


def boundary_kernel(scale, pick, amp, local, cell, *refs):
    w = refs[0:4]
    halo = [refs[4 + f] for f in (2, 3, 0, 1)]
    field, xlo, xhi, ylo, yhi = refs[8:13]
    base_halo = refs[13:17]
    add = refs[17:21]
    nx, rows, nz = local.shape
    nv = add[0].shape[0]
    ny = rows // nv
    for f in range(4):
        add[f][...] = whole_of(halo[f], 0)
        base_halo[f][...] = whole_of(halo[f], 1)

    def face(j, carry):
        for f in range(4):
            add[f][j] -= summed(pick, amp, halo[f], w[f], j)
        return carry

    lax.fori_loop(0, nv, face, 0)
    row = row_of((rows, nz), ny)

    def plane(x, carry):
        lo, hi = spread(add[2], x, ny), spread(add[3], x, ny)
        g = local[x] + jnp.where(row == 0, lo, 0.0) - jnp.where(row == ny - 1, hi, 0.0)
        g = g + jnp.where(x == 0, 1.0, 0.0) * add[0][...].reshape(rows, nz)
        g = g - jnp.where(x == nx - 1, 1.0, 0.0) * add[1][...].reshape(rows, nz)
        g = g * jnp.concatenate([weight_of(cell[x]) * scale] * nv, axis=0)
        field[x] = g
        write_lines(g, x, ny, ylo, yhi)
        return carry

    lax.fori_loop(0, nx, plane, 0, unroll=2)
    xlo[...] = field[0].reshape(xlo.shape)
    xhi[...] = field[nx - 1].reshape(xhi.shape)


def boundary(scale, pick, amp, local, cell, w_faces, halo):
    nx, rows, nz = local.shape
    face = [sds(a.shape[1:], F32) for a in halo]
    return pl.pallas_call(
        lambda *refs: boundary_kernel(scale, *refs),
        in_specs=[in_smem()] * 2 + [in_vmem()] * 10,
        out_specs=[in_vmem()] * 9,
        out_shape=[sds(local.shape, F32)] + face * 2,
        scratch_shapes=[pltpu.VMEM(f.shape, F32) for f in face],
        compiler_params=params(28),
        name="boundary",
    )(pick, amp, local, cell, *w_faces, *halo[2:], *halo[:2])


def mix_rows(lw, values):
    hi = values.astype(BF16)
    lo = (values - hi.astype(F32)).astype(BF16)
    return jnp.dot(lw, jnp.concatenate([hi, lo, hi], axis=0), preferred_element_type=F32)


def step_kernel(last, lw, lw_y, base, cell, field, *refs):
    got = [refs[f] for f in (2, 3, 0, 1)]
    got_base = refs[4:8]
    out = refs[8]
    faces = refs[9:13]
    b_pad, c0, bh_lo, bh_hi, ch_lo, ch_hi = refs[-6:]
    nv, nx, ny, nz = base.shape
    rows = nv * ny
    for f, at in ((0, 0), (1, nx + 1)):
        b = got_base[f][...].reshape(rows, nz)
        b_pad[at] = b
        c0[at] = b * mix_rows(lw[:rows], got[f][...].reshape(rows, nz))
    for f, bh, ch in ((2, bh_lo, ch_lo), (3, bh_hi, ch_hi)):
        b = got_base[f][...]
        bh[...] = b
        ch[...] = b * mix_rows(lw_y[...], got[f][...].reshape(nv * nx, nz)).reshape(nv, nx, nz)

    def fill(x, carry):
        b_pad[x + 1] = base[:, x].reshape(rows, nz)
        return carry

    lax.fori_loop(0, nx, fill, 0, unroll=4)

    def plane(x, carry):
        w = mix_rows(lw[...], field[x])
        w0, w1, w2 = (w[n * rows : (n + 1) * rows] for n in range(3))
        b = b_pad[x + 1]
        c0[x + 1] = b * w0
        h = (b_pad[x + 2] - b_pad[x]) * w0
        h = h + diff_rows(b, ny, spread(bh_lo, x, ny), spread(bh_hi, x, ny)) * w1
        h = h - diff_rows(b * w1, ny, spread(ch_lo, x, ny), spread(ch_hi, x, ny))
        h = h + diff_lanes(b) * w2 - diff_lanes(b * w2)
        if last:
            out[:, x] = h.reshape(nv, ny, nz)
        else:
            out[x] = h
        return carry

    lax.fori_loop(0, nx, plane, 0, unroll=4)

    def finish(x, carry):
        change = c0[x] - c0[x + 2]
        if last:
            out[:, x] = out[:, x] + change.reshape(nv, ny, nz)
        else:
            g = (out[x] + change) * jnp.concatenate([weight_of(cell[x])] * nv, axis=0)
            out[x] = g
            write_lines(g, x, ny, faces[2], faces[3])
        return carry

    lax.fori_loop(0, nx, finish, 0, unroll=4)
    if not last:
        faces[0][...] = out[0].reshape(nv, ny, nz)
        faces[1][...] = out[nx - 1].reshape(nv, ny, nz)


def apply_step(last, lw, lw_y, base, cell, field, got_base, got):
    nv, nx, ny, nz = base.shape
    rows = nv * ny
    face = [] if last else [sds((nv, n, nz), F32) for n in (ny, ny, nx, nx)]
    line = pltpu.VMEM((nv, nx, nz), F32)
    padded = pltpu.VMEM((nx + 2, rows, nz), F32)
    return pl.pallas_call(
        lambda *refs: step_kernel(last, *refs),
        in_specs=[in_vmem()] * 13,
        out_specs=[in_vmem()] * (1 + len(face)),
        out_shape=[sds(base.shape if last else field.shape, F32)] + face,
        scratch_shapes=[padded, padded, line, line, line, line],
        compiler_params=params(28),
        name="step_two" if last else "step_one",
    )(lw, lw_y, base, cell, field, *got[2:], *got[:2], *got_base)


def exchange_axis(axis, lo, hi):
    count = lax.axis_size(axis)
    up = [(i, i + 1) for i in range(count - 1)]
    down = [(i + 1, i) for i in range(count - 1)]
    return [lax.ppermute(hi, axis, up), lax.ppermute(lo, axis, down)]


def exchange(arrays):
    normal = exchange_axis("normal", *arrays[2:])
    return exchange_axis("chord", *arrays[:2]) + normal


def sum_over(axis, values):
    count = lax.axis_size(axis)
    if count & (count - 1):
        return lax.psum(values, axis)
    bit = 1
    while bit < count:
        values = values + lax.ppermute(values, axis, [(i, i ^ bit) for i in range(count)])
        bit *= 2
    return values


def kron_rows(mix, n):
    nv = mix.shape[1]
    hi = lax.reduce_precision(mix, 8, 7)
    lo = lax.reduce_precision(mix - hi, 8, 7)
    small = jnp.concatenate([hi.transpose(0, 2, 1), lo.transpose(0, 2, 1)], axis=2)
    rows, cols = np.arange(nv * n), np.arange(2 * nv * n)
    left = jnp.asarray((rows[:, None] // n == np.arange(nv)[None]).astype(np.float32))
    right = jnp.asarray((cols[None] // n == np.arange(2 * nv)[:, None]).astype(np.float32))
    return jnp.einsum("rj,djc,ck->drk", left, small, right, precision=lax.Precision.HIGHEST)


def within(wide, n, cells):
    return (wide * jnp.asarray(np.tile(cells, (wide.shape[-2] // n, wide.shape[-1] // n)))).astype(BF16)


def main_rows(wide, n):
    eye, below, above = (np.eye(n, k=k, dtype=np.float32) for k in (0, -1, 1))
    return jnp.concatenate([within(wide[d], n, c) for d, c in ((0, eye), (1, below - eye), (1, eye - above), (2, eye))], axis=0)


def step_rows(lw):
    half = lw.shape[-1] // 2
    return jnp.concatenate([lw[..., :half], lw[..., :half], lw[..., half:]], axis=-1)


def per_device(direct, adjoint, base, cell, pick, mix):
    nm, nv, nx, ny, nz = direct.shape
    cells_all = nv * nx * ny * nz * lax.axis_size("chord") * lax.axis_size("normal")
    *own, sums = pack(direct)
    sums = sum_over("chord", sum_over("normal", jnp.sum(sums, axis=1)))
    amp = lax.rsqrt(sums / cells_all + 1e-06)
    wide = kron_rows(mix, ny)
    lw_y = within(wide, ny, np.eye(ny, dtype=np.float32))
    lw_x = lw_y if nx == ny else within(kron_rows(mix, nx), nx, np.eye(nx, dtype=np.float32))
    w_faces = [*mix_chord(lw_y[0], adjoint), *mix_normal(lw_x[1], adjoint)]
    halo = exchange(faces(pick, amp, base, own, w_faces))
    local = main(pick, amp, main_rows(wide, ny), direct, adjoint)
    field, *sides = boundary(1.0 / nm, pick, amp, local, cell, w_faces, halo)
    sides, base_halo = sides[:4], sides[4:]
    lw_step = step_rows(lw_y.reshape(3 * nv * ny, -1))
    lw_line = step_rows(lw_x[1])
    field, *sides = apply_step(False, lw_step, lw_line, base, cell, field, base_halo, exchange(sides))
    return apply_step(True, lw_step, lw_line, base, cell, field, base_halo, exchange(sides))[0]


def solution(mesh):
    return jax.shard_map(
        per_device,
        mesh=mesh,
        in_specs=(
            P(None, None, "chord", "normal", None),
            P(None, None, "chord", "normal", None),
            P(None, "chord", "normal", None),
            P("chord", "normal", None),
            P(),
            P(),
        ),
        out_specs=P(None, "chord", "normal", None),
        check_vma=False,
    )
```

```python
import jax
import jax.numpy as jnp
import numpy as np
from jax import lax
from jax.experimental import pallas as pl
from jax.experimental.pallas import tpu as pltpu
from jax.sharding import PartitionSpec as P

F32 = jnp.float32
BF16 = jnp.bfloat16
LANES = 128
MIB = 1024 * 1024
GROUP = 4
TAIL = 4
TURN = 16
LARGE = 51


def in_vmem():
    return pl.BlockSpec(memory_space=pltpu.VMEM)


def in_smem():
    return pl.BlockSpec(memory_space=pltpu.SMEM)


def in_hbm():
    return pl.BlockSpec(memory_space=pl.ANY)


def sds(shape, dtype):
    return jax.ShapeDtypeStruct(shape, dtype)


def params(mib):
    return pltpu.CompilerParams(vmem_limit_bytes=mib * MIB)


def edge_lines(cells, scratch):
    nx, ny, nz = cells.shape
    flat = cells.reshape(nx * ny, nz)
    out = ([], [])
    for h in range(nz // LANES):
        scratch[h] = flat[:, h * LANES : (h + 1) * LANES]
        for side, first in enumerate((0, ny - 1)):
            out[side].append(scratch[h, pl.ds(first, nx, stride=ny), :])
    return [jnp.concatenate(o, axis=1) for o in out]


def mode_copy(modes, buf, sem, m):
    return pltpu.make_async_copy(modes.at[m], buf.at[m], sem.at[m])


def direct_kernel(modes, xlo, xhi, ylo, yhi, energy, buf, scratch, sem):
    nm, nv, nx, ny, nz = buf.shape
    for m in range(nm):
        mode_copy(modes, buf, sem, m).start()

    def body(m, carry):
        mode_copy(modes, buf, sem, m).wait()
        xlo[m] = buf[m, :, 0]
        xhi[m] = buf[m, :, nx - 1]
        total = jnp.zeros((ny, nz), F32)
        for i in range(nv):
            cells = buf[m, i].astype(F32)
            lo, hi = edge_lines(cells, scratch.at[i])
            ylo[m, i] = lo.astype(BF16)
            yhi[m, i] = hi.astype(BF16)
            total = total + jnp.sum(cells * cells, axis=0)
        line = jnp.sum(total, axis=0, keepdims=True)
        energy[pl.ds(m, 1), :] = sum(line[:, h : h + LANES] for h in range(0, nz, LANES))
        return carry

    lax.fori_loop(0, nm, body, 0)


def mode_buffers(modes):
    nm, nv, nx, ny, nz = modes.shape
    return [
        pltpu.VMEM(modes.shape, BF16),
        pltpu.VMEM((nv, nz // LANES, nx * ny, LANES), F32),
        pltpu.SemaphoreType.DMA((nm,)),
    ]


def pack(direct):
    nm, nv, nx, ny, nz = direct.shape
    return pl.pallas_call(
        direct_kernel,
        in_specs=[in_hbm()],
        out_specs=[in_vmem()] * 5,
        out_shape=[sds((nm + TAIL, nv, n, nz), BF16) for n in (ny, ny, nx, nx)] + [sds((nm, LANES), F32)],
        scratch_shapes=mode_buffers(direct),
        compiler_params=params(LARGE),
        cost_estimate=pl.CostEstimate(flops=3 * direct.size, bytes_accessed=2 * direct.size, transcendentals=0),
        name="pack_direct",
    )(direct)


def mix_chord_kernel(lw, lo, hi, w_lo, w_hi):
    nm, nv, _, ny, nz = lo.shape
    rows = nv * ny

    def body(m, carry):
        for src, out in ((lo, w_lo), (hi, w_hi)):
            face = src[m, :, 0].reshape(rows, nz)
            out[m] = jnp.dot(lw[...], jnp.concatenate([face, face], axis=0), preferred_element_type=F32)
        return carry

    lax.fori_loop(0, nm, body, 0, unroll=4)


def mix_chord(lw, modes):
    nm, nv, nx, ny, nz = modes.shape
    block = (nm, nv, 1, ny, nz)
    w = sds((nm, nv * ny, nz), F32)
    whole = pl.BlockSpec(w.shape, lambda s: (0, 0, 0))
    return pl.pallas_call(
        mix_chord_kernel,
        grid=(1,),
        in_specs=[
            pl.BlockSpec(lw.shape, lambda s: (0, 0)),
            pl.BlockSpec(block, lambda s: (0, 0, 0, 0, 0)),
            pl.BlockSpec(block, lambda s: (0, 0, nx - 1, 0, 0)),
        ],
        out_specs=[whole, whole],
        out_shape=[w, w],
        compiler_params=params(LARGE),
        cost_estimate=pl.CostEstimate(flops=10**8, bytes_accessed=6 * 10**6, transcendentals=0),
        name="mix_chord",
    )(lw, modes, modes)


def mix_normal_kernel(lw, modes, w_lo, w_hi, buf, scratch, sem):
    nm, nv, nx, ny, nz = buf.shape
    for m in range(nm):
        mode_copy(modes, buf, sem, m).start()

    def body(m, carry):
        mode_copy(modes, buf, sem, m).wait()
        lines = [edge_lines(buf[m, i].astype(F32), scratch.at[i]) for i in range(nv)]
        for side, out in enumerate((w_lo, w_hi)):
            face = jnp.concatenate([line[side] for line in lines], axis=0).astype(BF16)
            out[m] = jnp.dot(lw[...], jnp.concatenate([face, face], axis=0), preferred_element_type=F32)
        return carry

    lax.fori_loop(0, nm, body, 0)


def mix_normal(lw, modes):
    nm, nv, nx, ny, nz = modes.shape
    w = sds((nm, nv * nx, nz), F32)
    return pl.pallas_call(
        mix_normal_kernel,
        in_specs=[in_vmem(), in_hbm()],
        out_specs=[in_vmem()] * 2,
        out_shape=[w, w],
        scratch_shapes=mode_buffers(modes),
        compiler_params=params(LARGE),
        cost_estimate=pl.CostEstimate(flops=3 * modes.size, bytes_accessed=3 * modes.size, transcendentals=0),
        name="mix_normal",
    )(lw, modes)


def summed(pick, amp, u, w, j):
    nm = w.shape[0]
    n, nz = u.shape[2:]
    total = jnp.zeros((n, nz), F32)
    for m in range(nm):
        total = total + amp[m] * (u[m, j].astype(F32) * w[pick[m], pl.ds(pl.multiple_of(j * n, n), n), :])
    return total


def whole_of(ref, part):
    n = ref.shape[0] - TAIL + 2 * part
    return ref[n].astype(F32) + ref[n + 1].astype(F32)


def faces_kernel(pick, amp, base, *refs):
    u = refs[0:4]
    w = refs[4:8]
    tails = refs[8:12]
    scratch = refs[12]
    nv, nx, ny, nz = base.shape

    def body(j, carry):
        lines = [base[j, 0], base[j, nx - 1], *edge_lines(base[j], scratch)]
        for f in range(4):
            for n, value in enumerate((summed(pick, amp, u[f], w[f], j), lines[f])):
                hi = value.astype(BF16)
                tails[f][2 * n, j] = hi
                tails[f][2 * n + 1, j] = (value - hi.astype(F32)).astype(BF16)
        return carry

    lax.fori_loop(0, nv, body, 0)


def faces(pick, amp, base, u_faces, w_faces):
    nv, nx, ny, nz = base.shape
    whole = lambda a: pl.BlockSpec(a.shape, lambda s: (0,) * a.ndim)
    return pl.pallas_call(
        faces_kernel,
        grid=(1,),
        in_specs=[in_smem()] * 2 + [whole(a) for a in (base, *u_faces, *w_faces)],
        out_specs=[pl.BlockSpec((TAIL,) + a.shape[1:], lambda s: (a.shape[0] // TAIL - 1, 0, 0, 0)) for a in u_faces],
        out_shape=[sds(a.shape, BF16) for a in u_faces],
        input_output_aliases={3: 0, 4: 1, 5: 2, 6: 3},
        scratch_shapes=[pltpu.VMEM((nz // LANES, nx * ny, LANES), F32)],
        compiler_params=params(36),
        name="faces",
    )(pick, amp, base, *u_faces, *w_faces)


def row_of(shape, n):
    return lax.broadcasted_iota(jnp.int32, shape, 0) % n


def diff_lanes(a):
    n = a.shape[-1]
    return pltpu.roll(a, n - 1, a.ndim - 1) - pltpu.roll(a, 1, a.ndim - 1)


def diff_rows(a, n, lo, hi):
    rows = a.shape[0]
    row = row_of(a.shape, n)
    return jnp.where(row == n - 1, hi, pltpu.roll(a, rows - 1, 0)) - jnp.where(row == 0, lo, pltpu.roll(a, 1, 0))


def main_kernel(pick, amp, lw, u_hbm, q_hbm, out, u_buf, q_buf, even, odd, u_even, u_odd, acc, c0, u_sem, q_sem):
    nx, nm, nv, ny, nz = u_buf.shape
    rows = nv * ny

    def u_copy(p):
        return pltpu.make_async_copy(u_hbm.at[:, :, p], u_buf.at[p], u_sem.at[p])

    def q_copy(p):
        return pltpu.make_async_copy(q_hbm.at[:, :, p], q_buf.at[p], q_sem.at[p])

    for p in range(nx):
        u_copy(p).start()
        q_copy(p).start()
    c0[0] = jnp.zeros((rows, nz), F32)
    c0[nx + 1] = jnp.zeros((rows, nz), F32)

    def products(p, m, dest):
        qm = q_buf[p, pick[m]].reshape(rows, nz)
        dest[m] = jnp.dot(lw[...], jnp.concatenate([qm, qm], axis=0), preferred_element_type=F32)

    def plane(p, src, dest, u_src, u_dest):
        after = jnp.minimum(p + 1, nx - 1)

        @pl.when(p < nx - 1)
        def _():
            u_copy(after).wait()
            q_copy(after).wait()

        acc[...] = jnp.zeros_like(acc)
        each = -(-TURN // nv)

        def body(step, carry):
            for j in range(nv):
                for k in range(each * j, min(each * (j + 1), TURN)):
                    products(after, step * TURN + k, dest)
                at = slice(j * ny, (j + 1) * ny)
                sums = [acc[n, at] for n in range(5)]
                for k in range(TURN):
                    m = step * TURN + k
                    w0, down, up, w2 = (src[m, n * rows + j * ny : n * rows + (j + 1) * ny] for n in range(4))
                    u = u_src[m, at]
                    following = u_buf[after, m, j].astype(F32) * amp[m]
                    dx = following - u_dest[m, at]
                    u_dest[m, at] = following
                    terms = [dx * w0 + diff_lanes(u) * w2, u * w0, u * down, u * up, u * w2]
                    sums = [v + t for v, t in zip(sums, terms)]
                for n in range(5):
                    acc[n, at] = sums[n]
            return carry

        lax.fori_loop(0, nm // TURN, body, 0)
        last = jnp.where(p == nx - 1, 1.0, 0.0)
        c0[p + 1] = acc[1]
        row = row_of((rows, nz), ny)
        h = acc[0] - diff_lanes(acc[4]) - last * acc[1]
        h = h + jnp.where(row == ny - 1, 0.0, pltpu.roll(acc[2], rows - 1, 0))
        out[p] = h + jnp.where(row == 0, 0.0, pltpu.roll(acc[3], 1, 0))

    u_copy(0).wait()
    q_copy(0).wait()
    u_odd[...] = jnp.zeros_like(u_odd)

    def first(m, carry):
        products(0, m, even)
        u_even[m] = u_buf[0, m].reshape(rows, nz).astype(F32) * amp[m]
        return carry

    lax.fori_loop(0, nm, first, 0, unroll=4)

    def pair(i, carry):
        plane(2 * i, even, odd, u_even, u_odd)
        plane(2 * i + 1, odd, even, u_odd, u_even)
        return carry

    lax.fori_loop(0, nx // 2, pair, 0)

    def finish(p, carry):
        out[p] = out[p] - c0[p + 2] + c0[p]
        return carry

    lax.fori_loop(0, nx, finish, 0, unroll=4)


def main(pick, amp, lw, direct, adjoint):
    nm, nv, nx, ny, nz = direct.shape
    rows = nv * ny
    buf = pltpu.VMEM((nx, nm, nv, ny, nz), BF16)
    return pl.pallas_call(
        main_kernel,
        in_specs=[in_smem(), in_smem(), in_vmem(), in_hbm(), in_hbm()],
        out_specs=in_vmem(),
        out_shape=sds((nx, rows, nz), F32),
        scratch_shapes=[
            buf,
            buf,
            pltpu.VMEM((nm, 4 * rows, nz), F32),
            pltpu.VMEM((nm, 4 * rows, nz), F32),
            pltpu.VMEM((nm, rows, nz), F32),
            pltpu.VMEM((nm, rows, nz), F32),
            pltpu.VMEM((5, rows, nz), F32),
            pltpu.VMEM((nx + 2, rows, nz), F32),
            pltpu.SemaphoreType.DMA((nx,)),
            pltpu.SemaphoreType.DMA((nx,)),
        ],
        compiler_params=params(LARGE),
        cost_estimate=pl.CostEstimate(flops=10**6, bytes_accessed=10**5, transcendentals=0),
        name="main",
    )(pick, amp, lw, direct, adjoint)


def weight_of(cells):
    return jnp.where(cells == 0, 1.0, jnp.where(cells == 1, 0.5, 0.0)).astype(F32)


def spread(ref, x, n):
    nv, _, nz = ref.shape
    return jnp.concatenate([jnp.broadcast_to(ref[j, pl.ds(x, 1), :], (n, nz)) for j in range(nv)], axis=0)


def write_lines(values, x, n, lo, hi):
    for j in range(lo.shape[0]):
        lo[j, pl.ds(x, 1), :] = values[j * n : j * n + 1]
        hi[j, pl.ds(x, 1), :] = values[(j + 1) * n - 1 : (j + 1) * n]


def boundary_kernel(scale, pick, amp, local, cell, *refs):
    w = refs[0:4]
    halo = [refs[4 + f] for f in (2, 3, 0, 1)]
    field, xlo, xhi, ylo, yhi = refs[8:13]
    base_halo = refs[13:17]
    add = refs[17:21]
    nx, rows, nz = local.shape
    nv = add[0].shape[0]
    ny = rows // nv
    for f in range(4):
        add[f][...] = whole_of(halo[f], 0)
        base_halo[f][...] = whole_of(halo[f], 1)

    def face(j, carry):
        for f in range(4):
            add[f][j] -= summed(pick, amp, halo[f], w[f], j)
        return carry

    lax.fori_loop(0, nv, face, 0)
    row = row_of((rows, nz), ny)

    def plane(x, carry):
        lo, hi = spread(add[2], x, ny), spread(add[3], x, ny)
        g = local[x] + jnp.where(row == 0, lo, 0.0) - jnp.where(row == ny - 1, hi, 0.0)
        g = g + jnp.where(x == 0, 1.0, 0.0) * add[0][...].reshape(rows, nz)
        g = g - jnp.where(x == nx - 1, 1.0, 0.0) * add[1][...].reshape(rows, nz)
        g = g * jnp.concatenate([weight_of(cell[x]) * scale] * nv, axis=0)
        field[x] = g
        write_lines(g, x, ny, ylo, yhi)
        return carry

    lax.fori_loop(0, nx, plane, 0, unroll=2)
    xlo[...] = field[0].reshape(xlo.shape)
    xhi[...] = field[nx - 1].reshape(xhi.shape)


def boundary(scale, pick, amp, local, cell, w_faces, halo):
    nx, rows, nz = local.shape
    face = [sds(a.shape[1:], F32) for a in halo]
    return pl.pallas_call(
        lambda *refs: boundary_kernel(scale, *refs),
        in_specs=[in_smem()] * 2 + [in_vmem()] * 10,
        out_specs=[in_vmem()] * 9,
        out_shape=[sds(local.shape, F32)] + face * 2,
        scratch_shapes=[pltpu.VMEM(f.shape, F32) for f in face],
        compiler_params=params(28),
        name="boundary",
    )(pick, amp, local, cell, *w_faces, *halo[2:], *halo[:2])


def mix_rows(lw, values):
    hi = values.astype(BF16)
    lo = (values - hi.astype(F32)).astype(BF16)
    return jnp.dot(lw, jnp.concatenate([hi, lo, hi], axis=0), preferred_element_type=F32)


def step_kernel(last, lw, lw_y, base, cell, field, *refs):
    got = [refs[f] for f in (2, 3, 0, 1)]
    got_base = refs[4:8]
    out = refs[8]
    faces = refs[9:13]
    b_pad, c0, bh_lo, bh_hi, ch_lo, ch_hi = refs[-6:]
    nv, nx, ny, nz = base.shape
    rows = nv * ny
    for f, at in ((0, 0), (1, nx + 1)):
        b = got_base[f][...].reshape(rows, nz)
        b_pad[at] = b
        c0[at] = b * mix_rows(lw[:rows], got[f][...].reshape(rows, nz))
    for f, bh, ch in ((2, bh_lo, ch_lo), (3, bh_hi, ch_hi)):
        b = got_base[f][...]
        bh[...] = b
        ch[...] = b * mix_rows(lw_y[...], got[f][...].reshape(nv * nx, nz)).reshape(nv, nx, nz)

    def fill(x, carry):
        b_pad[x + 1] = base[:, x].reshape(rows, nz)
        return carry

    lax.fori_loop(0, nx, fill, 0, unroll=4)

    def plane(x, carry):
        w = mix_rows(lw[...], field[x])
        w0, w1, w2 = (w[n * rows : (n + 1) * rows] for n in range(3))
        b = b_pad[x + 1]
        c0[x + 1] = b * w0
        h = (b_pad[x + 2] - b_pad[x]) * w0
        h = h + diff_rows(b, ny, spread(bh_lo, x, ny), spread(bh_hi, x, ny)) * w1
        h = h - diff_rows(b * w1, ny, spread(ch_lo, x, ny), spread(ch_hi, x, ny))
        h = h + diff_lanes(b) * w2 - diff_lanes(b * w2)
        if last:
            out[:, x] = h.reshape(nv, ny, nz)
        else:
            out[x] = h
        return carry

    lax.fori_loop(0, nx, plane, 0, unroll=4)

    def finish(x, carry):
        change = c0[x] - c0[x + 2]
        if last:
            out[:, x] = out[:, x] + change.reshape(nv, ny, nz)
        else:
            g = (out[x] + change) * jnp.concatenate([weight_of(cell[x])] * nv, axis=0)
            out[x] = g
            write_lines(g, x, ny, faces[2], faces[3])
        return carry

    lax.fori_loop(0, nx, finish, 0, unroll=4)
    if not last:
        faces[0][...] = out[0].reshape(nv, ny, nz)
        faces[1][...] = out[nx - 1].reshape(nv, ny, nz)


def apply_step(last, lw, lw_y, base, cell, field, got_base, got):
    nv, nx, ny, nz = base.shape
    rows = nv * ny
    face = [] if last else [sds((nv, n, nz), F32) for n in (ny, ny, nx, nx)]
    line = pltpu.VMEM((nv, nx, nz), F32)
    padded = pltpu.VMEM((nx + 2, rows, nz), F32)
    return pl.pallas_call(
        lambda *refs: step_kernel(last, *refs),
        in_specs=[in_vmem()] * 13,
        out_specs=[in_vmem()] * (1 + len(face)),
        out_shape=[sds(base.shape if last else field.shape, F32)] + face,
        scratch_shapes=[padded, padded, line, line, line, line],
        compiler_params=params(28),
        name="step_two" if last else "step_one",
    )(lw, lw_y, base, cell, field, *got[2:], *got[:2], *got_base)


def exchange_axis(axis, lo, hi):
    count = lax.axis_size(axis)
    up = [(i, i + 1) for i in range(count - 1)]
    down = [(i + 1, i) for i in range(count - 1)]
    return [lax.ppermute(hi, axis, up), lax.ppermute(lo, axis, down)]


def exchange(arrays):
    normal = exchange_axis("normal", *arrays[2:])
    return exchange_axis("chord", *arrays[:2]) + normal


def sum_over(axis, values):
    count = lax.axis_size(axis)
    if count & (count - 1):
        return lax.psum(values, axis)
    bit = 1
    while bit < count:
        values = values + lax.ppermute(values, axis, [(i, i ^ bit) for i in range(count)])
        bit *= 2
    return values


def kron_rows(mix, n):
    nv = mix.shape[1]
    hi = lax.reduce_precision(mix, 8, 7)
    lo = lax.reduce_precision(mix - hi, 8, 7)
    small = jnp.concatenate([hi.transpose(0, 2, 1), lo.transpose(0, 2, 1)], axis=2)
    rows, cols = np.arange(nv * n), np.arange(2 * nv * n)
    left = jnp.asarray((rows[:, None] // n == np.arange(nv)[None]).astype(np.float32))
    right = jnp.asarray((cols[None] // n == np.arange(2 * nv)[:, None]).astype(np.float32))
    return jnp.einsum("rj,djc,ck->drk", left, small, right, precision=lax.Precision.HIGHEST)


def within(wide, n, cells):
    return (wide * jnp.asarray(np.tile(cells, (wide.shape[-2] // n, wide.shape[-1] // n)))).astype(BF16)


def main_rows(wide, n):
    eye, below, above = (np.eye(n, k=k, dtype=np.float32) for k in (0, -1, 1))
    return jnp.concatenate([within(wide[d], n, c) for d, c in ((0, eye), (1, below - eye), (1, eye - above), (2, eye))], axis=0)


def step_rows(lw):
    half = lw.shape[-1] // 2
    return jnp.concatenate([lw[..., :half], lw[..., :half], lw[..., half:]], axis=-1)


def per_device(direct, adjoint, base, cell, pick, mix):
    nm, nv, nx, ny, nz = direct.shape
    cells_all = nv * nx * ny * nz * lax.axis_size("chord") * lax.axis_size("normal")
    *own, sums = pack(direct)
    sums = sum_over("chord", sum_over("normal", jnp.sum(sums, axis=1)))
    amp = lax.rsqrt(sums / cells_all + 1e-06)
    wide = kron_rows(mix, ny)
    lw_y = within(wide, ny, np.eye(ny, dtype=np.float32))
    lw_x = lw_y if nx == ny else within(kron_rows(mix, nx), nx, np.eye(nx, dtype=np.float32))
    w_faces = [*mix_chord(lw_y[0], adjoint), *mix_normal(lw_x[1], adjoint)]
    halo = exchange(faces(pick, amp, base, own, w_faces))
    local = main(pick, amp, main_rows(wide, ny), direct, adjoint)
    field, *sides = boundary(1.0 / nm, pick, amp, local, cell, w_faces, halo)
    sides, base_halo = sides[:4], sides[4:]
    lw_step = step_rows(lw_y.reshape(3 * nv * ny, -1))
    lw_line = step_rows(lw_x[1])
    field, *sides = apply_step(False, lw_step, lw_line, base, cell, field, base_halo, exchange(sides))
    return apply_step(True, lw_step, lw_line, base, cell, field, base_halo, exchange(sides))[0]


def solution(mesh):
    return jax.shard_map(
        per_device,
        mesh=mesh,
        in_specs=(
            P(None, None, "chord", "normal", None),
            P(None, None, "chord", "normal", None),
            P(None, "chord", "normal", None),
            P("chord", "normal", None),
            P(),
            P(),
        ),
        out_specs=P(None, "chord", "normal", None),
        check_vma=False,
    )
```

```python
import jax
import jax.numpy as jnp
import numpy as np
from jax import lax
from jax.experimental import pallas as pl
from jax.experimental.pallas import tpu as pltpu
from jax.sharding import PartitionSpec as P

F32 = jnp.float32
BF16 = jnp.bfloat16
LANES = 128
MIB = 1024 * 1024
GROUP = 4
TAIL = 4
TURN = 16
LARGE = 51


def in_vmem():
    return pl.BlockSpec(memory_space=pltpu.VMEM)


def in_smem():
    return pl.BlockSpec(memory_space=pltpu.SMEM)


def in_hbm():
    return pl.BlockSpec(memory_space=pl.ANY)


def sds(shape, dtype):
    return jax.ShapeDtypeStruct(shape, dtype)


def params(mib):
    return pltpu.CompilerParams(vmem_limit_bytes=mib * MIB)


def edge_lines(cells, scratch):
    nx, ny, nz = cells.shape
    flat = cells.reshape(nx * ny, nz)
    out = ([], [])
    for h in range(nz // LANES):
        scratch[h] = flat[:, h * LANES : (h + 1) * LANES]
        for side, first in enumerate((0, ny - 1)):
            out[side].append(scratch[h, pl.ds(first, nx, stride=ny), :])
    return [jnp.concatenate(o, axis=1) for o in out]


def mode_copy(modes, buf, sem, m):
    return pltpu.make_async_copy(modes.at[m], buf.at[m], sem.at[m])


def direct_kernel(modes, xlo, xhi, ylo, yhi, energy, buf, scratch, sem):
    nm, nv, nx, ny, nz = buf.shape
    for m in range(nm):
        mode_copy(modes, buf, sem, m).start()

    def body(m, carry):
        mode_copy(modes, buf, sem, m).wait()
        xlo[m] = buf[m, :, 0]
        xhi[m] = buf[m, :, nx - 1]
        total = jnp.zeros((ny, nz), F32)
        for i in range(nv):
            cells = buf[m, i].astype(F32)
            lo, hi = edge_lines(cells, scratch.at[i])
            ylo[m, i] = lo.astype(BF16)
            yhi[m, i] = hi.astype(BF16)
            total = total + jnp.sum(cells * cells, axis=0)
        line = jnp.sum(total, axis=0, keepdims=True)
        energy[pl.ds(m, 1), :] = sum(line[:, h : h + LANES] for h in range(0, nz, LANES))
        return carry

    lax.fori_loop(0, nm, body, 0)


def mode_buffers(modes):
    nm, nv, nx, ny, nz = modes.shape
    return [
        pltpu.VMEM(modes.shape, BF16),
        pltpu.VMEM((nv, nz // LANES, nx * ny, LANES), F32),
        pltpu.SemaphoreType.DMA((nm,)),
    ]


def pack(direct):
    nm, nv, nx, ny, nz = direct.shape
    return pl.pallas_call(
        direct_kernel,
        in_specs=[in_hbm()],
        out_specs=[in_vmem()] * 5,
        out_shape=[sds((nm + TAIL, nv, n, nz), BF16) for n in (ny, ny, nx, nx)] + [sds((nm, LANES), F32)],
        scratch_shapes=mode_buffers(direct),
        compiler_params=params(LARGE),
        cost_estimate=pl.CostEstimate(flops=3 * direct.size, bytes_accessed=2 * direct.size, transcendentals=0),
        name="pack_direct",
    )(direct)


def mix_chord_kernel(lw, lo, hi, w_lo, w_hi):
    nm, nv, _, ny, nz = lo.shape
    rows = nv * ny

    def body(m, carry):
        for src, out in ((lo, w_lo), (hi, w_hi)):
            face = src[m, :, 0].reshape(rows, nz)
            out[m] = jnp.dot(lw[...], jnp.concatenate([face, face], axis=0), preferred_element_type=F32)
        return carry

    lax.fori_loop(0, nm, body, 0, unroll=4)


def mix_chord(lw, modes):
    nm, nv, nx, ny, nz = modes.shape
    block = (nm, nv, 1, ny, nz)
    w = sds((nm, nv * ny, nz), F32)
    whole = pl.BlockSpec(w.shape, lambda s: (0, 0, 0))
    return pl.pallas_call(
        mix_chord_kernel,
        grid=(1,),
        in_specs=[
            pl.BlockSpec(lw.shape, lambda s: (0, 0)),
            pl.BlockSpec(block, lambda s: (0, 0, 0, 0, 0)),
            pl.BlockSpec(block, lambda s: (0, 0, nx - 1, 0, 0)),
        ],
        out_specs=[whole, whole],
        out_shape=[w, w],
        compiler_params=params(LARGE),
        cost_estimate=pl.CostEstimate(flops=10**8, bytes_accessed=6 * 10**6, transcendentals=0),
        name="mix_chord",
    )(lw, modes, modes)


def mix_normal_kernel(lw, modes, w_lo, w_hi, buf, scratch, sem):
    nm, nv, nx, ny, nz = buf.shape
    for m in range(nm):
        mode_copy(modes, buf, sem, m).start()

    def body(m, carry):
        mode_copy(modes, buf, sem, m).wait()
        lines = [edge_lines(buf[m, i].astype(F32), scratch.at[i]) for i in range(nv)]
        for side, out in enumerate((w_lo, w_hi)):
            face = jnp.concatenate([line[side] for line in lines], axis=0).astype(BF16)
            out[m] = jnp.dot(lw[...], jnp.concatenate([face, face], axis=0), preferred_element_type=F32)
        return carry

    lax.fori_loop(0, nm, body, 0)


def mix_normal(lw, modes):
    nm, nv, nx, ny, nz = modes.shape
    w = sds((nm, nv * nx, nz), F32)
    return pl.pallas_call(
        mix_normal_kernel,
        in_specs=[in_vmem(), in_hbm()],
        out_specs=[in_vmem()] * 2,
        out_shape=[w, w],
        scratch_shapes=mode_buffers(modes),
        compiler_params=params(LARGE),
        cost_estimate=pl.CostEstimate(flops=3 * modes.size, bytes_accessed=3 * modes.size, transcendentals=0),
        name="mix_normal",
    )(lw, modes)


def summed(pick, amp, u, w, j):
    nm = w.shape[0]
    n, nz = u.shape[2:]
    total = jnp.zeros((n, nz), F32)
    for m in range(nm):
        total = total + amp[m] * (u[m, j].astype(F32) * w[pick[m], pl.ds(pl.multiple_of(j * n, n), n), :])
    return total


def whole_of(ref, part):
    n = ref.shape[0] - TAIL + 2 * part
    return ref[n].astype(F32) + ref[n + 1].astype(F32)


def faces_kernel(across, pick, amp, base, *refs):
    u, w, tails, scratch = refs[0:2], refs[2:4], refs[4:6], refs[6]
    nv, nx, ny, nz = base.shape

    def body(j, carry):
        lines = [base[j, 0], base[j, nx - 1]] if across == "chord" else edge_lines(base[j], scratch)
        for f in range(2):
            for n, value in enumerate((summed(pick, amp, u[f], w[f], j), lines[f])):
                hi = value.astype(BF16)
                tails[f][2 * n, j] = hi
                tails[f][2 * n + 1, j] = (value - hi.astype(F32)).astype(BF16)
        return carry

    lax.fori_loop(0, nv, body, 0)


def faces(across, pick, amp, base, u_faces, w_faces):
    nv, nx, ny, nz = base.shape
    whole = lambda a: pl.BlockSpec(a.shape, lambda s: (0,) * a.ndim)
    return pl.pallas_call(
        lambda *refs: faces_kernel(across, *refs),
        grid=(1,),
        in_specs=[in_smem()] * 2 + [whole(a) for a in (base, *u_faces, *w_faces)],
        out_specs=[pl.BlockSpec((TAIL,) + a.shape[1:], lambda s: (a.shape[0] // TAIL - 1, 0, 0, 0)) for a in u_faces],
        out_shape=[sds(a.shape, BF16) for a in u_faces],
        input_output_aliases={3: 0, 4: 1},
        scratch_shapes=[pltpu.VMEM((nz // LANES, nx * ny, LANES), F32)],
        compiler_params=params(36),
        cost_estimate=pl.CostEstimate(flops=10**7, bytes_accessed=5 * 10**6, transcendentals=0),
        name="faces_" + across,
    )(pick, amp, base, *u_faces, *w_faces)


def row_of(shape, n):
    return lax.broadcasted_iota(jnp.int32, shape, 0) % n


def diff_lanes(a):
    n = a.shape[-1]
    return pltpu.roll(a, n - 1, a.ndim - 1) - pltpu.roll(a, 1, a.ndim - 1)


def diff_rows(a, n, lo, hi):
    rows = a.shape[0]
    row = row_of(a.shape, n)
    return jnp.where(row == n - 1, hi, pltpu.roll(a, rows - 1, 0)) - jnp.where(row == 0, lo, pltpu.roll(a, 1, 0))


def main_kernel(pick, amp, lw, u_hbm, q_hbm, out, u_buf, q_buf, even, odd, u_even, u_odd, acc, c0, u_sem, q_sem):
    nx, nm, nv, ny, nz = u_buf.shape
    rows = nv * ny

    def u_copy(p):
        return pltpu.make_async_copy(u_hbm.at[:, :, p], u_buf.at[p], u_sem.at[p])

    def q_copy(p):
        return pltpu.make_async_copy(q_hbm.at[:, :, p], q_buf.at[p], q_sem.at[p])

    for p in range(nx):
        u_copy(p).start()
        q_copy(p).start()
    c0[0] = jnp.zeros((rows, nz), F32)
    c0[nx + 1] = jnp.zeros((rows, nz), F32)

    def products(p, m, dest):
        qm = q_buf[p, pick[m]].reshape(rows, nz)
        dest[m] = jnp.dot(lw[...], jnp.concatenate([qm, qm], axis=0), preferred_element_type=F32)

    def plane(p, src, dest, u_src, u_dest):
        after = jnp.minimum(p + 1, nx - 1)

        @pl.when(p < nx - 1)
        def _():
            u_copy(after).wait()
            q_copy(after).wait()

        acc[...] = jnp.zeros_like(acc)
        each = -(-TURN // nv)

        def body(step, carry):
            for j in range(nv):
                for k in range(each * j, min(each * (j + 1), TURN)):
                    products(after, step * TURN + k, dest)
                at = slice(j * ny, (j + 1) * ny)
                sums = [acc[n, at] for n in range(5)]
                for k in range(TURN):
                    m = step * TURN + k
                    w0, down, up, w2 = (src[m, n * rows + j * ny : n * rows + (j + 1) * ny] for n in range(4))
                    u = u_src[m, at]
                    following = u_buf[after, m, j].astype(F32) * amp[m]
                    dx = following - u_dest[m, at]
                    u_dest[m, at] = following
                    terms = [dx * w0 + diff_lanes(u) * w2, u * w0, u * down, u * up, u * w2]
                    sums = [v + t for v, t in zip(sums, terms)]
                for n in range(5):
                    acc[n, at] = sums[n]
            return carry

        lax.fori_loop(0, nm // TURN, body, 0)
        last = jnp.where(p == nx - 1, 1.0, 0.0)
        c0[p + 1] = acc[1]
        row = row_of((rows, nz), ny)
        h = acc[0] - diff_lanes(acc[4]) - last * acc[1]
        h = h + jnp.where(row == ny - 1, 0.0, pltpu.roll(acc[2], rows - 1, 0))
        out[p] = h + jnp.where(row == 0, 0.0, pltpu.roll(acc[3], 1, 0))

    u_copy(0).wait()
    q_copy(0).wait()
    u_odd[...] = jnp.zeros_like(u_odd)

    def first(m, carry):
        products(0, m, even)
        u_even[m] = u_buf[0, m].reshape(rows, nz).astype(F32) * amp[m]
        return carry

    lax.fori_loop(0, nm, first, 0, unroll=4)

    def pair(i, carry):
        plane(2 * i, even, odd, u_even, u_odd)
        plane(2 * i + 1, odd, even, u_odd, u_even)
        return carry

    lax.fori_loop(0, nx // 2, pair, 0)

    def finish(p, carry):
        out[p] = out[p] - c0[p + 2] + c0[p]
        return carry

    lax.fori_loop(0, nx, finish, 0, unroll=4)


def main(pick, amp, lw, direct, adjoint):
    nm, nv, nx, ny, nz = direct.shape
    rows = nv * ny
    buf = pltpu.VMEM((nx, nm, nv, ny, nz), BF16)
    return pl.pallas_call(
        main_kernel,
        in_specs=[in_smem(), in_smem(), in_vmem(), in_hbm(), in_hbm()],
        out_specs=in_vmem(),
        out_shape=sds((nx, rows, nz), F32),
        scratch_shapes=[
            buf,
            buf,
            pltpu.VMEM((nm, 4 * rows, nz), F32),
            pltpu.VMEM((nm, 4 * rows, nz), F32),
            pltpu.VMEM((nm, rows, nz), F32),
            pltpu.VMEM((nm, rows, nz), F32),
            pltpu.VMEM((5, rows, nz), F32),
            pltpu.VMEM((nx + 2, rows, nz), F32),
            pltpu.SemaphoreType.DMA((nx,)),
            pltpu.SemaphoreType.DMA((nx,)),
        ],
        compiler_params=params(LARGE),
        cost_estimate=pl.CostEstimate(flops=10**6, bytes_accessed=10**5, transcendentals=0),
        name="main",
    )(pick, amp, lw, direct, adjoint)


def weight_of(cells):
    return jnp.where(cells == 0, 1.0, jnp.where(cells == 1, 0.5, 0.0)).astype(F32)


def spread(ref, x, n):
    nv, _, nz = ref.shape
    return jnp.concatenate([jnp.broadcast_to(ref[j, pl.ds(x, 1), :], (n, nz)) for j in range(nv)], axis=0)


def write_lines(values, x, n, lo, hi):
    for j in range(lo.shape[0]):
        lo[j, pl.ds(x, 1), :] = values[j * n : j * n + 1]
        hi[j, pl.ds(x, 1), :] = values[(j + 1) * n - 1 : (j + 1) * n]


def boundary_kernel(scale, pick, amp, local, cell, *refs):
    w = refs[0:4]
    halo = [refs[4 + f] for f in (2, 3, 0, 1)]
    field, xlo, xhi, ylo, yhi = refs[8:13]
    base_halo = refs[13:17]
    add = refs[17:21]
    nx, rows, nz = local.shape
    nv = add[0].shape[0]
    ny = rows // nv
    for f in range(4):
        add[f][...] = whole_of(halo[f], 0)
        base_halo[f][...] = whole_of(halo[f], 1)

    def face(j, carry):
        for f in range(4):
            add[f][j] -= summed(pick, amp, halo[f], w[f], j)
        return carry

    lax.fori_loop(0, nv, face, 0)
    row = row_of((rows, nz), ny)

    def plane(x, carry):
        lo, hi = spread(add[2], x, ny), spread(add[3], x, ny)
        g = local[x] + jnp.where(row == 0, lo, 0.0) - jnp.where(row == ny - 1, hi, 0.0)
        g = g + jnp.where(x == 0, 1.0, 0.0) * add[0][...].reshape(rows, nz)
        g = g - jnp.where(x == nx - 1, 1.0, 0.0) * add[1][...].reshape(rows, nz)
        g = g * jnp.concatenate([weight_of(cell[x]) * scale] * nv, axis=0)
        field[x] = g
        write_lines(g, x, ny, ylo, yhi)
        return carry

    lax.fori_loop(0, nx, plane, 0, unroll=2)
    xlo[...] = field[0].reshape(xlo.shape)
    xhi[...] = field[nx - 1].reshape(xhi.shape)


def boundary(scale, pick, amp, local, cell, w_faces, halo):
    nx, rows, nz = local.shape
    face = [sds(a.shape[1:], F32) for a in halo]
    return pl.pallas_call(
        lambda *refs: boundary_kernel(scale, *refs),
        in_specs=[in_smem()] * 2 + [in_vmem()] * 10,
        out_specs=[in_vmem()] * 9,
        out_shape=[sds(local.shape, F32)] + face * 2,
        scratch_shapes=[pltpu.VMEM(f.shape, F32) for f in face],
        compiler_params=params(28),
        name="boundary",
    )(pick, amp, local, cell, *w_faces, *halo[2:], *halo[:2])


def mix_rows(lw, values):
    hi = values.astype(BF16)
    lo = (values - hi.astype(F32)).astype(BF16)
    return jnp.dot(lw, jnp.concatenate([hi, lo, hi], axis=0), preferred_element_type=F32)


def step_kernel(last, lw, lw_y, base, cell, field, *refs):
    got = [refs[f] for f in (2, 3, 0, 1)]
    got_base = refs[4:8]
    out = refs[8]
    faces = refs[9:13]
    b_pad, c0, bh_lo, bh_hi, ch_lo, ch_hi = refs[-6:]
    nv, nx, ny, nz = base.shape
    rows = nv * ny
    for f, at in ((0, 0), (1, nx + 1)):
        b = got_base[f][...].reshape(rows, nz)
        b_pad[at] = b
        c0[at] = b * mix_rows(lw[:rows], got[f][...].reshape(rows, nz))
    for f, bh, ch in ((2, bh_lo, ch_lo), (3, bh_hi, ch_hi)):
        b = got_base[f][...]
        bh[...] = b
        ch[...] = b * mix_rows(lw_y[...], got[f][...].reshape(nv * nx, nz)).reshape(nv, nx, nz)

    def fill(x, carry):
        b_pad[x + 1] = base[:, x].reshape(rows, nz)
        return carry

    lax.fori_loop(0, nx, fill, 0, unroll=4)

    def plane(x, carry):
        w = mix_rows(lw[...], field[x])
        w0, w1, w2 = (w[n * rows : (n + 1) * rows] for n in range(3))
        b = b_pad[x + 1]
        c0[x + 1] = b * w0
        h = (b_pad[x + 2] - b_pad[x]) * w0
        h = h + diff_rows(b, ny, spread(bh_lo, x, ny), spread(bh_hi, x, ny)) * w1
        h = h - diff_rows(b * w1, ny, spread(ch_lo, x, ny), spread(ch_hi, x, ny))
        h = h + diff_lanes(b) * w2 - diff_lanes(b * w2)
        if last:
            out[:, x] = h.reshape(nv, ny, nz)
        else:
            out[x] = h
        return carry

    lax.fori_loop(0, nx, plane, 0, unroll=4)

    def finish(x, carry):
        change = c0[x] - c0[x + 2]
        if last:
            out[:, x] = out[:, x] + change.reshape(nv, ny, nz)
        else:
            g = (out[x] + change) * jnp.concatenate([weight_of(cell[x])] * nv, axis=0)
            out[x] = g
            write_lines(g, x, ny, faces[2], faces[3])
        return carry

    lax.fori_loop(0, nx, finish, 0, unroll=4)
    if not last:
        faces[0][...] = out[0].reshape(nv, ny, nz)
        faces[1][...] = out[nx - 1].reshape(nv, ny, nz)


def apply_step(last, lw, lw_y, base, cell, field, got_base, got):
    nv, nx, ny, nz = base.shape
    rows = nv * ny
    face = [] if last else [sds((nv, n, nz), F32) for n in (ny, ny, nx, nx)]
    line = pltpu.VMEM((nv, nx, nz), F32)
    padded = pltpu.VMEM((nx + 2, rows, nz), F32)
    return pl.pallas_call(
        lambda *refs: step_kernel(last, *refs),
        in_specs=[in_vmem()] * 13,
        out_specs=[in_vmem()] * (1 + len(face)),
        out_shape=[sds(base.shape if last else field.shape, F32)] + face,
        scratch_shapes=[padded, padded, line, line, line, line],
        compiler_params=params(28),
        name="step_two" if last else "step_one",
    )(lw, lw_y, base, cell, field, *got[2:], *got[:2], *got_base)


def exchange_axis(axis, lo, hi):
    count = lax.axis_size(axis)
    up = [(i, i + 1) for i in range(count - 1)]
    down = [(i + 1, i) for i in range(count - 1)]
    return [lax.ppermute(hi, axis, up), lax.ppermute(lo, axis, down)]


def exchange(arrays):
    normal = exchange_axis("normal", *arrays[2:])
    return exchange_axis("chord", *arrays[:2]) + normal


def sum_over(axis, values):
    count = lax.axis_size(axis)
    if count & (count - 1):
        return lax.psum(values, axis)
    bit = 1
    while bit < count:
        values = values + lax.ppermute(values, axis, [(i, i ^ bit) for i in range(count)])
        bit *= 2
    return values


def kron_rows(mix, n):
    nv = mix.shape[1]
    hi = lax.reduce_precision(mix, 8, 7)
    lo = lax.reduce_precision(mix - hi, 8, 7)
    small = jnp.concatenate([hi.transpose(0, 2, 1), lo.transpose(0, 2, 1)], axis=2)
    rows, cols = np.arange(nv * n), np.arange(2 * nv * n)
    left = jnp.asarray((rows[:, None] // n == np.arange(nv)[None]).astype(np.float32))
    right = jnp.asarray((cols[None] // n == np.arange(2 * nv)[:, None]).astype(np.float32))
    return jnp.einsum("rj,djc,ck->drk", left, small, right, precision=lax.Precision.HIGHEST)


def within(wide, n, cells):
    return (wide * jnp.asarray(np.tile(cells, (wide.shape[-2] // n, wide.shape[-1] // n)))).astype(BF16)


def main_rows(wide, n):
    eye, below, above = (np.eye(n, k=k, dtype=np.float32) for k in (0, -1, 1))
    return jnp.concatenate([within(wide[d], n, c) for d, c in ((0, eye), (1, below - eye), (1, eye - above), (2, eye))], axis=0)


def step_rows(lw):
    half = lw.shape[-1] // 2
    return jnp.concatenate([lw[..., :half], lw[..., :half], lw[..., half:]], axis=-1)


def per_device(direct, adjoint, base, cell, pick, mix):
    nm, nv, nx, ny, nz = direct.shape
    cells_all = nv * nx * ny * nz * lax.axis_size("chord") * lax.axis_size("normal")
    *own, sums = pack(direct)
    sums = sum_over("chord", sum_over("normal", jnp.sum(sums, axis=1)))
    amp = lax.rsqrt(sums / cells_all + 1e-06)
    wide = kron_rows(mix, ny)
    lw_y = within(wide, ny, np.eye(ny, dtype=np.float32))
    lw_x = lw_y if nx == ny else within(kron_rows(mix, nx), nx, np.eye(nx, dtype=np.float32))
    w_normal = mix_normal(lw_x[1], adjoint)
    y_faces = faces("normal", pick, amp, base, own[2:], w_normal)
    *y_faces, lw_chord = lax.optimization_barrier((*y_faces, lw_y[0]))
    y_halo = exchange_axis("normal", *y_faces)
    w_chord = mix_chord(lw_chord, adjoint)
    halo = exchange_axis("chord", *faces("chord", pick, amp, base, own[:2], w_chord)) + y_halo
    w_faces = [*w_chord, *w_normal]
    local = main(pick, amp, main_rows(wide, ny), direct, adjoint)
    field, *sides = boundary(1.0 / nm, pick, amp, local, cell, w_faces, halo)
    sides, base_halo = sides[:4], sides[4:]
    lw_step = step_rows(lw_y.reshape(3 * nv * ny, -1))
    lw_line = step_rows(lw_x[1])
    field, *sides = apply_step(False, lw_step, lw_line, base, cell, field, base_halo, exchange(sides))
    return apply_step(True, lw_step, lw_line, base, cell, field, base_halo, exchange(sides))[0]


def solution(mesh):
    return jax.shard_map(
        per_device,
        mesh=mesh,
        in_specs=(
            P(None, None, "chord", "normal", None),
            P(None, None, "chord", "normal", None),
            P(None, "chord", "normal", None),
            P("chord", "normal", None),
            P(),
            P(),
        ),
        out_specs=P(None, "chord", "normal", None),
        check_vma=False,
    )
```

```python
import jax
import jax.numpy as jnp
import numpy as np
from jax import lax
from jax.experimental import pallas as pl
from jax.experimental.pallas import tpu as pltpu
from jax.sharding import PartitionSpec as P

F32 = jnp.float32
BF16 = jnp.bfloat16
LANES = 128
MIB = 1024 * 1024
GROUP = 4
TAIL = 4
TURN = 16
LARGE = 51


def in_vmem():
    return pl.BlockSpec(memory_space=pltpu.VMEM)


def in_smem():
    return pl.BlockSpec(memory_space=pltpu.SMEM)


def in_hbm():
    return pl.BlockSpec(memory_space=pl.ANY)


def sds(shape, dtype):
    return jax.ShapeDtypeStruct(shape, dtype)


def params(mib):
    return pltpu.CompilerParams(vmem_limit_bytes=mib * MIB)


def edge_lines(cells, scratch):
    nx, ny, nz = cells.shape
    flat = cells.reshape(nx * ny, nz)
    out = ([], [])
    for h in range(nz // LANES):
        scratch[h] = flat[:, h * LANES : (h + 1) * LANES]
        for side, first in enumerate((0, ny - 1)):
            out[side].append(scratch[h, pl.ds(first, nx, stride=ny), :])
    return [jnp.concatenate(o, axis=1) for o in out]


def mode_copy(modes, buf, sem, m):
    return pltpu.make_async_copy(modes.at[m], buf.at[m], sem.at[m])


def direct_kernel(modes, xlo, xhi, ylo, yhi, energy, buf, scratch, sem):
    nm, nv, nx, ny, nz = buf.shape
    for m in range(nm):
        mode_copy(modes, buf, sem, m).start()

    def body(m, carry):
        mode_copy(modes, buf, sem, m).wait()
        xlo[m] = buf[m, :, 0]
        xhi[m] = buf[m, :, nx - 1]
        total = jnp.zeros((ny, nz), F32)
        for i in range(nv):
            cells = buf[m, i].astype(F32)
            lo, hi = edge_lines(cells, scratch.at[i])
            ylo[m, i] = lo.astype(BF16)
            yhi[m, i] = hi.astype(BF16)
            total = total + jnp.sum(cells * cells, axis=0)
        line = jnp.sum(total, axis=0, keepdims=True)
        energy[pl.ds(m, 1), :] = sum(line[:, h : h + LANES] for h in range(0, nz, LANES))
        return carry

    lax.fori_loop(0, nm, body, 0)


def mode_buffers(modes):
    nm, nv, nx, ny, nz = modes.shape
    return [
        pltpu.VMEM(modes.shape, BF16),
        pltpu.VMEM((nv, nz // LANES, nx * ny, LANES), F32),
        pltpu.SemaphoreType.DMA((nm,)),
    ]


def pack(direct):
    nm, nv, nx, ny, nz = direct.shape
    return pl.pallas_call(
        direct_kernel,
        in_specs=[in_hbm()],
        out_specs=[in_vmem()] * 5,
        out_shape=[sds((nm + TAIL, nv, n, nz), BF16) for n in (ny, ny, nx, nx)] + [sds((nm, LANES), F32)],
        scratch_shapes=mode_buffers(direct),
        compiler_params=params(LARGE),
        cost_estimate=pl.CostEstimate(flops=3 * direct.size, bytes_accessed=2 * direct.size, transcendentals=0),
        name="pack_direct",
    )(direct)


def mix_chord_kernel(lw, lo, hi, w_lo, w_hi):
    nm, nv, _, ny, nz = lo.shape
    rows = nv * ny

    def body(m, carry):
        for src, out in ((lo, w_lo), (hi, w_hi)):
            face = src[m, :, 0].reshape(rows, nz)
            out[m] = jnp.dot(lw[...], jnp.concatenate([face, face], axis=0), preferred_element_type=F32)
        return carry

    lax.fori_loop(0, nm, body, 0, unroll=4)


def mix_chord(lw, modes):
    nm, nv, nx, ny, nz = modes.shape
    block = (nm, nv, 1, ny, nz)
    w = sds((nm, nv * ny, nz), F32)
    whole = pl.BlockSpec(w.shape, lambda s: (0, 0, 0))
    return pl.pallas_call(
        mix_chord_kernel,
        grid=(1,),
        in_specs=[
            pl.BlockSpec(lw.shape, lambda s: (0, 0)),
            pl.BlockSpec(block, lambda s: (0, 0, 0, 0, 0)),
            pl.BlockSpec(block, lambda s: (0, 0, nx - 1, 0, 0)),
        ],
        out_specs=[whole, whole],
        out_shape=[w, w],
        compiler_params=params(LARGE),
        cost_estimate=pl.CostEstimate(flops=10**8, bytes_accessed=6 * 10**6, transcendentals=0),
        name="mix_chord",
    )(lw, modes, modes)


def mix_normal_kernel(lw, modes, w_lo, w_hi, buf, scratch, sem):
    nm, nv, nx, ny, nz = buf.shape
    for m in range(nm):
        mode_copy(modes, buf, sem, m).start()

    def body(m, carry):
        mode_copy(modes, buf, sem, m).wait()
        lines = [edge_lines(buf[m, i].astype(F32), scratch.at[i]) for i in range(nv)]
        for side, out in enumerate((w_lo, w_hi)):
            face = jnp.concatenate([line[side] for line in lines], axis=0).astype(BF16)
            out[m] = jnp.dot(lw[...], jnp.concatenate([face, face], axis=0), preferred_element_type=F32)
        return carry

    lax.fori_loop(0, nm, body, 0)


def mix_normal(lw, modes):
    nm, nv, nx, ny, nz = modes.shape
    w = sds((nm, nv * nx, nz), F32)
    return pl.pallas_call(
        mix_normal_kernel,
        in_specs=[in_vmem(), in_hbm()],
        out_specs=[in_vmem()] * 2,
        out_shape=[w, w],
        scratch_shapes=mode_buffers(modes),
        compiler_params=params(LARGE),
        cost_estimate=pl.CostEstimate(flops=3 * modes.size, bytes_accessed=3 * modes.size, transcendentals=0),
        name="mix_normal",
    )(lw, modes)


def summed(pick, amp, u, w, j):
    nm = w.shape[0]
    n, nz = u.shape[2:]
    total = jnp.zeros((n, nz), F32)
    for m in range(nm):
        total = total + amp[m] * (u[m, j].astype(F32) * w[pick[m], pl.ds(pl.multiple_of(j * n, n), n), :])
    return total


def whole_of(ref, part):
    n = ref.shape[0] - TAIL + 2 * part
    return ref[n].astype(F32) + ref[n + 1].astype(F32)


def faces_kernel(across, pick, amp, base, *refs):
    u, w, tails, scratch = refs[0:2], refs[2:4], refs[4:6], refs[6]
    nv, nx, ny, nz = base.shape

    def body(j, carry):
        lines = [base[j, 0], base[j, nx - 1]] if across == "chord" else edge_lines(base[j], scratch)
        for f in range(2):
            for n, value in enumerate((summed(pick, amp, u[f], w[f], j), lines[f])):
                hi = value.astype(BF16)
                tails[f][2 * n, j] = hi
                tails[f][2 * n + 1, j] = (value - hi.astype(F32)).astype(BF16)
        return carry

    lax.fori_loop(0, nv, body, 0)


def faces(across, pick, amp, base, u_faces, w_faces):
    nv, nx, ny, nz = base.shape
    whole = lambda a: pl.BlockSpec(a.shape, lambda s: (0,) * a.ndim)
    return pl.pallas_call(
        lambda *refs: faces_kernel(across, *refs),
        grid=(1,),
        in_specs=[in_smem()] * 2 + [whole(a) for a in (base, *u_faces, *w_faces)],
        out_specs=[pl.BlockSpec((TAIL,) + a.shape[1:], lambda s: (a.shape[0] // TAIL - 1, 0, 0, 0)) for a in u_faces],
        out_shape=[sds(a.shape, BF16) for a in u_faces],
        input_output_aliases={3: 0, 4: 1},
        scratch_shapes=[pltpu.VMEM((nz // LANES, nx * ny, LANES), F32)],
        compiler_params=params(36),
        cost_estimate=pl.CostEstimate(flops=10**7, bytes_accessed=5 * 10**6, transcendentals=0),
        name="faces_" + across,
    )(pick, amp, base, *u_faces, *w_faces)


def row_of(shape, n):
    return lax.broadcasted_iota(jnp.int32, shape, 0) % n


def diff_lanes(a):
    n = a.shape[-1]
    return pltpu.roll(a, n - 1, a.ndim - 1) - pltpu.roll(a, 1, a.ndim - 1)


def diff_rows(a, n, lo, hi):
    rows = a.shape[0]
    row = row_of(a.shape, n)
    return jnp.where(row == n - 1, hi, pltpu.roll(a, rows - 1, 0)) - jnp.where(row == 0, lo, pltpu.roll(a, 1, 0))


def main_kernel(pick, amp, lw, u_hbm, q_hbm, out, u_buf, q_buf, even, odd, u_even, u_odd, acc, c0, u_sem, q_sem):
    nx, nm, nv, ny, nz = u_buf.shape
    rows = nv * ny

    def u_copy(p):
        return pltpu.make_async_copy(u_hbm.at[:, :, p], u_buf.at[p], u_sem.at[p])

    def q_copy(p):
        return pltpu.make_async_copy(q_hbm.at[:, :, p], q_buf.at[p], q_sem.at[p])

    for p in range(nx):
        u_copy(p).start()
        q_copy(p).start()
    c0[0] = jnp.zeros((rows, nz), F32)
    c0[nx + 1] = jnp.zeros((rows, nz), F32)

    def products(p, m, dest):
        qm = q_buf[p, pick[m]].reshape(rows, nz)
        dest[m] = jnp.dot(lw[...], jnp.concatenate([qm, qm], axis=0), preferred_element_type=F32)

    def plane(p, src, dest, u_src, u_dest):
        after = jnp.minimum(p + 1, nx - 1)

        @pl.when(p < nx - 1)
        def _():
            u_copy(after).wait()
            q_copy(after).wait()

        acc[...] = jnp.zeros_like(acc)
        each = -(-TURN // nv)

        def body(step, carry):
            for j in range(nv):
                for k in range(each * j, min(each * (j + 1), TURN)):
                    products(after, step * TURN + k, dest)
                at = slice(j * ny, (j + 1) * ny)
                sums = [acc[n, at] for n in range(5)]
                for k in range(TURN):
                    m = step * TURN + k
                    w0, down, up, w2 = (src[m, n * rows + j * ny : n * rows + (j + 1) * ny] for n in range(4))
                    u = u_src[m, at]
                    following = u_buf[after, m, j].astype(F32) * amp[m]
                    dx = following - u_dest[m, at]
                    u_dest[m, at] = following
                    terms = [dx * w0 + diff_lanes(u) * w2, u * w0, u * down, u * up, u * w2]
                    sums = [v + t for v, t in zip(sums, terms)]
                for n in range(5):
                    acc[n, at] = sums[n]
            return carry

        lax.fori_loop(0, nm // TURN, body, 0)
        last = jnp.where(p == nx - 1, 1.0, 0.0)
        c0[p + 1] = acc[1]
        row = row_of((rows, nz), ny)
        h = acc[0] - diff_lanes(acc[4]) - last * acc[1]
        h = h + jnp.where(row == ny - 1, 0.0, pltpu.roll(acc[2], rows - 1, 0))
        out[p] = h + jnp.where(row == 0, 0.0, pltpu.roll(acc[3], 1, 0))

    u_copy(0).wait()
    q_copy(0).wait()
    u_odd[...] = jnp.zeros_like(u_odd)

    def first(m, carry):
        products(0, m, even)
        u_even[m] = u_buf[0, m].reshape(rows, nz).astype(F32) * amp[m]
        return carry

    lax.fori_loop(0, nm, first, 0, unroll=4)

    def pair(i, carry):
        plane(2 * i, even, odd, u_even, u_odd)
        plane(2 * i + 1, odd, even, u_odd, u_even)
        return carry

    lax.fori_loop(0, nx // 2, pair, 0)

    def finish(p, carry):
        out[p] = out[p] - c0[p + 2] + c0[p]
        return carry

    lax.fori_loop(0, nx, finish, 0, unroll=4)


def main(pick, amp, lw, direct, adjoint):
    nm, nv, nx, ny, nz = direct.shape
    rows = nv * ny
    buf = pltpu.VMEM((nx, nm, nv, ny, nz), BF16)
    return pl.pallas_call(
        main_kernel,
        in_specs=[in_smem(), in_smem(), in_vmem(), in_hbm(), in_hbm()],
        out_specs=in_vmem(),
        out_shape=sds((nx, rows, nz), F32),
        scratch_shapes=[
            buf,
            buf,
            pltpu.VMEM((nm, 4 * rows, nz), F32),
            pltpu.VMEM((nm, 4 * rows, nz), F32),
            pltpu.VMEM((nm, rows, nz), F32),
            pltpu.VMEM((nm, rows, nz), F32),
            pltpu.VMEM((5, rows, nz), F32),
            pltpu.VMEM((nx + 2, rows, nz), F32),
            pltpu.SemaphoreType.DMA((nx,)),
            pltpu.SemaphoreType.DMA((nx,)),
        ],
        compiler_params=params(LARGE),
        cost_estimate=pl.CostEstimate(flops=10**6, bytes_accessed=10**5, transcendentals=0),
        name="main",
    )(pick, amp, lw, direct, adjoint)


def weight_of(cells):
    return jnp.where(cells == 0, 1.0, jnp.where(cells == 1, 0.5, 0.0)).astype(F32)


def spread(ref, x, n):
    nv, _, nz = ref.shape
    return jnp.concatenate([jnp.broadcast_to(ref[j, pl.ds(x, 1), :], (n, nz)) for j in range(nv)], axis=0)


def write_lines(values, x, n, lo, hi):
    for j in range(lo.shape[0]):
        lo[j, pl.ds(x, 1), :] = values[j * n : j * n + 1]
        hi[j, pl.ds(x, 1), :] = values[(j + 1) * n - 1 : (j + 1) * n]


def boundary_kernel(scale, pick, amp, local, cell, *refs):
    w = refs[0:4]
    halo = [refs[4 + f] for f in (2, 3, 0, 1)]
    field, xlo, xhi, ylo, yhi = refs[8:13]
    base_halo = refs[13:17]
    add = refs[17:21]
    nx, rows, nz = local.shape
    nv = add[0].shape[0]
    ny = rows // nv
    for f in range(4):
        add[f][...] = whole_of(halo[f], 0)
        base_halo[f][...] = whole_of(halo[f], 1)

    def face(j, carry):
        for f in range(4):
            add[f][j] -= summed(pick, amp, halo[f], w[f], j)
        return carry

    lax.fori_loop(0, nv, face, 0)
    row = row_of((rows, nz), ny)

    def plane(x, carry):
        lo, hi = spread(add[2], x, ny), spread(add[3], x, ny)
        g = local[x] + jnp.where(row == 0, lo, 0.0) - jnp.where(row == ny - 1, hi, 0.0)
        g = g + jnp.where(x == 0, 1.0, 0.0) * add[0][...].reshape(rows, nz)
        g = g - jnp.where(x == nx - 1, 1.0, 0.0) * add[1][...].reshape(rows, nz)
        g = g * jnp.concatenate([weight_of(cell[x]) * scale] * nv, axis=0)
        field[x] = g
        write_lines(g, x, ny, ylo, yhi)
        return carry

    lax.fori_loop(0, nx, plane, 0, unroll=4)
    xlo[...] = field[0].reshape(xlo.shape)
    xhi[...] = field[nx - 1].reshape(xhi.shape)


def boundary(scale, pick, amp, local, cell, w_faces, halo):
    nx, rows, nz = local.shape
    face = [sds(a.shape[1:], F32) for a in halo]
    return pl.pallas_call(
        lambda *refs: boundary_kernel(scale, *refs),
        in_specs=[in_smem()] * 2 + [in_vmem()] * 10,
        out_specs=[in_vmem()] * 9,
        out_shape=[sds(local.shape, F32)] + face * 2,
        scratch_shapes=[pltpu.VMEM(f.shape, F32) for f in face],
        compiler_params=params(28),
        name="boundary",
    )(pick, amp, local, cell, *w_faces, *halo[2:], *halo[:2])


def mix_rows(lw, values):
    hi = values.astype(BF16)
    lo = (values - hi.astype(F32)).astype(BF16)
    return jnp.dot(lw, jnp.concatenate([hi, lo, hi], axis=0), preferred_element_type=F32)


def step_kernel(last, lw, lw_y, base, cell, field, *refs):
    got = [refs[f] for f in (2, 3, 0, 1)]
    got_base = refs[4:8]
    out = refs[8]
    faces = refs[9:13]
    b_pad, c0, bh_lo, bh_hi, ch_lo, ch_hi = refs[-6:]
    nv, nx, ny, nz = base.shape
    rows = nv * ny
    for f, at in ((0, 0), (1, nx + 1)):
        b = got_base[f][...].reshape(rows, nz)
        b_pad[at] = b
        c0[at] = b * mix_rows(lw[:rows], got[f][...].reshape(rows, nz))
    for f, bh, ch in ((2, bh_lo, ch_lo), (3, bh_hi, ch_hi)):
        b = got_base[f][...]
        bh[...] = b
        ch[...] = b * mix_rows(lw_y[...], got[f][...].reshape(nv * nx, nz)).reshape(nv, nx, nz)

    def fill(x, carry):
        b_pad[x + 1] = base[:, x].reshape(rows, nz)
        return carry

    lax.fori_loop(0, nx, fill, 0, unroll=4)

    def plane(x, carry):
        w = mix_rows(lw[...], field[x])
        w0, w1, w2 = (w[n * rows : (n + 1) * rows] for n in range(3))
        b = b_pad[x + 1]
        c0[x + 1] = b * w0
        h = (b_pad[x + 2] - b_pad[x]) * w0
        h = h + diff_rows(b, ny, spread(bh_lo, x, ny), spread(bh_hi, x, ny)) * w1
        h = h - diff_rows(b * w1, ny, spread(ch_lo, x, ny), spread(ch_hi, x, ny))
        h = h + diff_lanes(b) * w2 - diff_lanes(b * w2)
        if last:
            out[:, x] = h.reshape(nv, ny, nz)
        else:
            out[x] = h
        return carry

    lax.fori_loop(0, nx, plane, 0, unroll=8)

    def finish(x, carry):
        change = c0[x] - c0[x + 2]
        if last:
            out[:, x] = out[:, x] + change.reshape(nv, ny, nz)
        else:
            g = (out[x] + change) * jnp.concatenate([weight_of(cell[x])] * nv, axis=0)
            out[x] = g
            write_lines(g, x, ny, faces[2], faces[3])
        return carry

    lax.fori_loop(0, nx, finish, 0, unroll=4)
    if not last:
        faces[0][...] = out[0].reshape(nv, ny, nz)
        faces[1][...] = out[nx - 1].reshape(nv, ny, nz)


def apply_step(last, lw, lw_y, base, cell, field, got_base, got):
    nv, nx, ny, nz = base.shape
    rows = nv * ny
    face = [] if last else [sds((nv, n, nz), F32) for n in (ny, ny, nx, nx)]
    line = pltpu.VMEM((nv, nx, nz), F32)
    padded = pltpu.VMEM((nx + 2, rows, nz), F32)
    return pl.pallas_call(
        lambda *refs: step_kernel(last, *refs),
        in_specs=[in_vmem()] * 13,
        out_specs=[in_vmem()] * (1 + len(face)),
        out_shape=[sds(base.shape if last else field.shape, F32)] + face,
        scratch_shapes=[padded, padded, line, line, line, line],
        compiler_params=params(28),
        name="step_two" if last else "step_one",
    )(lw, lw_y, base, cell, field, *got[2:], *got[:2], *got_base)


def exchange_axis(axis, lo, hi):
    count = lax.axis_size(axis)
    up = [(i, i + 1) for i in range(count - 1)]
    down = [(i + 1, i) for i in range(count - 1)]
    return [lax.ppermute(hi, axis, up), lax.ppermute(lo, axis, down)]


def exchange(arrays):
    normal = exchange_axis("normal", *arrays[2:])
    return exchange_axis("chord", *arrays[:2]) + normal


def sum_over(axis, values):
    count = lax.axis_size(axis)
    if count & (count - 1):
        return lax.psum(values, axis)
    bit = 1
    while bit < count:
        values = values + lax.ppermute(values, axis, [(i, i ^ bit) for i in range(count)])
        bit *= 2
    return values


def kron_rows(mix, n):
    nv = mix.shape[1]
    hi = lax.reduce_precision(mix, 8, 7)
    lo = lax.reduce_precision(mix - hi, 8, 7)
    small = jnp.concatenate([hi.transpose(0, 2, 1), lo.transpose(0, 2, 1)], axis=2)
    rows, cols = np.arange(nv * n), np.arange(2 * nv * n)
    left = jnp.asarray((rows[:, None] // n == np.arange(nv)[None]).astype(np.float32))
    right = jnp.asarray((cols[None] // n == np.arange(2 * nv)[:, None]).astype(np.float32))
    return jnp.einsum("rj,djc,ck->drk", left, small, right, precision=lax.Precision.HIGHEST)


def within(wide, n, cells):
    return (wide * jnp.asarray(np.tile(cells, (wide.shape[-2] // n, wide.shape[-1] // n)))).astype(BF16)


def main_rows(wide, n):
    eye, below, above = (np.eye(n, k=k, dtype=np.float32) for k in (0, -1, 1))
    return jnp.concatenate([within(wide[d], n, c) for d, c in ((0, eye), (1, below - eye), (1, eye - above), (2, eye))], axis=0)


def step_rows(lw):
    half = lw.shape[-1] // 2
    return jnp.concatenate([lw[..., :half], lw[..., :half], lw[..., half:]], axis=-1)


def per_device(direct, adjoint, base, cell, pick, mix):
    nm, nv, nx, ny, nz = direct.shape
    cells_all = nv * nx * ny * nz * lax.axis_size("chord") * lax.axis_size("normal")
    *own, sums = pack(direct)
    sums = sum_over("chord", sum_over("normal", jnp.sum(sums, axis=1)))
    amp = lax.rsqrt(sums / cells_all + 1e-06)
    wide = kron_rows(mix, ny)
    lw_y = within(wide, ny, np.eye(ny, dtype=np.float32))
    lw_x = lw_y if nx == ny else within(kron_rows(mix, nx), nx, np.eye(nx, dtype=np.float32))
    w_normal = mix_normal(lw_x[1], adjoint)
    y_faces = faces("normal", pick, amp, base, own[2:], w_normal)
    *y_faces, lw_chord = lax.optimization_barrier((*y_faces, lw_y[0]))
    y_halo = exchange_axis("normal", *y_faces)
    w_chord = mix_chord(lw_chord, adjoint)
    halo = exchange_axis("chord", *faces("chord", pick, amp, base, own[:2], w_chord)) + y_halo
    w_faces = [*w_chord, *w_normal]
    local = main(pick, amp, main_rows(wide, ny), direct, adjoint)
    field, *sides = boundary(1.0 / nm, pick, amp, local, cell, w_faces, halo)
    sides, base_halo = sides[:4], sides[4:]
    lw_step = step_rows(lw_y.reshape(3 * nv * ny, -1))
    lw_line = step_rows(lw_x[1])
    field, *sides = apply_step(False, lw_step, lw_line, base, cell, field, base_halo, exchange(sides))
    return apply_step(True, lw_step, lw_line, base, cell, field, base_halo, exchange(sides))[0]


def solution(mesh):
    return jax.shard_map(
        per_device,
        mesh=mesh,
        in_specs=(
            P(None, None, "chord", "normal", None),
            P(None, None, "chord", "normal", None),
            P(None, "chord", "normal", None),
            P("chord", "normal", None),
            P(),
            P(),
        ),
        out_specs=P(None, "chord", "normal", None),
        check_vma=False,
    )
```
